32 devices in a mesh: dp: 2 (over core), expert: 16 (over z, y, x).
Axes of the slice: x: 2, y: 2, z: 4, core: 2. Of those that a mesh axis runs over, the one named last changes fastest.
Arguments:
- tokens: bfloat16 [32, 256, 1024], P(('dp', 'expert'))
- router: bfloat16 [1024, 64], replicated
- weight_in: bfloat16 [64, 1024, 2048], P('expert', None, 'dp'), may hold values from -0.1875 to 0.1875
- weight_out: bfloat16 [64, 2048, 1024], P('expert', 'dp'), may hold values from -0.125 to 0.125
- cotangent: bfloat16 [32, 256, 1024], P(('dp', 'expert')), may hold values from -6 to 6
Outputs:
- mixed: bfloat16 [32, 256, 1024], P(('dp', 'expert'))
- grad_tokens: bfloat16 [32, 256, 1024], P(('dp', 'expert'))
- grad_router: float32 [1024, 64], replicated
- grad_weight_in: bfloat16 [64, 1024, 2048], P('expert', None, 'dp')
- grad_weight_out: bfloat16 [64, 2048, 1024], P('expert', 'dp')
The draws below stay inside these ranges and needn't reach their ends.
All inputs are finite; a program needn't handle non-finite values.
Results may differ from the reference program's by a relative error of at most 0.018.
Values may be sent and summed in bfloat16 or wider, within the bound.
No kernel may reach another device: no remote copies, remote signals or barrier semaphores. Data moves between devices by JAX's collectives and lax.ppermute only.
A program may use at most 64 MiB of HBM per device.

```python
import math
import jax
import jax.numpy as jnp
from jax import lax

D = 1024
FF = 2048
S = 256
EXPERTS = 64
IMAGES = 32
N_DP = 2


def draw_tokens(key, part):
    first_key = jax.random.fold_in(jax.random.fold_in(key, 11), 0)
    shape = (IMAGES, S, D)
    values = jnp.clip(jax.random.normal(first_key, shape, jnp.float32), -6.0, 6.0)
    return values.astype(jnp.bfloat16)


def draw_router(key, part):
    first_key = jax.random.fold_in(key, 23)
    shape = (D, EXPERTS)
    values = jnp.clip(jax.random.normal(first_key, shape, jnp.float32), -6.0, 6.0) / math.sqrt(D)
    return values.astype(jnp.bfloat16)


def steps_of(rng, dims, cuts, low, top_value):
    loudness, own = 1.0, jax.random.fold_in(rng, 6)
    for dim, shards_of in cuts:
        steps = jnp.exp(jax.random.uniform(jax.random.fold_in(own, dim), (shards_of,), jnp.float32, low / len(cuts), top_value / len(cuts)))
        loudness = loudness * jnp.repeat(steps, dims[dim] // shards_of).reshape([-1 if axis == dim else 1 for axis in range(len(dims))])
    return loudness


def bell_draw(stream_key, shape, scale, most, shards=(), held_as=jnp.bfloat16):
    loudness = steps_of(stream_key, shape, shards, -0.22, 0.18) if shards else 1.0
    values = jax.random.normal(stream_key, shape, jnp.float32) * scale * loudness
    return jnp.minimum(jnp.maximum(values, -most), most).astype(held_as)


def setup_inputs(seed: int = 0) -> dict:
    key_of = jax.random.split(jax.random.key(seed), 6)
    tokens = draw_tokens(jax.random.fold_in(key_of[5], 71), 0)
    router = draw_router(jax.random.fold_in(key_of[5], 71), 0)
    weight_in = bell_draw(key_of[2], (EXPERTS, D, FF), D ** -0.5, 0.1875, ((0, 16), (2, 2)))
    weight_out = bell_draw(key_of[3], (EXPERTS, FF, D), FF ** -0.5, 0.125, ((0, 16), (1, 2)))
    cotangent = bell_draw(key_of[4], (IMAGES, S, D), 1.0, 6.0, ((0, 32),))
    return dict(tokens=tokens, router=router, weight_in=weight_in, weight_out=weight_out, cotangent=cotangent)


def gelu_exact(values):
    return jax.nn.gelu(values, approximate=False)

def group_total(pieces):
    rounded = lax.optimization_barrier(pieces.astype(jnp.bfloat16))
    return lax.optimization_barrier(jnp.sum(rounded.astype(jnp.float32), axis=1)).astype(jnp.bfloat16)

def reference(tokens, router, weight_in, weight_out, cotangent):
    ff_dev = FF // N_DP

    def router_probs(image):
        logits = jnp.dot(image, router, preferred_element_type=jnp.float32)
        return (jax.nn.softmax(logits, axis=0), jax.nn.softmax(logits, axis=1))

    def front_side(pair):
        image, grad_image = pair
        dispatch_prob, combine_prob = router_probs(image)
        dispatch = dispatch_prob.astype(jnp.bfloat16)
        combine = combine_prob.astype(jnp.bfloat16)
        slots = jnp.dot(dispatch.T, image, preferred_element_type=jnp.float32).astype(jnp.bfloat16)
        grad_slots = jnp.dot(combine.T, grad_image, preferred_element_type=jnp.float32).astype(jnp.bfloat16)
        return (slots, grad_slots)
    slots, grad_slots = lax.map(front_side, (tokens, cotangent))

    def expert_side(group):
        slot_rows, grad_rows, w_first, w_second = group
        pre_act = jnp.dot(slot_rows, w_first, preferred_element_type=jnp.float32)
        hidden = gelu_exact(pre_act).astype(jnp.bfloat16)
        pieces = jnp.einsum('ipf,pfd->ipd', hidden.reshape(IMAGES, N_DP, ff_dev).astype(jnp.float32), w_second.reshape(N_DP, ff_dev, D).astype(jnp.float32))
        expert_out = group_total(pieces)
        grad_hidden = jnp.dot(grad_rows, w_second.T, preferred_element_type=jnp.float32)
        _, gelu_back = jax.vjp(gelu_exact, pre_act)
        grad_pre = gelu_back(grad_hidden)[0].astype(jnp.bfloat16)
        grad_second = jnp.dot(hidden.T, grad_rows, preferred_element_type=jnp.float32).astype(jnp.bfloat16)
        grad_first = jnp.dot(slot_rows.T, grad_pre, preferred_element_type=jnp.float32).astype(jnp.bfloat16)
        first_parts = jnp.transpose(w_first.reshape(D, N_DP, ff_dev), (1, 0, 2))
        back_pieces = jnp.einsum('ipf,pdf->ipd', grad_pre.reshape(IMAGES, N_DP, ff_dev).astype(jnp.float32), first_parts.astype(jnp.float32))
        grad_slot = group_total(back_pieces)
        return (expert_out, grad_slot, grad_first, grad_second)
    outs_by_expert, grad_by_expert, grad_weight_in, grad_weight_out = lax.map(expert_side, (jnp.transpose(slots, (1, 0, 2)), jnp.transpose(grad_slots, (1, 0, 2)), weight_in, weight_out))
    expert_outs = jnp.transpose(outs_by_expert, (1, 0, 2))
    grad_slot_all = jnp.transpose(grad_by_expert, (1, 0, 2))

    def back_side(total, group):
        image, grad_image, expert_out, grad_slot = group
        dispatch_prob, combine_prob = router_probs(image)
        dispatch = dispatch_prob.astype(jnp.bfloat16)
        combine = combine_prob.astype(jnp.bfloat16)
        mixed = jnp.dot(combine, expert_out, preferred_element_type=jnp.float32).astype(jnp.bfloat16)
        grad_comb = jnp.dot(grad_image, expert_out.T, preferred_element_type=jnp.float32)
        grad_disp = jnp.dot(image, grad_slot.T, preferred_element_type=jnp.float32)
        part_disp = dispatch_prob * (grad_disp - lax.optimization_barrier(jnp.sum(dispatch_prob * grad_disp, axis=0, keepdims=True)))
        part_comb = combine_prob * (grad_comb - lax.optimization_barrier(jnp.sum(combine_prob * grad_comb, axis=1, keepdims=True)))
        grad_logits = (part_disp + part_comb).astype(jnp.bfloat16)
        grad_image_out = (jnp.dot(dispatch, grad_slot, preferred_element_type=jnp.float32) + jnp.dot(grad_logits, router.T, preferred_element_type=jnp.float32)).astype(jnp.bfloat16)
        router_term = jnp.dot(image.T, grad_logits, preferred_element_type=jnp.float32)
        return (total + router_term, (mixed, grad_image_out))
    start = jnp.zeros((D, EXPERTS), jnp.float32)
    grad_router, (mixed, grad_tokens) = lax.scan(back_side, start, (tokens, cotangent, expert_outs, grad_slot_all))
    return (mixed, grad_tokens, grad_router, grad_weight_in, grad_weight_out)
```

```python
import functools
import math

import jax
import jax.numpy as jnp
from jax import lax
from jax.experimental import pallas as pl
from jax.experimental.pallas import tpu as pltpu
from jax.sharding import PartitionSpec as P

F32 = jnp.float32
BF16 = jnp.bfloat16
MIB = 1024 * 1024


def dot(left, right, left_dim=1, right_dim=0):
    return lax.dot_general(
        left, right, (((left_dim,), (right_dim,)), ((), ())), preferred_element_type=F32
    )


def iota(shape, dim):
    return lax.broadcasted_iota(jnp.int32, shape, dim)


def spread(per, experts):
    shape = (2 * experts, experts)
    row = iota(shape, 0)
    picked = (row // (2 * per)) * per + row % per
    return (picked == iota(shape, 1)).astype(BF16)


def first_half(per, shape):
    return iota(shape, 1) % (2 * per) < per


def front_kernel(per, tokens, router_t, cotangent, rows, disp, comb):
    experts = router_t.shape[0]
    paired_router = dot(spread(per, experts), router_t[...]).astype(BF16)
    logits = dot(tokens[...], paired_router, 1, 1)
    first = first_half(per, logits.shape)
    down = jnp.exp(logits - jnp.max(logits, axis=0, keepdims=True))
    disp_prob = down / jnp.sum(down, axis=0, keepdims=True)
    across = jnp.exp(logits - jnp.max(logits, axis=1, keepdims=True))
    comb_prob = across / jnp.sum(jnp.where(first, across, 0.0), axis=1, keepdims=True)
    disp[...] = disp_prob
    comb[...] = comb_prob
    disp_cols = jnp.where(first, disp_prob, 0.0).astype(BF16)
    comb_cols = jnp.where(first, 0.0, comb_prob).astype(BF16)
    rows[...] = (
        dot(disp_cols, tokens[...], 0, 0) + dot(comb_cols, cotangent[...], 0, 0)
    ).astype(BF16)


def front(per, tokens, router_t, cotangent):
    seq, width = tokens.shape
    experts = router_t.shape[0]
    return pl.pallas_call(
        functools.partial(front_kernel, per),
        out_shape=(
            jax.ShapeDtypeStruct((2 * experts, width), BF16),
            jax.ShapeDtypeStruct((seq, 2 * experts), F32),
            jax.ShapeDtypeStruct((seq, 2 * experts), F32),
        ),
        compiler_params=pltpu.CompilerParams(vmem_limit_bytes=32 * MIB),
        cost_estimate=pl.CostEstimate(
            flops=12 * seq * width * experts, bytes_accessed=6 * seq * width, transcendentals=0
        ),
        name="front",
    )(tokens, router_t, cotangent)


def sort_matrix(images, wide, transposed):
    shape = (images * wide, images * wide)
    to, start = (iota(shape, 1), iota(shape, 0)) if transposed else (iota(shape, 0), iota(shape, 1))
    return ((to % images) * wide + to // images == start).astype(BF16)


def experts_kernel(
    per, group, rows, w_first, w_second, back_rows, slots_out, grads_out, hidden_out, pre_out, sorted_rows, results
):
    wide = 2 * per
    images = sorted_rows.shape[1]
    width = rows.shape[1]
    step = pl.program_id(0)
    block = group * wide

    @pl.when(step == 0)
    def _():
        matrix = sort_matrix(group, wide, False)
        for part in range(images // group):
            moved = dot(matrix, rows[part * block : (part + 1) * block, :]).astype(BF16)
            for j in range(wide):
                sorted_rows[j, part * group : (part + 1) * group, :] = moved[
                    j * group : (j + 1) * group, :
                ]

    slots = sorted_rows[step]
    grads = sorted_rows[per + step]
    first = w_first[0]
    second = w_second[0]
    pre_act = dot(slots, first)
    phi = 0.5 * (1.0 + lax.erf(pre_act * math.sqrt(0.5)))
    density = jnp.exp(pre_act * pre_act * -0.5) * (1.0 / math.sqrt(2.0 * math.pi))
    hidden = (pre_act * phi).astype(BF16)
    results[step] = dot(hidden, second).astype(BF16)
    grad_pre = ((phi + pre_act * density) * dot(grads, second, 1, 1)).astype(BF16)
    results[per + step] = dot(grad_pre, first, 1, 1).astype(BF16)
    slots_out[0] = slots
    grads_out[0] = grads
    hidden_out[0] = hidden
    pre_out[0] = grad_pre

    @pl.when(step == per - 1)
    def _():
        matrix = sort_matrix(group, wide, True)
        for part in range(images // group):
            mine = jnp.concatenate(
                [results[j, part * group : (part + 1) * group, :] for j in range(wide)], axis=0
            )
            back_rows[part * block : (part + 1) * block, :] = dot(matrix, mine).astype(BF16)


def run_experts(rows, w_first, w_second):
    per, width, units = w_first.shape
    total = rows.shape[0]
    images = total // (2 * per)
    group = math.gcd(images, 32)
    whole = pl.BlockSpec((total, width), lambda k: (0, 0))
    per_expert = lambda a, b: pl.BlockSpec((1, a, b), lambda k: (k, 0, 0))
    return pl.pallas_call(
        functools.partial(experts_kernel, per, group),
        grid=(per,),
        in_specs=[whole, per_expert(width, units), per_expert(units, width)],
        out_specs=[
            whole,
            per_expert(images, width),
            per_expert(images, width),
            per_expert(images, units),
            per_expert(images, units),
        ],
        out_shape=(
            jax.ShapeDtypeStruct((total, width), BF16),
            jax.ShapeDtypeStruct((per, images, width), BF16),
            jax.ShapeDtypeStruct((per, images, width), BF16),
            jax.ShapeDtypeStruct((per, images, units), BF16),
            jax.ShapeDtypeStruct((per, images, units), BF16),
        ),
        scratch_shapes=[
            pltpu.VMEM((2 * per, images, width), BF16),
            pltpu.VMEM((2 * per, images, width), BF16),
        ],
        compiler_params=pltpu.CompilerParams(vmem_limit_bytes=40 * MIB),
        cost_estimate=pl.CostEstimate(
            flops=8 * per * images * width * units,
            bytes_accessed=4 * per * width * units,
            transcendentals=0,
        ),
        name="experts",
    )(rows, w_first, w_second)


def outer_kernel(left, right, out):
    out[0] = dot(left[0], right[0], 0, 0).astype(BF16)


def outer(left, right, name):
    per, images, height = left.shape
    units = right.shape[2]
    per_expert = lambda a, b: pl.BlockSpec((1, a, b), lambda k: (k, 0, 0))
    return pl.pallas_call(
        outer_kernel,
        grid=(per,),
        in_specs=[per_expert(images, height), per_expert(images, units)],
        out_specs=per_expert(height, units),
        out_shape=jax.ShapeDtypeStruct((per, height, units), BF16),
        compiler_params=pltpu.CompilerParams(vmem_limit_bytes=32 * MIB),
        cost_estimate=pl.CostEstimate(
            flops=2 * per * images * height * units,
            bytes_accessed=2 * per * height * units,
            transcendentals=0,
        ),
        name=name,
    )(left, right)


def logits_kernel(per, tokens, cotangent, pieces, disp, comb, chunks, outs, grad_logits):
    rows = jnp.sum(pieces[...].astype(F32), axis=0).astype(BF16)
    outs[...] = rows
    disp_prob = disp[...]
    comb_prob = comb[...]
    first = first_half(per, disp_prob.shape)
    grad_comb = dot(cotangent[...], rows, 1, 1)
    grad_disp = dot(tokens[...], rows, 1, 1)
    part_disp = disp_prob * (
        grad_disp - jnp.sum(disp_prob * grad_disp, axis=0, keepdims=True)
    )
    comb_sum = jnp.sum(jnp.where(first, comb_prob * grad_comb, 0.0), axis=1, keepdims=True)
    part_comb = comb_prob * (grad_comb - comb_sum)
    both = jnp.where(first, part_comb, part_disp)
    cols = both.shape[1]
    other = jnp.where(first, pltpu.roll(both, cols - per, 1), pltpu.roll(both, per, 1))
    paired = (both + other).astype(BF16)
    grad_logits[...] = jnp.where(first, paired.astype(F32), 0.0).astype(BF16)
    experts = cols // 2
    one_each = dot(paired, pick_first(per, experts)).astype(BF16)
    term = dot(one_each, tokens[...], 0, 0).astype(BF16)
    count, height, lanes = chunks.shape
    across = term.shape[1] // lanes
    for index in range(count):
        top, side = index // across, index % across
        chunks[index] = term[
            top * height : (top + 1) * height, side * lanes : (side + 1) * lanes
        ]


def pick_first(per, experts):
    shape = (2 * experts, experts)
    row, col = iota(shape, 0), iota(shape, 1)
    return (row == (col // per) * (2 * per) + col % per).astype(BF16)


def finish_logits(per, devices, tokens, cotangent, pieces, disp, comb):
    seq, width = tokens.shape
    cols = disp.shape[1]
    height = (cols // 2) * width // (devices * 128)
    return pl.pallas_call(
        functools.partial(logits_kernel, per),
        out_shape=(
            jax.ShapeDtypeStruct((devices, height, 128), BF16),
            jax.ShapeDtypeStruct((cols, width), BF16),
            jax.ShapeDtypeStruct((seq, cols), BF16),
        ),
        compiler_params=pltpu.CompilerParams(vmem_limit_bytes=32 * MIB),
        cost_estimate=pl.CostEstimate(
            flops=6 * seq * width * cols, bytes_accessed=6 * seq * width, transcendentals=0
        ),
        name="grad_logits",
    )(tokens, cotangent, pieces, disp, comb)


def images_kernel(per, outs, disp, comb, grad_logits, router_t, mixed, grad_tokens):
    experts = router_t.shape[0]
    rows = outs[...]
    first = first_half(per, disp.shape)
    comb_cols = jnp.where(first, comb[...], 0.0).astype(BF16)
    mixed[...] = dot(comb_cols, rows).astype(BF16)
    disp_cols = jnp.where(first, 0.0, disp[...]).astype(BF16)
    paired_router = dot(spread(per, experts), router_t[...]).astype(BF16)
    grad_tokens[...] = (dot(disp_cols, rows) + dot(grad_logits[...], paired_router)).astype(BF16)


def finish_images(per, outs, disp, comb, grad_logits, router_t):
    seq, cols = disp.shape
    width = outs.shape[1]
    return pl.pallas_call(
        functools.partial(images_kernel, per),
        out_shape=(
            jax.ShapeDtypeStruct((seq, width), BF16),
            jax.ShapeDtypeStruct((seq, width), BF16),
        ),
        compiler_params=pltpu.CompilerParams(vmem_limit_bytes=32 * MIB),
        cost_estimate=pl.CostEstimate(
            flops=6 * seq * width * cols, bytes_accessed=6 * seq * width, transcendentals=0
        ),
        name="mixed_and_grad_tokens",
    )(outs, disp, comb, grad_logits, router_t)


def sum_kernel(parts, out):
    total = jnp.sum(parts[...].astype(F32), axis=0, keepdims=True)
    out[...] = jnp.broadcast_to(total, out.shape).astype(BF16)


def sum_chunks(parts):
    return pl.pallas_call(
        sum_kernel,
        out_shape=jax.ShapeDtypeStruct(parts.shape, BF16),
        name="sum_chunks",
    )(parts)


def join_kernel(chunks, out):
    count, height, lanes = chunks.shape
    across = out.shape[1] // lanes
    for index in range(count):
        top, side = index // across, index % across
        out[top * height : (top + 1) * height, side * lanes : (side + 1) * lanes] = chunks[
            index
        ].astype(F32)


def join_chunks(chunks, experts, width):
    return pl.pallas_call(
        join_kernel,
        out_shape=jax.ShapeDtypeStruct((experts, width), F32),
        name="join_chunks",
    )(chunks)


def local(devices, tokens, router, weight_in, weight_out, cotangent):
    per = weight_in.shape[0]
    experts = router.shape[1]
    tokens, cotangent = tokens[0], cotangent[0]
    width = tokens.shape[1]
    router_t = router.T
    both = ("dp", "expert")

    rows, disp, comb = front(per, tokens, router_t, cotangent)
    chips = experts // per
    rows = lax.all_to_all(
        rows.reshape(chips, 2 * per, width), "expert", split_axis=0, concat_axis=0, tiled=True
    )
    rows = lax.all_gather(rows, "dp", axis=0, tiled=True)
    rows = rows.reshape(-1, width)
    back_rows, slots, grads, hidden, grad_pre = run_experts(rows, weight_in, weight_out)
    pieces = lax.all_to_all(
        back_rows.reshape(devices, 2 * per, width), both, split_axis=0, concat_axis=0, tiled=True
    )
    pieces = pieces.reshape(devices // chips, 2 * experts, width)
    grad_second = outer(hidden, grads, "grad_weight_out")
    grad_first = outer(slots, grad_pre, "grad_weight_in")
    chunks, outs, grad_logits = finish_logits(per, devices, tokens, cotangent, pieces, disp, comb)
    parts = lax.all_to_all(chunks, both, split_axis=0, concat_axis=0, tiled=True)
    sums = lax.all_to_all(sum_chunks(parts), both, split_axis=0, concat_axis=0, tiled=True)
    mixed, grad_tokens = finish_images(per, outs, disp, comb, grad_logits, router_t)
    grad_router = join_chunks(sums, experts, width).T
    return (mixed[None], grad_tokens[None], grad_router, grad_first, grad_second)


def solution(mesh):
    return jax.shard_map(
        functools.partial(local, mesh.size),
        mesh=mesh,
        in_specs=(
            P(("dp", "expert"), None, None),
            P(),
            P("expert", None, "dp"),
            P("expert", "dp", None),
            P(("dp", "expert"), None, None),
        ),
        out_specs=(
            P(("dp", "expert"), None, None),
            P(("dp", "expert"), None, None),
            P(),
            P("expert", None, "dp"),
            P("expert", "dp", None),
        ),
        check_vma=False,
    )
```

```python
import functools
import math

import jax
import jax.numpy as jnp
from jax import lax
from jax.experimental import pallas as pl
from jax.experimental.pallas import tpu as pltpu
from jax.sharding import PartitionSpec as P

F32 = jnp.float32
BF16 = jnp.bfloat16
MIB = 1024 * 1024


def dot(left, right, left_dim=1, right_dim=0):
    return lax.dot_general(
        left, right, (((left_dim,), (right_dim,)), ((), ())), preferred_element_type=F32
    )


def iota(shape, dim):
    return lax.broadcasted_iota(jnp.int32, shape, dim)


def picked_expert(per, experts, me, rows):
    chips = experts // per
    return ((me + rows // (2 * per)) % chips) * per + rows % per


def spread(per, experts, me):
    shape = (2 * experts, experts)
    return (picked_expert(per, experts, me, iota(shape, 0)) == iota(shape, 1)).astype(BF16)


def first_half(per, shape):
    return iota(shape, 1) % (2 * per) < per


def front_kernel(per, tokens_hbm, router_hbm, cotangent_hbm, *refs):
    *rows, disp, comb, tokens, router_t, cotangent, sems = refs
    copies = [
        pltpu.make_async_copy(source, target, sems.at[index])
        for index, (source, target) in enumerate(
            ((router_hbm, router_t), (tokens_hbm, tokens), (cotangent_hbm, cotangent))
        )
    ]
    for copy in copies:
        copy.start()
    experts = router_t.shape[0]
    matrix = spread(per, experts, lax.axis_index("expert"))
    copies[0].wait()
    paired_router = dot(matrix, router_t[...]).astype(BF16)
    copies[1].wait()
    logits = dot(tokens[...], paired_router, 1, 1)
    first = first_half(per, logits.shape)
    down = jnp.exp(logits - jnp.max(logits, axis=0, keepdims=True))
    disp_prob = down / jnp.sum(down, axis=0, keepdims=True)
    across = jnp.exp(logits - jnp.max(logits, axis=1, keepdims=True))
    comb_prob = across / jnp.sum(jnp.where(first, across, 0.0), axis=1, keepdims=True)
    disp[...] = disp_prob
    comb[...] = comb_prob
    disp_cols = jnp.where(first, disp_prob, 0.0).astype(BF16)
    comb_cols = jnp.where(first, 0.0, comb_prob).astype(BF16)
    copies[2].wait()
    total = dot(disp_cols, tokens[...], 0, 0) + dot(comb_cols, cotangent[...], 0, 0)
    for block, out in enumerate(rows):
        out[...] = total[block * 2 * per : (block + 1) * 2 * per, :].astype(BF16)


def front(per, tokens, router_t, cotangent):
    seq, width = tokens.shape
    experts = router_t.shape[0]
    chips = experts // per
    return pl.pallas_call(
        functools.partial(front_kernel, per),
        in_specs=[pl.BlockSpec(memory_space=pltpu.HBM)] * 3,
        out_shape=[jax.ShapeDtypeStruct((2 * per, width), BF16)] * chips
        + [jax.ShapeDtypeStruct((seq, 2 * experts), F32)] * 2,
        scratch_shapes=[
            pltpu.VMEM(tokens.shape, BF16),
            pltpu.VMEM(router_t.shape, BF16),
            pltpu.VMEM(cotangent.shape, BF16),
            pltpu.SemaphoreType.DMA((3,)),
        ],
        compiler_params=pltpu.CompilerParams(vmem_limit_bytes=32 * MIB),
        cost_estimate=pl.CostEstimate(
            flops=12 * seq * width * experts, bytes_accessed=6 * seq * width, transcendentals=0
        ),
        name="front",
    )(tokens, router_t, cotangent)


def pack_kernel(*refs):
    *blocks, out = refs
    out[...] = jnp.concatenate([block[...].astype(F32) for block in blocks], axis=0).astype(BF16)


def pack(blocks):
    height, width = blocks[0].shape
    return pl.pallas_call(
        pack_kernel,
        out_shape=jax.ShapeDtypeStruct((len(blocks) * height, width), BF16),
        name="pack",
    )(*blocks)


def unpack_kernel(chips, *refs):
    pieces, outs = refs[:-chips], refs[-chips:]
    total = sum(piece[...].astype(F32) for piece in pieces)
    height = outs[0].shape[0]
    for block, out in enumerate(outs):
        out[...] = total[block * height : (block + 1) * height, :].astype(BF16)


def sum_and_unpack(chips, pieces):
    height, width = pieces[0].shape
    return pl.pallas_call(
        functools.partial(unpack_kernel, chips),
        out_shape=[jax.ShapeDtypeStruct((height // chips, width), BF16)] * chips,
        name="sum_groups",
    )(*pieces)


def shifted(value, axis, by):
    size = lax.axis_size(axis)
    return lax.ppermute(value, axis, [(i, (i + by) % size) for i in range(size)])


def exchange(blocks, axis, sign):
    return [blocks[0]] + [shifted(block, axis, sign * k) for k, block in enumerate(blocks) if k]


def sort_matrix(images, wide, transposed):
    shape = (images * wide, images * wide)
    to, start = (iota(shape, 1), iota(shape, 0)) if transposed else (iota(shape, 0), iota(shape, 1))
    return ((to % images) * wide + to // images == start).astype(BF16)


def experts_kernel(per, groups, *refs):
    rows, (w_first, w_second), refs = refs[:groups], refs[groups : groups + 2], refs[groups + 2 :]
    back_rows, refs = refs[:groups], refs[groups:]
    slots_out, grads_out, hidden_out, pre_out, sorted_rows, results = refs
    wide = 2 * per
    size = rows[0].shape[0] // wide
    step = pl.program_id(0)

    @pl.when(step == 0)
    def _():
        matrix = sort_matrix(size, wide, False)
        for part in range(groups):
            moved = dot(matrix, rows[part][...]).astype(BF16)
            for j in range(wide):
                sorted_rows[j, part * size : (part + 1) * size, :] = moved[
                    j * size : (j + 1) * size, :
                ]

    slots = sorted_rows[step]
    grads = sorted_rows[per + step]
    first = w_first[0]
    second = w_second[0]
    pre_act = dot(slots, first)
    phi = 0.5 * (1.0 + lax.erf(pre_act * math.sqrt(0.5)))
    density = jnp.exp(pre_act * pre_act * -0.5) * (1.0 / math.sqrt(2.0 * math.pi))
    hidden = (pre_act * phi).astype(BF16)
    results[step] = dot(hidden, second).astype(BF16)
    grad_pre = ((phi + pre_act * density) * dot(grads, second, 1, 1)).astype(BF16)
    results[per + step] = dot(grad_pre, first, 1, 1).astype(BF16)
    slots_out[0] = slots
    grads_out[0] = grads
    hidden_out[0] = hidden
    pre_out[0] = grad_pre

    @pl.when(step == per - 1)
    def _():
        matrix = sort_matrix(size, wide, True)
        for part in range(groups):
            mine = jnp.concatenate(
                [results[j, part * size : (part + 1) * size, :] for j in range(wide)], axis=0
            )
            back_rows[part][...] = dot(matrix, mine).astype(BF16)


def run_experts(rows, w_first, w_second):
    per, width, units = w_first.shape
    groups = len(rows)
    total = rows[0].shape[0]
    images = groups * total // (2 * per)
    whole = pl.BlockSpec((total, width), lambda k: (0, 0))
    per_expert = lambda a, b: pl.BlockSpec((1, a, b), lambda k: (k, 0, 0))
    results = pl.pallas_call(
        functools.partial(experts_kernel, per, groups),
        grid=(per,),
        in_specs=[whole] * groups + [per_expert(width, units), per_expert(units, width)],
        out_specs=[whole] * groups
        + [per_expert(images, width)] * 2
        + [per_expert(images, units)] * 2,
        out_shape=[jax.ShapeDtypeStruct((total, width), BF16)] * groups
        + [jax.ShapeDtypeStruct((per, images, width), BF16)] * 2
        + [jax.ShapeDtypeStruct((per, images, units), BF16)] * 2,
        scratch_shapes=[
            pltpu.VMEM((2 * per, images, width), BF16),
            pltpu.VMEM((2 * per, images, width), BF16),
        ],
        compiler_params=pltpu.CompilerParams(vmem_limit_bytes=40 * MIB),
        cost_estimate=pl.CostEstimate(
            flops=8 * per * images * width * units,
            bytes_accessed=4 * per * width * units,
            transcendentals=0,
        ),
        name="experts",
    )(*rows, w_first, w_second)
    return results[:groups], results[groups:]


def outer_kernel(left, right, out):
    out[0] = dot(left[0], right[0], 0, 0).astype(BF16)


def outer(left, right, name):
    per, images, height = left.shape
    units = right.shape[2]
    per_expert = lambda a, b: pl.BlockSpec((1, a, b), lambda k: (k, 0, 0))
    return pl.pallas_call(
        outer_kernel,
        grid=(per,),
        in_specs=[per_expert(images, height), per_expert(images, units)],
        out_specs=per_expert(height, units),
        out_shape=jax.ShapeDtypeStruct((per, height, units), BF16),
        compiler_params=pltpu.CompilerParams(vmem_limit_bytes=32 * MIB),
        cost_estimate=pl.CostEstimate(
            flops=2 * per * images * height * units,
            bytes_accessed=2 * per * height * units,
            transcendentals=0,
        ),
        name=name,
    )(left, right)


def logits_kernel(per, tokens, cotangent, disp, comb, *refs):
    *blocks, chunks, outs, grad_logits = refs
    rows = jnp.concatenate([block[...].astype(F32) for block in blocks], axis=0).astype(BF16)
    outs[...] = rows
    disp_prob = disp[...]
    comb_prob = comb[...]
    first = first_half(per, disp_prob.shape)
    grad_comb = dot(cotangent[...], rows, 1, 1)
    grad_disp = dot(tokens[...], rows, 1, 1)
    part_disp = disp_prob * (
        grad_disp - jnp.sum(disp_prob * grad_disp, axis=0, keepdims=True)
    )
    comb_sum = jnp.sum(jnp.where(first, comb_prob * grad_comb, 0.0), axis=1, keepdims=True)
    part_comb = comb_prob * (grad_comb - comb_sum)
    both = jnp.where(first, part_comb, part_disp)
    cols = both.shape[1]
    other = jnp.where(first, pltpu.roll(both, cols - per, 1), pltpu.roll(both, per, 1))
    paired = (both + other).astype(BF16)
    grad_logits[...] = jnp.where(first, paired.astype(F32), 0.0).astype(BF16)
    experts = cols // 2
    one_each = dot(paired, pick_first(per, experts, lax.axis_index("expert"))).astype(BF16)
    term = dot(one_each, tokens[...], 0, 0).astype(BF16)
    count, height, lanes = chunks.shape
    across = term.shape[1] // lanes
    for index in range(count):
        top, side = index // across, index % across
        chunks[index] = term[
            top * height : (top + 1) * height, side * lanes : (side + 1) * lanes
        ]


def pick_first(per, experts, me):
    shape = (2 * experts, experts)
    row = iota(shape, 0)
    same = picked_expert(per, experts, me, row) == iota(shape, 1)
    return (same & (row % (2 * per) < per)).astype(BF16)


def finish_logits(per, devices, tokens, cotangent, disp, comb, blocks):
    seq, width = tokens.shape
    cols = disp.shape[1]
    height = (cols // 2) * width // (devices * 128)
    return pl.pallas_call(
        functools.partial(logits_kernel, per),
        out_shape=(
            jax.ShapeDtypeStruct((devices, height, 128), BF16),
            jax.ShapeDtypeStruct((cols, width), BF16),
            jax.ShapeDtypeStruct((seq, cols), BF16),
        ),
        compiler_params=pltpu.CompilerParams(vmem_limit_bytes=32 * MIB),
        cost_estimate=pl.CostEstimate(
            flops=6 * seq * width * cols, bytes_accessed=6 * seq * width, transcendentals=0
        ),
        name="grad_logits",
    )(tokens, cotangent, disp, comb, *blocks)


def images_kernel(per, outs, disp, comb, grad_logits, router_t, mixed, grad_tokens):
    experts = router_t.shape[0]
    rows = outs[...]
    first = first_half(per, disp.shape)
    comb_cols = jnp.where(first, comb[...], 0.0).astype(BF16)
    mixed[...] = dot(comb_cols, rows).astype(BF16)
    disp_cols = jnp.where(first, 0.0, disp[...]).astype(BF16)
    matrix = spread(per, experts, lax.axis_index("expert"))
    paired_router = dot(matrix, router_t[...]).astype(BF16)
    grad_tokens[...] = (dot(disp_cols, rows) + dot(grad_logits[...], paired_router)).astype(BF16)


def finish_images(per, outs, disp, comb, grad_logits, router_t):
    seq, cols = disp.shape
    width = outs.shape[1]
    return pl.pallas_call(
        functools.partial(images_kernel, per),
        out_shape=(
            jax.ShapeDtypeStruct((seq, width), BF16),
            jax.ShapeDtypeStruct((seq, width), BF16),
        ),
        compiler_params=pltpu.CompilerParams(vmem_limit_bytes=32 * MIB),
        cost_estimate=pl.CostEstimate(
            flops=6 * seq * width * cols, bytes_accessed=6 * seq * width, transcendentals=0
        ),
        name="mixed_and_grad_tokens",
    )(outs, disp, comb, grad_logits, router_t)


def sum_kernel(parts, out):
    total = jnp.sum(parts[...].astype(F32), axis=0, keepdims=True)
    out[...] = jnp.broadcast_to(total, out.shape).astype(BF16)


def sum_chunks(parts):
    return pl.pallas_call(
        sum_kernel,
        out_shape=jax.ShapeDtypeStruct(parts.shape, BF16),
        name="sum_chunks",
    )(parts)


def join_kernel(chunks, out):
    count, height, lanes = chunks.shape
    across = out.shape[1] // lanes
    for index in range(count):
        top, side = index // across, index % across
        out[top * height : (top + 1) * height, side * lanes : (side + 1) * lanes] = chunks[
            index
        ].astype(F32)


def join_chunks(chunks, experts, width):
    return pl.pallas_call(
        join_kernel,
        out_shape=jax.ShapeDtypeStruct((experts, width), F32),
        name="join_chunks",
    )(chunks)


def local(devices, tokens, router, weight_in, weight_out, cotangent):
    per = weight_in.shape[0]
    experts = router.shape[1]
    tokens, cotangent = tokens[0], cotangent[0]
    width = tokens.shape[1]
    router_t = router.T
    both = ("dp", "expert")

    *blocks, disp, comb = front(per, tokens, router_t, cotangent)
    chips = experts // per
    groups = devices // chips
    mine = pack(exchange(blocks, "expert", 1))
    rows = exchange([mine] * groups, "dp", 1)
    back_rows, (slots, grads, hidden, grad_pre) = run_experts(rows, weight_in, weight_out)
    pieces = exchange(back_rows, "dp", -1)
    blocks = exchange(sum_and_unpack(chips, pieces), "expert", -1)
    grad_second = outer(hidden, grads, "grad_weight_out")
    grad_first = outer(slots, grad_pre, "grad_weight_in")
    chunks, outs, grad_logits = finish_logits(
        per, devices, tokens, cotangent, disp, comb, blocks
    )
    parts = lax.all_to_all(chunks, both, split_axis=0, concat_axis=0, tiled=True)
    sums = lax.all_to_all(sum_chunks(parts), both, split_axis=0, concat_axis=0, tiled=True)
    mixed, grad_tokens = finish_images(per, outs, disp, comb, grad_logits, router_t)
    grad_router = join_chunks(sums, experts, width).T
    return (mixed[None], grad_tokens[None], grad_router, grad_first, grad_second)


def solution(mesh):
    return jax.shard_map(
        functools.partial(local, mesh.size),
        mesh=mesh,
        in_specs=(
            P(("dp", "expert"), None, None),
            P(),
            P("expert", None, "dp"),
            P("expert", "dp", None),
            P(("dp", "expert"), None, None),
        ),
        out_specs=(
            P(("dp", "expert"), None, None),
            P(("dp", "expert"), None, None),
            P(),
            P("expert", None, "dp"),
            P("expert", "dp", None),
        ),
        check_vma=False,
    )
```

```python
import functools
import math

import jax
import jax.numpy as jnp
from jax import lax
from jax.experimental import pallas as pl
from jax.experimental.pallas import tpu as pltpu
from jax.sharding import PartitionSpec as P

F32 = jnp.float32
BF16 = jnp.bfloat16
MIB = 1024 * 1024


def dot(left, right, left_dim=1, right_dim=0):
    return lax.dot_general(
        left, right, (((left_dim,), (right_dim,)), ((), ())), preferred_element_type=F32
    )


def iota(shape, dim):
    return lax.broadcasted_iota(jnp.int32, shape, dim)


def in_hbm(value):
    return pltpu.with_memory_space_constraint(value, pltpu.HBM)


def call(kernel, name, out_shape, limit, flops, moved, **more):
    return pl.pallas_call(
        kernel,
        out_shape=out_shape,
        compiler_params=pltpu.CompilerParams(vmem_limit_bytes=limit * MIB),
        cost_estimate=pl.CostEstimate(flops=flops, bytes_accessed=moved, transcendentals=0),
        name=name,
        **more,
    )


def picked_expert(per, rows):
    return (rows // (2 * per)) * per + rows % per


def spread(per, experts):
    shape = (2 * experts, experts)
    return (picked_expert(per, iota(shape, 0)) == iota(shape, 1)).astype(BF16)


def pick_first(per, experts):
    shape = (2 * experts, experts)
    row = iota(shape, 0)
    return ((picked_expert(per, row) == iota(shape, 1)) & (row % (2 * per) < per)).astype(BF16)


def first_half(per, shape):
    return iota(shape, 1) % (2 * per) < per


def front_kernel(
    per, tokens_hbm, router_hbm, cotangent_hbm, rows, disp, comb, tokens, cotangent, router_t, sems
):
    copies = [
        pltpu.make_async_copy(source, target, sems.at[index])
        for index, (source, target) in enumerate(
            ((router_hbm, router_t), (tokens_hbm, tokens), (cotangent_hbm, cotangent))
        )
    ]
    for copy in copies:
        copy.start()
    matrix = spread(per, router_t.shape[0])
    copies[0].wait()
    paired_router = dot(matrix, router_t[...]).astype(BF16)
    copies[1].wait()
    logits = dot(tokens[...], paired_router, 1, 1)
    first = first_half(per, logits.shape)
    down = jnp.exp(logits - jnp.max(logits, axis=0, keepdims=True))
    disp_prob = down / jnp.sum(down, axis=0, keepdims=True)
    across = jnp.exp(logits - jnp.max(logits, axis=1, keepdims=True))
    comb_prob = across / jnp.sum(jnp.where(first, across, 0.0), axis=1, keepdims=True)
    disp[...] = disp_prob
    comb[...] = comb_prob
    disp_cols = jnp.where(first, disp_prob, 0.0).astype(BF16)
    comb_cols = jnp.where(first, 0.0, comb_prob).astype(BF16)
    copies[2].wait()
    rows[...] = (
        dot(disp_cols, tokens[...], 0, 0) + dot(comb_cols, cotangent[...], 0, 0)
    ).astype(BF16)


def front(per, tokens, router_t, cotangent):
    seq, width = tokens.shape
    experts = router_t.shape[0]
    return call(
        functools.partial(front_kernel, per),
        "front",
        (
            pltpu.VMEM((2 * experts, width), BF16),
            pltpu.VMEM((seq, 2 * experts), F32),
            pltpu.VMEM((seq, 2 * experts), F32),
            pltpu.VMEM(tokens.shape, BF16),
            pltpu.VMEM(cotangent.shape, BF16),
        ),
        8,
        12 * seq * width * experts,
        6 * seq * width,
        in_specs=[pl.BlockSpec(memory_space=pltpu.HBM)] * 3,
        scratch_shapes=[pltpu.VMEM(router_t.shape, BF16), pltpu.SemaphoreType.DMA((3,))],
    )(in_hbm(tokens), in_hbm(router_t), in_hbm(cotangent))


def fetch_kernel(first_hbm, second_hbm, after, first, second, sems):
    copies = [
        pltpu.make_async_copy(source.at[k], target.at[k], sems.at[index, k])
        for k in range(first.shape[0])
        for index, (source, target) in enumerate(((first_hbm, first), (second_hbm, second)))
    ]
    for copy in copies:
        copy.start()
    for copy in copies:
        copy.wait()


def fetch(w_first, w_second, after):
    return call(
        fetch_kernel,
        "fetch_weights",
        (pltpu.VMEM(w_first.shape, BF16), pltpu.VMEM(w_second.shape, BF16)),
        2,
        0,
        4 * w_first.size,
        in_specs=[pl.BlockSpec(memory_space=pltpu.HBM)] * 2 + [pl.BlockSpec(memory_space=pl.ANY)],
        scratch_shapes=[pltpu.SemaphoreType.DMA((2, w_first.shape[0]))],
    )(in_hbm(w_first), in_hbm(w_second), after)


def shifted(value, axis, by):
    size = lax.axis_size(axis)
    return lax.ppermute(value, axis, [(i, (i + by) % size) for i in range(size)])


def exchange(blocks, axis, sign):
    return [blocks[0]] + [shifted(block, axis, sign * k) for k, block in enumerate(blocks) if k]


def add_kernel(*refs):
    *pieces, out = refs
    out[...] = sum(piece[...].astype(F32) for piece in pieces).astype(BF16)


def add(pieces, name):
    size = pieces[0].size
    return call(
        add_kernel, name, pltpu.VMEM(pieces[0].shape, BF16), 4, len(pieces) * size, 4 * size
    )(*pieces)


def sort_matrix(images, wide, transposed):
    shape = (images * wide, images * wide)
    to, start = (iota(shape, 1), iota(shape, 0)) if transposed else (iota(shape, 0), iota(shape, 1))
    return ((to % images) * wide + to // images == start).astype(BF16)


def experts_kernel(per, groups, *refs):
    rows, (w_first, w_second), refs = refs[:groups], refs[groups : groups + 2], refs[groups + 2 :]
    back_rows, (slots_out, grads_out, hidden_out, pre_out) = refs[:groups], refs[groups:]
    wide = 2 * per
    size = rows[0].shape[0] // wide
    matrix = sort_matrix(size, wide, False)
    for part in range(groups):
        moved = dot(matrix, rows[part][...]).astype(BF16)
        for j in range(wide):
            target, k = (slots_out, j) if j < per else (grads_out, j - per)
            target[k, part * size : (part + 1) * size, :] = moved[j * size : (j + 1) * size, :]
    results = [None] * wide
    for k in range(per):
        pre_act = dot(slots_out[k], w_first[k])
        phi = 0.5 * (1.0 + lax.erf(pre_act * math.sqrt(0.5)))
        density = jnp.exp(pre_act * pre_act * -0.5) * (1.0 / math.sqrt(2.0 * math.pi))
        hidden = (pre_act * phi).astype(BF16)
        results[k] = dot(hidden, w_second[k]).astype(BF16)
        grad_hidden = dot(grads_out[k], w_second[k], 1, 1)
        grad_pre = ((phi + pre_act * density) * grad_hidden).astype(BF16)
        results[per + k] = dot(grad_pre, w_first[k], 1, 1).astype(BF16)
        hidden_out[k] = hidden
        pre_out[k] = grad_pre
    matrix = sort_matrix(size, wide, True)
    for part in range(groups):
        mine = jnp.concatenate([value[part * size : (part + 1) * size, :] for value in results])
        back_rows[part][...] = dot(matrix, mine).astype(BF16)


def run_experts(rows, w_first, w_second):
    per, width, units = w_first.shape
    groups = len(rows)
    total = rows[0].shape[0]
    images = groups * total // (2 * per)
    results = call(
        functools.partial(experts_kernel, per, groups),
        "experts",
        [pltpu.VMEM((total, width), BF16)] * groups
        + [pltpu.VMEM((per, images, width), BF16)] * 2
        + [pltpu.VMEM((per, images, units), BF16)] * 2,
        16,
        8 * per * images * width * units,
        4 * per * width * units,
    )(*rows, w_first, w_second)
    return results[:groups], results[groups:]


def outer_kernel(left, right, after, out):
    out[0] = dot(left[0], right[0], 0, 0).astype(BF16)


def outer(left, right, after, name):
    per, images, height = left.shape
    units = right.shape[2]
    per_expert = lambda a, b: pl.BlockSpec((1, a, b), lambda k: (k, 0, 0))
    return call(
        outer_kernel,
        name,
        jax.ShapeDtypeStruct((per, height, units), BF16),
        16,
        2 * per * images * height * units,
        2 * per * height * units,
        grid=(per,),
        in_specs=[
            per_expert(images, height),
            per_expert(images, units),
            pl.BlockSpec(memory_space=pl.ANY),
        ],
        out_specs=per_expert(height, units),
    )(left, right, after)


def logits_kernel(per, groups, tokens, cotangent, disp, comb, outs, after1, after2, *refs):
    *parts, grad_logits, terms = refs
    rows = outs[...]
    disp_prob = disp[...]
    comb_prob = comb[...]
    first = first_half(per, disp_prob.shape)
    grad_comb = dot(cotangent[...], rows, 1, 1)
    grad_disp = dot(tokens[...], rows, 1, 1)
    part_disp = disp_prob * (
        grad_disp - jnp.sum(disp_prob * grad_disp, axis=0, keepdims=True)
    )
    comb_sum = jnp.sum(jnp.where(first, comb_prob * grad_comb, 0.0), axis=1, keepdims=True)
    part_comb = comb_prob * (grad_comb - comb_sum)
    both = jnp.where(first, part_comb, part_disp)
    cols = both.shape[1]
    other = jnp.where(first, pltpu.roll(both, cols - per, 1), pltpu.roll(both, per, 1))
    paired = (both + other).astype(BF16)
    grad_logits[...] = jnp.where(first, paired.astype(F32), 0.0).astype(BF16)
    one_each = dot(paired, pick_first(per, cols // 2)).astype(BF16)
    term = dot(one_each, tokens[...], 0, 0)
    height = terms.shape[1]
    for part in range(groups):
        terms[part] = term[part * height : (part + 1) * height, :].astype(BF16)
    me = lax.axis_index("dp")
    for part, out in enumerate(parts):
        out[...] = terms[lax.rem(me + part, groups)]


def finish_logits(per, groups, tokens, cotangent, disp, comb, outs, after1, after2):
    seq, width = tokens.shape
    cols = disp.shape[1]
    height = cols // 2 // groups
    results = call(
        functools.partial(logits_kernel, per, groups),
        "grad_logits",
        [pltpu.VMEM((height, width), BF16)] * groups + [pltpu.VMEM((seq, cols), BF16)],
        8,
        6 * seq * width * cols,
        6 * seq * width,
        in_specs=[pl.BlockSpec(memory_space=pltpu.VMEM)] * 5
        + [pl.BlockSpec(memory_space=pltpu.HBM)] * 2,
        scratch_shapes=[pltpu.VMEM((groups, height, width), BF16)],
    )(tokens, cotangent, disp, comb, outs, in_hbm(after1), in_hbm(after2))
    return results[:groups], results[groups]


def images_kernel(per, outs, disp, comb, grad_logits, router_t, mixed, grad_tokens):
    rows = outs[...]
    first = first_half(per, disp.shape)
    comb_cols = jnp.where(first, comb[...], 0.0).astype(BF16)
    mixed[...] = dot(comb_cols, rows).astype(BF16)
    disp_cols = jnp.where(first, 0.0, disp[...]).astype(BF16)
    paired_router = dot(spread(per, router_t.shape[0]), router_t[...]).astype(BF16)
    grad_tokens[...] = (dot(disp_cols, rows) + dot(grad_logits[...], paired_router)).astype(BF16)


def finish_images(per, outs, disp, comb, grad_logits, router_t):
    seq, cols = disp.shape
    width = outs.shape[1]
    return call(
        functools.partial(images_kernel, per),
        "mixed_and_grad_tokens",
        (jax.ShapeDtypeStruct((seq, width), BF16), jax.ShapeDtypeStruct((seq, width), BF16)),
        8,
        6 * seq * width * cols,
        6 * seq * width,
    )(outs, disp, comb, grad_logits, router_t)


def join_kernel(*refs):
    *parts, out = refs
    groups = len(parts)
    me = lax.axis_index("dp")
    for part, ref in enumerate(parts):
        out[lax.rem(me - part + groups, groups)] = ref[...].astype(F32)


def join(parts):
    height, width = parts[0].shape
    return call(
        join_kernel,
        "join",
        jax.ShapeDtypeStruct((len(parts), height, width), F32),
        4,
        0,
        6 * height * width,
    )(*parts).reshape(-1, width)


def total_over_devices(parts):
    value = add(exchange(parts, "dp", 1), "add_cores")
    size = lax.axis_size("expert")
    bit = 1
    while bit < size:
        other = lax.ppermute(value, "expert", [(i, i ^ bit) for i in range(size)])
        value = add([value, other], "add_chips")
        bit *= 2
    return join(exchange([value] * len(parts), "dp", 1))


def local(tokens, router, weight_in, weight_out, cotangent):
    per = weight_in.shape[0]
    experts = router.shape[1]
    chips = experts // per
    groups = lax.axis_size("dp")
    tokens, cotangent = tokens[0], cotangent[0]
    width = tokens.shape[1]
    router_t = router.T

    def to_chips(rows):
        blocks = rows.reshape(chips, 2 * per, width)
        blocks = lax.all_to_all(blocks, "expert", split_axis=0, concat_axis=0, tiled=True)
        return blocks.reshape(rows.shape)

    rows, disp, comb, tokens, cotangent = front(per, tokens, router_t, cotangent)
    w_first, w_second = fetch(weight_in, weight_out, comb)
    rows, w_first, w_second = lax.optimization_barrier((to_chips(rows), w_first, w_second))
    rows = exchange([rows] * groups, "dp", 1)
    back_rows, (slots, grads, hidden, grad_pre) = run_experts(rows, w_first, w_second)
    back_rows = add(exchange(back_rows, "dp", -1), "add_groups")
    outs = to_chips(back_rows)
    grad_second = outer(hidden, grads, back_rows, "grad_weight_out")
    grad_first = outer(slots, grad_pre, back_rows, "grad_weight_in")
    parts, grad_logits = finish_logits(
        per, groups, tokens, cotangent, disp, comb, outs, grad_first, grad_second
    )
    mixed, grad_tokens = finish_images(per, outs, disp, comb, grad_logits, router_t)
    grad_router = total_over_devices(parts).T
    return (mixed[None], grad_tokens[None], grad_router, grad_first, grad_second)


def solution(mesh):
    return jax.shard_map(
        local,
        mesh=mesh,
        in_specs=(
            P(("dp", "expert"), None, None),
            P(),
            P("expert", None, "dp"),
            P("expert", "dp", None),
            P(("dp", "expert"), None, None),
        ),
        out_specs=(
            P(("dp", "expert"), None, None),
            P(("dp", "expert"), None, None),
            P(),
            P("expert", None, "dp"),
            P("expert", "dp", None),
        ),
        check_vma=False,
    )
```

```python
import functools
import math

import jax
import jax.numpy as jnp
from jax import lax
from jax.experimental import pallas as pl
from jax.experimental.pallas import tpu as pltpu
from jax.sharding import PartitionSpec as P

F32 = jnp.float32
BF16 = jnp.bfloat16
MIB = 1024 * 1024


def dot(left, right, left_dim=1, right_dim=0):
    return lax.dot_general(
        left, right, (((left_dim,), (right_dim,)), ((), ())), preferred_element_type=F32
    )


def iota(shape, dim):
    return lax.broadcasted_iota(jnp.int32, shape, dim)


def in_hbm(value):
    return pltpu.with_memory_space_constraint(value, pltpu.HBM)


def call(kernel, name, out_shape, limit, flops, moved, **more):
    return pl.pallas_call(
        kernel,
        out_shape=out_shape,
        compiler_params=pltpu.CompilerParams(vmem_limit_bytes=limit * MIB),
        cost_estimate=pl.CostEstimate(flops=flops, bytes_accessed=moved, transcendentals=0),
        name=name,
        **more,
    )


def picked_expert(per, rows):
    return (rows // (2 * per)) * per + rows % per


def spread(per, experts):
    shape = (2 * experts, experts)
    return (picked_expert(per, iota(shape, 0)) == iota(shape, 1)).astype(BF16)


def pick_first(per, experts):
    shape = (2 * experts, experts)
    row = iota(shape, 0)
    return ((picked_expert(per, row) == iota(shape, 1)) & (row % (2 * per) < per)).astype(BF16)


def first_half(per, shape):
    return iota(shape, 1) % (2 * per) < per


def front_kernel(
    per, tokens_hbm, router_hbm, cotangent_hbm, rows, disp, comb, tokens, cotangent, router_t, sems
):
    copies = [
        pltpu.make_async_copy(source, target, sems.at[index])
        for index, (source, target) in enumerate(
            ((router_hbm, router_t), (tokens_hbm, tokens), (cotangent_hbm, cotangent))
        )
    ]
    for copy in copies:
        copy.start()
    matrix = spread(per, router_t.shape[0])
    copies[0].wait()
    paired_router = dot(matrix, router_t[...]).astype(BF16)
    copies[1].wait()
    logits = dot(tokens[...], paired_router, 1, 1)
    first = first_half(per, logits.shape)
    down = jnp.exp(logits - jnp.max(logits, axis=0, keepdims=True))
    disp_prob = down / jnp.sum(down, axis=0, keepdims=True)
    across = jnp.exp(logits - jnp.max(logits, axis=1, keepdims=True))
    comb_prob = across / jnp.sum(jnp.where(first, across, 0.0), axis=1, keepdims=True)
    disp[...] = disp_prob
    comb[...] = comb_prob
    disp_cols = jnp.where(first, disp_prob, 0.0).astype(BF16)
    comb_cols = jnp.where(first, 0.0, comb_prob).astype(BF16)
    copies[2].wait()
    rows[...] = (
        dot(disp_cols, tokens[...], 0, 0) + dot(comb_cols, cotangent[...], 0, 0)
    ).astype(BF16)


def front(per, tokens, router_t, cotangent):
    seq, width = tokens.shape
    experts = router_t.shape[0]
    return call(
        functools.partial(front_kernel, per),
        "front",
        (
            pltpu.VMEM((2 * experts, width), BF16),
            pltpu.VMEM((seq, 2 * experts), F32),
            pltpu.VMEM((seq, 2 * experts), F32),
            pltpu.VMEM(tokens.shape, BF16),
            pltpu.VMEM(cotangent.shape, BF16),
        ),
        8,
        12 * seq * width * experts,
        6 * seq * width,
        in_specs=[pl.BlockSpec(memory_space=pltpu.HBM)] * 3,
        scratch_shapes=[pltpu.VMEM(router_t.shape, BF16), pltpu.SemaphoreType.DMA((3,))],
    )(in_hbm(tokens), in_hbm(router_t), in_hbm(cotangent))


def fetch_kernel(first_hbm, second_hbm, after, first, second, done, sems):
    done[...] = jnp.zeros(done.shape, F32)
    copies = [
        pltpu.make_async_copy(source.at[k], target.at[k], sems.at[index, k])
        for k in range(first.shape[0])
        for index, (source, target) in enumerate(((first_hbm, first), (second_hbm, second)))
    ]
    for copy in copies:
        copy.start()
    for copy in copies:
        copy.wait()


def fetch(w_first, w_second, after):
    return call(
        fetch_kernel,
        "fetch_weights",
        (
            pltpu.VMEM(w_first.shape, BF16),
            pltpu.VMEM(w_second.shape, BF16),
            pltpu.VMEM((8, 128), F32),
        ),
        2,
        0,
        4 * w_first.size,
        in_specs=[pl.BlockSpec(memory_space=pltpu.HBM)] * 2 + [pl.BlockSpec(memory_space=pl.ANY)],
        scratch_shapes=[pltpu.SemaphoreType.DMA((2, w_first.shape[0]))],
    )(in_hbm(w_first), in_hbm(w_second), after)


def shifted(value, axis, by):
    size = lax.axis_size(axis)
    return lax.ppermute(value, axis, [(i, (i + by) % size) for i in range(size)])


def exchange(blocks, axis, sign):
    return [blocks[0]] + [shifted(block, axis, sign * k) for k, block in enumerate(blocks) if k]


def sort_matrix(images, wide, transposed):
    shape = (images * wide, images * wide)
    to, start = (iota(shape, 1), iota(shape, 0)) if transposed else (iota(shape, 0), iota(shape, 1))
    return ((to % images) * wide + to // images == start).astype(BF16)


def sort_kernel(images, rows, after, out):
    matrix = sort_matrix(images, rows.shape[0] // images, False)
    out[...] = dot(matrix, rows[...]).astype(BF16)


def sort_rows(images, rows, after):
    total, width = rows.shape
    return call(
        functools.partial(sort_kernel, images),
        "sort_rows",
        pltpu.VMEM(rows.shape, BF16),
        4,
        2 * total * total * width,
        4 * total * width,
        in_specs=[pl.BlockSpec(memory_space=pltpu.VMEM), pl.BlockSpec(memory_space=pl.ANY)],
    )(rows, after)


def add_kernel(images, *refs):
    *pieces, out = refs
    total = sum(piece[...].astype(F32) for piece in pieces).astype(BF16)
    if images:
        total = dot(sort_matrix(images, total.shape[0] // images, True), total).astype(BF16)
    out[...] = total


def add(pieces, name, images=0):
    size = pieces[0].size
    return call(
        functools.partial(add_kernel, images),
        name,
        pltpu.VMEM(pieces[0].shape, BF16),
        4,
        len(pieces) * size,
        4 * size,
    )(*pieces)


def experts_kernel(per, groups, *refs):
    rows, (w_first, w_second), refs = refs[:groups], refs[groups : groups + 2], refs[groups + 2 :]
    back_rows, (slots_out, grads_out, hidden_out, pre_out) = refs[:groups], refs[groups:]
    size = rows[0].shape[0] // (2 * per)
    span = lambda j: slice(j * size, (j + 1) * size)
    for k in range(per):
        slots = jnp.concatenate([part[span(k), :] for part in rows])
        grads = jnp.concatenate([part[span(per + k), :] for part in rows])
        slots_out[k] = slots
        grads_out[k] = grads
        pre_act = dot(slots, w_first[k])
        phi = 0.5 * (1.0 + lax.erf(pre_act * math.sqrt(0.5)))
        density = jnp.exp(pre_act * pre_act * -0.5) * (1.0 / math.sqrt(2.0 * math.pi))
        hidden = (pre_act * phi).astype(BF16)
        hidden_out[k] = hidden
        out = dot(hidden, w_second[k]).astype(BF16)
        grad_hidden = dot(grads, w_second[k], 1, 1)
        grad_pre = ((phi + pre_act * density) * grad_hidden).astype(BF16)
        pre_out[k] = grad_pre
        grad_slot = dot(grad_pre, w_first[k], 1, 1).astype(BF16)
        for part, target in enumerate(back_rows):
            target[span(k), :] = out[span(part), :]
            target[span(per + k), :] = grad_slot[span(part), :]


def run_experts(rows, w_first, w_second):
    per, width, units = w_first.shape
    groups = len(rows)
    total = rows[0].shape[0]
    images = groups * total // (2 * per)
    results = call(
        functools.partial(experts_kernel, per, groups),
        "experts",
        [pltpu.VMEM((total, width), BF16)] * groups
        + [pltpu.VMEM((per, images, width), BF16)] * 2
        + [pltpu.VMEM((per, images, units), BF16)] * 2,
        16,
        8 * per * images * width * units,
        4 * per * width * units,
    )(*rows, w_first, w_second)
    return results[:groups], results[groups:]


def outer_kernel(left, right, after, out):
    out[0] = dot(left[0], right[0], 0, 0).astype(BF16)


def outer(left, right, after, name):
    per, images, height = left.shape
    units = right.shape[2]
    per_expert = lambda a, b: pl.BlockSpec((1, a, b), lambda k: (k, 0, 0))
    return call(
        outer_kernel,
        name,
        jax.ShapeDtypeStruct((per, height, units), BF16),
        16,
        2 * per * images * height * units,
        2 * per * height * units,
        grid=(per,),
        in_specs=[
            per_expert(images, height),
            per_expert(images, units),
            pl.BlockSpec(memory_space=pl.ANY),
        ],
        out_specs=per_expert(height, units),
    )(left, right, after)


def logits_kernel(per, groups, tokens, cotangent, disp, comb, outs, after, *refs):
    *parts, grad_logits, terms = refs
    rows = outs[...]
    disp_prob = disp[...]
    comb_prob = comb[...]
    first = first_half(per, disp_prob.shape)
    grad_comb = dot(cotangent[...], rows, 1, 1)
    grad_disp = dot(tokens[...], rows, 1, 1)
    part_disp = disp_prob * (
        grad_disp - jnp.sum(disp_prob * grad_disp, axis=0, keepdims=True)
    )
    comb_sum = jnp.sum(jnp.where(first, comb_prob * grad_comb, 0.0), axis=1, keepdims=True)
    part_comb = comb_prob * (grad_comb - comb_sum)
    both = jnp.where(first, part_comb, part_disp)
    cols = both.shape[1]
    other = jnp.where(first, pltpu.roll(both, cols - per, 1), pltpu.roll(both, per, 1))
    paired = (both + other).astype(BF16)
    grad_logits[...] = jnp.where(first, paired.astype(F32), 0.0).astype(BF16)
    one_each = dot(paired, pick_first(per, cols // 2)).astype(BF16)
    term = dot(one_each, tokens[...], 0, 0)
    height = terms.shape[1]
    for part in range(groups):
        terms[part] = term[part * height : (part + 1) * height, :].astype(BF16)
    me = lax.axis_index("dp")
    for part, out in enumerate(parts):
        out[...] = terms[lax.rem(me + part, groups)]


def finish_logits(per, groups, tokens, cotangent, disp, comb, outs, after):
    seq, width = tokens.shape
    cols = disp.shape[1]
    height = cols // 2 // groups
    results = call(
        functools.partial(logits_kernel, per, groups),
        "grad_logits",
        [pltpu.VMEM((height, width), BF16)] * groups + [pltpu.VMEM((seq, cols), BF16)],
        8,
        6 * seq * width * cols,
        6 * seq * width,
        in_specs=[pl.BlockSpec(memory_space=pltpu.VMEM)] * 5
        + [pl.BlockSpec(memory_space=pltpu.HBM)],
        scratch_shapes=[pltpu.VMEM((groups, height, width), BF16)],
    )(tokens, cotangent, disp, comb, outs, in_hbm(after))
    return results[:groups], results[groups]


def images_kernel(per, outs, disp, comb, grad_logits, router_t, mixed, grad_tokens):
    rows = outs[...]
    first = first_half(per, disp.shape)
    comb_cols = jnp.where(first, comb[...], 0.0).astype(BF16)
    mixed[...] = dot(comb_cols, rows).astype(BF16)
    disp_cols = jnp.where(first, 0.0, disp[...]).astype(BF16)
    paired_router = dot(spread(per, router_t.shape[0]), router_t[...]).astype(BF16)
    grad_tokens[...] = (dot(disp_cols, rows) + dot(grad_logits[...], paired_router)).astype(BF16)


def finish_images(per, outs, disp, comb, grad_logits, router_t):
    seq, cols = disp.shape
    width = outs.shape[1]
    return call(
        functools.partial(images_kernel, per),
        "mixed_and_grad_tokens",
        (jax.ShapeDtypeStruct((seq, width), BF16), jax.ShapeDtypeStruct((seq, width), BF16)),
        8,
        6 * seq * width * cols,
        6 * seq * width,
    )(outs, disp, comb, grad_logits, router_t)


def join_kernel(*refs):
    *parts, out = refs
    groups = len(parts)
    me = lax.axis_index("dp")
    for part, ref in enumerate(parts):
        out[lax.rem(me - part + groups, groups)] = ref[...].astype(F32)


def join(parts):
    height, width = parts[0].shape
    return call(
        join_kernel,
        "join",
        jax.ShapeDtypeStruct((len(parts), height, width), F32),
        4,
        0,
        6 * height * width,
    )(*parts).reshape(-1, width)


def sum_kernel(parts, out):
    out[...] = jnp.sum(parts[...].astype(F32), axis=0).astype(BF16)


def sum_chunks(parts):
    return call(
        sum_kernel, "sum_chunks", pltpu.VMEM(parts.shape[1:], BF16), 4, parts.size, 2 * parts.size
    )(parts)


def total_over_devices(parts):
    value = add(exchange(parts, "dp", 1), "add_cores")
    height, width = value.shape
    chips = lax.axis_size("expert")
    value = value.reshape(chips, height * width // (chips * 128), 128)
    value = lax.all_to_all(value, "expert", split_axis=0, concat_axis=0, tiled=True)
    value = lax.all_gather(sum_chunks(value), "expert", axis=0)
    value = value.reshape(height, width)
    return join(exchange([value] * len(parts), "dp", 1))


def local(tokens, router, weight_in, weight_out, cotangent):
    per = weight_in.shape[0]
    experts = router.shape[1]
    chips = experts // per
    groups = lax.axis_size("dp")
    tokens, cotangent = tokens[0], cotangent[0]
    width = tokens.shape[1]
    router_t = router.T

    def to_chips(rows):
        blocks = rows.reshape(chips, 2 * per, width)
        blocks = lax.all_to_all(blocks, "expert", split_axis=0, concat_axis=0, tiled=True)
        return blocks.reshape(rows.shape)

    rows, disp, comb, tokens, cotangent = front(per, tokens, router_t, cotangent)
    w_first, w_second, fetched = fetch(weight_in, weight_out, comb)
    rows = sort_rows(chips, to_chips(rows), fetched)
    rows = exchange([rows] * groups, "dp", 1)
    back_rows, (slots, grads, hidden, grad_pre) = run_experts(rows, w_first, w_second)
    back_rows = add(exchange(back_rows, "dp", -1), "add_groups", chips)
    outs = to_chips(back_rows)
    grad_second = outer(hidden, grads, back_rows, "grad_weight_out")
    grad_first = outer(slots, grad_pre, back_rows, "grad_weight_in")
    parts, grad_logits = finish_logits(
        per, groups, tokens, cotangent, disp, comb, outs, grad_second
    )
    mixed, grad_tokens = finish_images(per, outs, disp, comb, grad_logits, router_t)
    grad_router = total_over_devices(parts).T
    return (mixed[None], grad_tokens[None], grad_router, grad_first, grad_second)


def solution(mesh):
    return jax.shard_map(
        local,
        mesh=mesh,
        in_specs=(
            P(("dp", "expert"), None, None),
            P(),
            P("expert", None, "dp"),
            P("expert", "dp", None),
            P(("dp", "expert"), None, None),
        ),
        out_specs=(
            P(("dp", "expert"), None, None),
            P(("dp", "expert"), None, None),
            P(),
            P("expert", None, "dp"),
            P("expert", "dp", None),
        ),
        check_vma=False,
    )
```

```python
import functools
import math

import jax
import jax.numpy as jnp
from jax import lax
from jax.experimental import pallas as pl
from jax.experimental.pallas import tpu as pltpu
from jax.sharding import PartitionSpec as P

F32 = jnp.float32
BF16 = jnp.bfloat16
MIB = 1024 * 1024


def dot(left, right, left_dim=1, right_dim=0):
    return lax.dot_general(
        left, right, (((left_dim,), (right_dim,)), ((), ())), preferred_element_type=F32
    )


def iota(shape, dim):
    return lax.broadcasted_iota(jnp.int32, shape, dim)


def in_hbm(value):
    return pltpu.with_memory_space_constraint(value, pltpu.HBM)


def call(kernel, name, out_shape, limit, flops, moved, **more):
    return pl.pallas_call(
        kernel,
        out_shape=out_shape,
        compiler_params=pltpu.CompilerParams(vmem_limit_bytes=limit * MIB),
        cost_estimate=pl.CostEstimate(flops=flops, bytes_accessed=moved, transcendentals=0),
        name=name,
        **more,
    )


def picked_expert(per, rows):
    return (rows // (2 * per)) * per + rows % per


def spread(per, experts):
    shape = (2 * experts, experts)
    return (picked_expert(per, iota(shape, 0)) == iota(shape, 1)).astype(BF16)


def pick_first(per, experts):
    shape = (2 * experts, experts)
    row = iota(shape, 0)
    return ((picked_expert(per, row) == iota(shape, 1)) & (row % (2 * per) < per)).astype(BF16)


def first_half(per, shape):
    return iota(shape, 1) % (2 * per) < per


def front_kernel(
    per, tokens_hbm, router_hbm, cotangent_hbm, rows, disp, comb, tokens, cotangent, router_t, sems
):
    copies = [
        pltpu.make_async_copy(source, target, sems.at[index])
        for index, (source, target) in enumerate(
            ((router_hbm, router_t), (tokens_hbm, tokens), (cotangent_hbm, cotangent))
        )
    ]
    for copy in copies:
        copy.start()
    matrix = spread(per, router_t.shape[0])
    copies[0].wait()
    paired_router = dot(matrix, router_t[...]).astype(BF16)
    copies[1].wait()
    logits = dot(tokens[...], paired_router, 1, 1)
    first = first_half(per, logits.shape)
    down = jnp.exp(logits - jnp.max(logits, axis=0, keepdims=True))
    disp_prob = down / jnp.sum(down, axis=0, keepdims=True)
    across = jnp.exp(logits - jnp.max(logits, axis=1, keepdims=True))
    comb_prob = across / jnp.sum(jnp.where(first, across, 0.0), axis=1, keepdims=True)
    disp[...] = disp_prob
    comb[...] = comb_prob
    disp_cols = jnp.where(first, disp_prob, 0.0).astype(BF16)
    comb_cols = jnp.where(first, 0.0, comb_prob).astype(BF16)
    copies[2].wait()
    rows[...] = (
        dot(disp_cols, tokens[...], 0, 0) + dot(comb_cols, cotangent[...], 0, 0)
    ).astype(BF16)


def front(per, tokens, router_t, cotangent):
    seq, width = tokens.shape
    experts = router_t.shape[0]
    return call(
        functools.partial(front_kernel, per),
        "front",
        (
            pltpu.VMEM((2 * experts, width), BF16),
            pltpu.VMEM((seq, 2 * experts), F32),
            pltpu.VMEM((seq, 2 * experts), F32),
            pltpu.VMEM(tokens.shape, BF16),
            pltpu.VMEM(cotangent.shape, BF16),
        ),
        8,
        12 * seq * width * experts,
        6 * seq * width,
        in_specs=[pl.BlockSpec(memory_space=pltpu.HBM)] * 3,
        scratch_shapes=[pltpu.VMEM(router_t.shape, BF16), pltpu.SemaphoreType.DMA((3,))],
    )(in_hbm(tokens), in_hbm(router_t), in_hbm(cotangent))


def shifted(value, axis, by):
    size = lax.axis_size(axis)
    return lax.ppermute(value, axis, [(i, (i + by) % size) for i in range(size)])


def exchange(blocks, axis, sign):
    return [blocks[0]] + [shifted(block, axis, sign * k) for k, block in enumerate(blocks) if k]


def sort_matrix(images, wide, transposed):
    shape = (images * wide, images * wide)
    to, start = (iota(shape, 1), iota(shape, 0)) if transposed else (iota(shape, 0), iota(shape, 1))
    return ((to % images) * wide + to // images == start).astype(BF16)


def add_kernel(images, count, *refs):
    pieces, out = refs[:count], refs[-1]
    total = sum(piece[...].astype(F32) for piece in pieces).astype(BF16)
    if images:
        total = dot(sort_matrix(images, total.shape[0] // images, True), total).astype(BF16)
    out[...] = total


def add(pieces, name, images=0, after=()):
    size = pieces[0].size
    return call(
        functools.partial(add_kernel, images, len(pieces)),
        name,
        pltpu.VMEM(pieces[0].shape, BF16),
        4,
        len(pieces) * size,
        4 * size,
        in_specs=[pl.BlockSpec(memory_space=pltpu.VMEM)] * len(pieces)
        + [pl.BlockSpec(memory_space=pltpu.HBM)] * len(after),
    )(*pieces, *map(in_hbm, after))


def experts_kernel(per, groups, *refs):
    rows, weights_hbm, refs = refs[:groups], refs[groups : groups + 2], refs[groups + 2 :]
    back_rows, refs = refs[:groups], refs[groups:]
    slots_out, grads_out, hidden_out, pre_out, w_first, w_second, sems = refs
    wide = 2 * per
    size = rows[0].shape[0] // wide
    span = lambda j: slice(j * size, (j + 1) * size)
    copies = [
        [
            pltpu.make_async_copy(source.at[k], target.at[k], sems.at[index, k])
            for index, (source, target) in enumerate(zip(weights_hbm, (w_first, w_second)))
        ]
        for k in range(per)
    ]
    for copy in copies[0]:
        copy.start()
    matrix = sort_matrix(size, wide, False)
    for part in range(groups):
        moved = dot(matrix, rows[part][...]).astype(BF16)
        for k in range(per):
            slots_out[k, span(part), :] = moved[span(k), :]
            grads_out[k, span(part), :] = moved[span(per + k), :]
    for k in range(per):
        copies[k][0].wait()
        for copy in copies[k + 1] if k + 1 < per else ():
            copy.start()
        pre_act = dot(slots_out[k], w_first[k])
        phi = 0.5 * (1.0 + lax.erf(pre_act * math.sqrt(0.5)))
        density = jnp.exp(pre_act * pre_act * -0.5) * (1.0 / math.sqrt(2.0 * math.pi))
        hidden = (pre_act * phi).astype(BF16)
        hidden_out[k] = hidden
        copies[k][1].wait()
        grad_hidden = dot(grads_out[k], w_second[k], 1, 1)
        out = dot(hidden, w_second[k]).astype(BF16)
        grad_pre = ((phi + pre_act * density) * grad_hidden).astype(BF16)
        pre_out[k] = grad_pre
        grad_slot = dot(grad_pre, w_first[k], 1, 1).astype(BF16)
        for part, target in enumerate(back_rows):
            target[span(k), :] = out[span(part), :]
            target[span(per + k), :] = grad_slot[span(part), :]


def run_experts(rows, w_first, w_second):
    per, width, units = w_first.shape
    groups = len(rows)
    total = rows[0].shape[0]
    images = groups * total // (2 * per)
    results = call(
        functools.partial(experts_kernel, per, groups),
        "experts",
        [pltpu.VMEM((total, width), BF16)] * groups
        + [pltpu.VMEM((per, images, width), BF16)] * 2
        + [pltpu.VMEM((per, images, units), BF16)] * 2,
        32,
        8 * per * images * width * units,
        4 * per * width * units,
        in_specs=[pl.BlockSpec(memory_space=pltpu.VMEM)] * groups
        + [pl.BlockSpec(memory_space=pltpu.HBM)] * 2,
        scratch_shapes=[
            pltpu.VMEM(w_first.shape, BF16),
            pltpu.VMEM(w_second.shape, BF16),
            pltpu.SemaphoreType.DMA((2, per)),
        ],
    )(*rows, in_hbm(w_first), in_hbm(w_second))
    return results[:groups], results[groups:]


def outer_kernel(left, right, *refs):
    refs[-1][0] = dot(left[0], right[0], 0, 0).astype(BF16)


def outer(left, right, after, name, only=None, into=None):
    per, images, height = left.shape
    units = right.shape[2]
    at = (lambda k: (k, 0, 0)) if only is None else (lambda k: (only, 0, 0))
    steps = per if only is None else 1
    per_expert = lambda a, b: pl.BlockSpec((1, a, b), at)
    more = () if into is None else (in_hbm(into),)
    return call(
        outer_kernel,
        name,
        jax.ShapeDtypeStruct((per, height, units), BF16),
        16,
        2 * steps * images * height * units,
        2 * steps * height * units,
        grid=(steps,),
        in_specs=[
            per_expert(images, height),
            per_expert(images, units),
            pl.BlockSpec(memory_space=pl.ANY),
        ]
        + [pl.BlockSpec(memory_space=pltpu.HBM)] * len(more),
        out_specs=per_expert(height, units),
        input_output_aliases={3: 0} if more else {},
    )(left, right, after, *more)


def logits_kernel(per, groups, tokens, cotangent, disp, comb, outs, after, *refs):
    *parts, grad_logits, terms = refs
    rows = outs[...]
    disp_prob = disp[...]
    comb_prob = comb[...]
    first = first_half(per, disp_prob.shape)
    grad_comb = dot(cotangent[...], rows, 1, 1)
    grad_disp = dot(tokens[...], rows, 1, 1)
    part_disp = disp_prob * (
        grad_disp - jnp.sum(disp_prob * grad_disp, axis=0, keepdims=True)
    )
    comb_sum = jnp.sum(jnp.where(first, comb_prob * grad_comb, 0.0), axis=1, keepdims=True)
    part_comb = comb_prob * (grad_comb - comb_sum)
    both = jnp.where(first, part_comb, part_disp)
    cols = both.shape[1]
    other = jnp.where(first, pltpu.roll(both, cols - per, 1), pltpu.roll(both, per, 1))
    paired = (both + other).astype(BF16)
    grad_logits[...] = jnp.where(first, paired.astype(F32), 0.0).astype(BF16)
    one_each = dot(paired, pick_first(per, cols // 2)).astype(BF16)
    term = dot(one_each, tokens[...], 0, 0)
    height = terms.shape[1]
    for part in range(groups):
        terms[part] = term[part * height : (part + 1) * height, :].astype(BF16)
    me = lax.axis_index("dp")
    for part, out in enumerate(parts):
        out[...] = terms[lax.rem(me + part, groups)]


def finish_logits(per, groups, tokens, cotangent, disp, comb, outs, after):
    seq, width = tokens.shape
    cols = disp.shape[1]
    height = cols // 2 // groups
    results = call(
        functools.partial(logits_kernel, per, groups),
        "grad_logits",
        [pltpu.VMEM((height, width), BF16)] * groups + [pltpu.VMEM((seq, cols), BF16)],
        8,
        6 * seq * width * cols,
        6 * seq * width,
        in_specs=[pl.BlockSpec(memory_space=pltpu.VMEM)] * 5
        + [pl.BlockSpec(memory_space=pltpu.HBM)],
        scratch_shapes=[pltpu.VMEM((groups, height, width), BF16)],
    )(tokens, cotangent, disp, comb, outs, in_hbm(after))
    return results[:groups], results[groups]


def mixed_kernel(per, outs, comb, mixed):
    first = first_half(per, comb.shape)
    mixed[...] = dot(jnp.where(first, comb[...], 0.0).astype(BF16), outs[...]).astype(BF16)


def finish_mixed(per, outs, comb):
    seq, cols = comb.shape
    width = outs.shape[1]
    return call(
        functools.partial(mixed_kernel, per),
        "mixed",
        jax.ShapeDtypeStruct((seq, width), BF16),
        8,
        2 * seq * width * cols,
        2 * seq * width,
    )(outs, comb)


def tokens_kernel(per, outs, disp, grad_logits, router_t, after, grad_tokens):
    first = first_half(per, disp.shape)
    disp_cols = jnp.where(first, 0.0, disp[...]).astype(BF16)
    paired_router = dot(spread(per, router_t.shape[0]), router_t[...]).astype(BF16)
    grad_tokens[...] = (
        dot(disp_cols, outs[...]) + dot(grad_logits[...], paired_router)
    ).astype(BF16)


def finish_tokens(per, outs, disp, grad_logits, router_t, after):
    seq, cols = disp.shape
    width = outs.shape[1]
    return call(
        functools.partial(tokens_kernel, per),
        "grad_tokens",
        jax.ShapeDtypeStruct((seq, width), BF16),
        8,
        4 * seq * width * cols,
        2 * seq * width,
        in_specs=[pl.BlockSpec(memory_space=pltpu.VMEM)] * 4 + [pl.BlockSpec(memory_space=pl.ANY)],
    )(outs, disp, grad_logits, router_t, after)


def join_kernel(*refs):
    *parts, out = refs
    groups = len(parts)
    me = lax.axis_index("dp")
    for part, ref in enumerate(parts):
        out[lax.rem(me - part + groups, groups)] = ref[...].astype(F32)


def join(parts):
    height, width = parts[0].shape
    return call(
        join_kernel,
        "join",
        jax.ShapeDtypeStruct((len(parts), height, width), F32),
        4,
        0,
        6 * height * width,
    )(*parts).reshape(-1, width)


def across_chips(value, step):
    groups, chips = lax.axis_size("dp"), lax.axis_size("expert")
    bits = chips.bit_length() - 1
    pairs = []
    for core in range(groups):
        bit = 1 << (step + core * (bits // 2)) % bits
        pairs += [(core * chips + i, core * chips + (i ^ bit)) for i in range(chips)]
    return lax.ppermute(value, ("dp", "expert"), pairs)


def total_over_devices(parts, first_beside, beside):
    value = add(exchange(parts, "dp", 1), "add_cores", after=[first_beside])
    chips = lax.axis_size("expert")
    steps = chips.bit_length() - 1
    for step in range(steps):
        count = -(-len(beside) // (steps - step))
        results = [beside.pop(0)(value) for _ in range(count)][-1:]
        value = add([value, across_chips(value, step)], "add_chips", after=results)
    return value, join(exchange([value] * len(parts), "dp", 1))


def local(tokens, router, weight_in, weight_out, cotangent):
    per = weight_in.shape[0]
    experts = router.shape[1]
    chips = experts // per
    groups = lax.axis_size("dp")
    tokens, cotangent = tokens[0], cotangent[0]
    width = tokens.shape[1]
    router_t = router.T

    def to_chips(rows):
        blocks = rows.reshape(chips, 2 * per, width)
        blocks = lax.all_to_all(blocks, "expert", split_axis=0, concat_axis=0, tiled=True)
        return blocks.reshape(rows.shape)

    rows, disp, comb, tokens, cotangent = front(per, tokens, router_t, cotangent)
    rows = exchange([to_chips(rows)] * groups, "dp", 1)
    back_rows, (slots, grads, hidden, grad_pre) = run_experts(rows, weight_in, weight_out)
    back_rows = add(exchange(back_rows, "dp", -1), "add_groups", chips)
    outs = to_chips(back_rows)
    grad_second = outer(hidden, grads, back_rows, "grad_weight_out")
    parts, grad_logits = finish_logits(
        per, groups, tokens, cotangent, disp, comb, outs, grad_second
    )
    mixed = finish_mixed(per, outs, comb)
    grad_first = None

    def piece(k, value):
        nonlocal grad_first
        grad_first = outer(slots, grad_pre, value, "grad_weight_in", k, grad_first)
        return grad_first

    value, total = total_over_devices(
        parts, mixed, [functools.partial(piece, k) for k in range(per)]
    )
    grad_tokens = finish_tokens(per, outs, disp, grad_logits, router_t, value)
    grad_router = total.T
    return (mixed[None], grad_tokens[None], grad_router, grad_first, grad_second)


def solution(mesh):
    return jax.shard_map(
        local,
        mesh=mesh,
        in_specs=(
            P(("dp", "expert"), None, None),
            P(),
            P("expert", None, "dp"),
            P("expert", "dp", None),
            P(("dp", "expert"), None, None),
        ),
        out_specs=(
            P(("dp", "expert"), None, None),
            P(("dp", "expert"), None, None),
            P(),
            P("expert", None, "dp"),
            P("expert", "dp", None),
        ),
        check_vma=False,
    )
```

```python
import functools
import math

import jax
import jax.numpy as jnp
from jax import lax
from jax.experimental import pallas as pl
from jax.experimental.pallas import tpu as pltpu
from jax.sharding import PartitionSpec as P

F32 = jnp.float32
BF16 = jnp.bfloat16
MIB = 1024 * 1024


def dot(left, right, left_dim=1, right_dim=0):
    return lax.dot_general(
        left, right, (((left_dim,), (right_dim,)), ((), ())), preferred_element_type=F32
    )


def iota(shape, dim):
    return lax.broadcasted_iota(jnp.int32, shape, dim)


def in_hbm(value):
    return pltpu.with_memory_space_constraint(value, pltpu.HBM)


def call(kernel, name, out_shape, limit, flops, moved, **more):
    return pl.pallas_call(
        kernel,
        out_shape=out_shape,
        compiler_params=pltpu.CompilerParams(vmem_limit_bytes=limit * MIB),
        cost_estimate=pl.CostEstimate(flops=flops, bytes_accessed=moved, transcendentals=0),
        name=name,
        **more,
    )


def picked_expert(per, rows):
    return (rows // (2 * per)) * per + rows % per


def spread(per, experts):
    shape = (2 * experts, experts)
    return (picked_expert(per, iota(shape, 0)) == iota(shape, 1)).astype(BF16)


def pick_first(per, experts):
    shape = (2 * experts, experts)
    row = iota(shape, 0)
    return ((picked_expert(per, row) == iota(shape, 1)) & (row % (2 * per) < per)).astype(BF16)


def first_half(per, shape):
    return iota(shape, 1) % (2 * per) < per


def front_kernel(
    per, tokens_hbm, router_hbm, cotangent_hbm, rows, disp, comb, tokens, cotangent, router_t, sems
):
    copies = [
        pltpu.make_async_copy(source, target, sems.at[index])
        for index, (source, target) in enumerate(
            ((router_hbm, router_t), (tokens_hbm, tokens), (cotangent_hbm, cotangent))
        )
    ]
    for copy in copies:
        copy.start()
    matrix = spread(per, router_t.shape[0])
    copies[0].wait()
    paired_router = dot(matrix, router_t[...]).astype(BF16)
    copies[1].wait()
    logits = dot(tokens[...], paired_router, 1, 1)
    first = first_half(per, logits.shape)
    down = jnp.exp(logits - jnp.max(logits, axis=0, keepdims=True))
    disp_prob = down / jnp.sum(down, axis=0, keepdims=True)
    across = jnp.exp(logits - jnp.max(logits, axis=1, keepdims=True))
    comb_prob = across / jnp.sum(jnp.where(first, across, 0.0), axis=1, keepdims=True)
    disp[...] = disp_prob
    comb[...] = comb_prob
    disp_cols = jnp.where(first, disp_prob, 0.0).astype(BF16)
    comb_cols = jnp.where(first, 0.0, comb_prob).astype(BF16)
    copies[2].wait()
    rows[...] = (
        dot(disp_cols, tokens[...], 0, 0) + dot(comb_cols, cotangent[...], 0, 0)
    ).astype(BF16)


def front(per, tokens, router_t, cotangent):
    seq, width = tokens.shape
    experts = router_t.shape[0]
    return call(
        functools.partial(front_kernel, per),
        "front",
        (
            pltpu.VMEM((2 * experts, width), BF16),
            pltpu.VMEM((seq, 2 * experts), F32),
            pltpu.VMEM((seq, 2 * experts), F32),
            pltpu.VMEM(tokens.shape, BF16),
            pltpu.VMEM(cotangent.shape, BF16),
        ),
        8,
        12 * seq * width * experts,
        6 * seq * width,
        in_specs=[pl.BlockSpec(memory_space=pltpu.HBM)] * 3,
        scratch_shapes=[pltpu.VMEM(router_t.shape, BF16), pltpu.SemaphoreType.DMA((3,))],
    )(in_hbm(tokens), in_hbm(router_t), in_hbm(cotangent))


def shifted(value, axis, by):
    size = lax.axis_size(axis)
    return lax.ppermute(value, axis, [(i, (i + by) % size) for i in range(size)])


def exchange(blocks, axis, sign):
    return [blocks[0]] + [shifted(block, axis, sign * k) for k, block in enumerate(blocks) if k]


def sort_matrix(images, wide, transposed):
    shape = (images * wide, images * wide)
    to, start = (iota(shape, 1), iota(shape, 0)) if transposed else (iota(shape, 0), iota(shape, 1))
    return ((to % images) * wide + to // images == start).astype(BF16)


def add_kernel(images, count, *refs):
    pieces, out = refs[:count], refs[-1]
    total = [piece[...].astype(F32) for piece in pieces]
    while len(total) > 1:
        total = [sum(total[index : index + 2]) for index in range(0, len(total), 2)]
    total = total[0].astype(BF16)
    if images:
        total = dot(sort_matrix(images, total.shape[0] // images, True), total).astype(BF16)
    out[...] = total


def add(pieces, name, images=0, after=()):
    size = pieces[0].size
    return call(
        functools.partial(add_kernel, images, len(pieces)),
        name,
        pltpu.VMEM(pieces[0].shape, BF16),
        4,
        len(pieces) * size,
        4 * size,
        in_specs=[pl.BlockSpec(memory_space=pltpu.VMEM)] * len(pieces)
        + [pl.BlockSpec(memory_space=pltpu.HBM)] * len(after),
    )(*pieces, *map(in_hbm, after))


def fetch_kernel(rows, source, target, sems):
    height = target.shape[0] // sems.shape[0]
    copies = [
        pltpu.make_async_copy(
            source.at[0, pl.ds(part * height, height)],
            target.at[pl.ds(part * height, height)],
            sems.at[part],
        )
        for part in range(sems.shape[0])
    ]
    for copy in copies:
        copy.start()
    for copy in copies:
        copy.wait()


def fetch(after, weight):
    return call(
        fetch_kernel,
        "fetch_first",
        pltpu.VMEM(weight.shape[1:], BF16),
        2,
        0,
        4 * weight[0].size,
        in_specs=[pl.BlockSpec(memory_space=pl.ANY), pl.BlockSpec(memory_space=pltpu.HBM)],
        scratch_shapes=[pltpu.SemaphoreType.DMA((2,))],
    )(after, in_hbm(weight))


def experts_kernel(per, groups, *refs):
    rows, refs = refs[:groups], refs[groups:]
    first_weight, *weights_hbm = refs[:3]
    refs = refs[3:]
    back_rows, refs = refs[:groups], refs[groups:]
    slots_out, grads_out, hidden_out, pre_out, w_first, w_second, sems = refs
    wide = 2 * per
    size = rows[0].shape[0] // wide
    span = lambda j: slice(j * size, (j + 1) * size)
    def copy(k, index):
        target = (w_first, w_second)[index]
        return pltpu.make_async_copy(weights_hbm[index].at[k], target.at[k], sems.at[index, k])

    copy_first = [None] + [copy(k, 0) for k in range(1, per)]
    copy_second = [copy(k, 1) for k in range(per)]
    copy_second[0].start()
    matrix = sort_matrix(size, wide, False)
    for part in range(groups):
        moved = dot(matrix, rows[part][...]).astype(BF16)
        for k in range(per):
            slots_out[k, span(part), :] = moved[span(k), :]
            grads_out[k, span(part), :] = moved[span(per + k), :]
    for k in range(per):
        if k:
            copy_first[k].wait()
        if k + 1 < per:
            copy_first[k + 1].start()
        first = w_first.at[k] if k else first_weight
        pre_act = dot(slots_out[k], first[...])
        phi = 0.5 * (1.0 + lax.erf(pre_act * math.sqrt(0.5)))
        density = jnp.exp(pre_act * pre_act * -0.5) * (1.0 / math.sqrt(2.0 * math.pi))
        hidden = (pre_act * phi).astype(BF16)
        hidden_out[k] = hidden
        copy_second[k].wait()
        if k + 1 < per:
            copy_second[k + 1].start()
        grad_hidden = dot(grads_out[k], w_second[k], 1, 1)
        out = dot(hidden, w_second[k]).astype(BF16)
        grad_pre = ((phi + pre_act * density) * grad_hidden).astype(BF16)
        pre_out[k] = grad_pre
        grad_slot = dot(grad_pre, first[...], 1, 1).astype(BF16)
        for part, target in enumerate(back_rows):
            target[span(k), :] = out[span(part), :]
            target[span(per + k), :] = grad_slot[span(part), :]


def run_experts(rows, first_weight, w_first, w_second):
    per, width, units = w_first.shape
    groups = len(rows)
    total = rows[0].shape[0]
    images = groups * total // (2 * per)
    results = call(
        functools.partial(experts_kernel, per, groups),
        "experts",
        [pltpu.VMEM((total, width), BF16)] * groups
        + [pltpu.VMEM((per, images, width), BF16)] * 2
        + [pltpu.VMEM((per, images, units), BF16)] * 2,
        32,
        8 * per * images * width * units,
        4 * per * width * units,
        in_specs=[pl.BlockSpec(memory_space=pltpu.VMEM)] * (groups + 1)
        + [pl.BlockSpec(memory_space=pltpu.HBM)] * 2,
        scratch_shapes=[
            pltpu.VMEM(w_first.shape, BF16),
            pltpu.VMEM(w_second.shape, BF16),
            pltpu.SemaphoreType.DMA((2, per)),
        ],
    )(*rows, first_weight, in_hbm(w_first), in_hbm(w_second))
    return results[:groups], results[groups:]


def outer_kernel(left, right, *refs):
    refs[-1][0] = dot(left[0], right[0], 0, 0).astype(BF16)


def outer(left, right, after, name, part, into=None):
    per, images, height = left.shape
    units = right.shape[2]
    begin, end = part
    per_expert = lambda a, b: pl.BlockSpec((1, a, b), lambda k: (k + begin, 0, 0))
    more = () if into is None else (in_hbm(into),)
    return call(
        outer_kernel,
        name,
        jax.ShapeDtypeStruct((per, height, units), BF16),
        16,
        2 * (end - begin) * images * height * units,
        2 * (end - begin) * height * units,
        grid=(end - begin,),
        in_specs=[
            per_expert(images, height),
            per_expert(images, units),
            pl.BlockSpec(memory_space=pl.ANY),
        ]
        + [pl.BlockSpec(memory_space=pltpu.HBM)] * len(more),
        out_specs=per_expert(height, units),
        input_output_aliases={3: 0} if more else {},
    )(left, right, after, *more)


def logits_kernel(per, groups, tokens, cotangent, disp, comb, outs, after1, after2, *refs):
    *parts, grad_logits, terms = refs
    rows = outs[...]
    disp_prob = disp[...]
    comb_prob = comb[...]
    first = first_half(per, disp_prob.shape)
    grad_comb = dot(cotangent[...], rows, 1, 1)
    grad_disp = dot(tokens[...], rows, 1, 1)
    part_disp = disp_prob * (
        grad_disp - jnp.sum(disp_prob * grad_disp, axis=0, keepdims=True)
    )
    comb_sum = jnp.sum(jnp.where(first, comb_prob * grad_comb, 0.0), axis=1, keepdims=True)
    part_comb = comb_prob * (grad_comb - comb_sum)
    both = jnp.where(first, part_comb, part_disp)
    cols = both.shape[1]
    other = jnp.where(first, pltpu.roll(both, cols - per, 1), pltpu.roll(both, per, 1))
    paired = (both + other).astype(BF16)
    grad_logits[...] = jnp.where(first, paired.astype(F32), 0.0).astype(BF16)
    one_each = dot(paired, pick_first(per, cols // 2)).astype(BF16)
    term = dot(one_each, tokens[...], 0, 0)
    height = terms.shape[1]
    for part in range(groups):
        terms[part] = term[part * height : (part + 1) * height, :].astype(BF16)
    me = lax.axis_index("dp")
    for part, out in enumerate(parts):
        out[...] = terms[lax.rem(me + part, groups)]


def finish_logits(per, groups, tokens, cotangent, disp, comb, outs, after1, after2):
    seq, width = tokens.shape
    cols = disp.shape[1]
    height = cols // 2 // groups
    results = call(
        functools.partial(logits_kernel, per, groups),
        "grad_logits",
        [pltpu.VMEM((height, width), BF16)] * groups + [pltpu.VMEM((seq, cols), BF16)],
        8,
        6 * seq * width * cols,
        6 * seq * width,
        in_specs=[pl.BlockSpec(memory_space=pltpu.VMEM)] * 5
        + [pl.BlockSpec(memory_space=pltpu.HBM)] * 2,
        scratch_shapes=[pltpu.VMEM((groups, height, width), BF16)],
    )(tokens, cotangent, disp, comb, outs, in_hbm(after1), in_hbm(after2))
    return results[:groups], results[groups]


def mixed_kernel(per, outs, comb, mixed):
    first = first_half(per, comb.shape)
    mixed[...] = dot(jnp.where(first, comb[...], 0.0).astype(BF16), outs[...]).astype(BF16)


def finish_mixed(per, outs, comb):
    seq, cols = comb.shape
    width = outs.shape[1]
    return call(
        functools.partial(mixed_kernel, per),
        "mixed",
        jax.ShapeDtypeStruct((seq, width), BF16),
        8,
        2 * seq * width * cols,
        2 * seq * width,
    )(outs, comb)


def tokens_kernel(per, outs, disp, grad_logits, router_t, after, grad_tokens):
    first = first_half(per, disp.shape)
    disp_cols = jnp.where(first, 0.0, disp[...]).astype(BF16)
    paired_router = dot(spread(per, router_t.shape[0]), router_t[...]).astype(BF16)
    grad_tokens[...] = (
        dot(disp_cols, outs[...]) + dot(grad_logits[...], paired_router)
    ).astype(BF16)


def finish_tokens(per, outs, disp, grad_logits, router_t, after):
    seq, cols = disp.shape
    width = outs.shape[1]
    return call(
        functools.partial(tokens_kernel, per),
        "grad_tokens",
        jax.ShapeDtypeStruct((seq, width), BF16),
        8,
        4 * seq * width * cols,
        2 * seq * width,
        in_specs=[pl.BlockSpec(memory_space=pltpu.VMEM)] * 4 + [pl.BlockSpec(memory_space=pl.ANY)],
    )(outs, disp, grad_logits, router_t, after)


def join_kernel(*refs):
    *parts, out = refs
    groups = len(parts)
    me = lax.axis_index("dp")
    for part, ref in enumerate(parts):
        out[lax.rem(me - part + groups, groups)] = ref[...].astype(F32)


def join(parts):
    height, width = parts[0].shape
    return call(
        join_kernel,
        "join",
        jax.ShapeDtypeStruct((len(parts), height, width), F32),
        4,
        0,
        6 * height * width,
    )(*parts).reshape(-1, width)


def across_chips(value, masks):
    groups, chips = lax.axis_size("dp"), lax.axis_size("expert")
    pairs = [
        (core * chips + i, core * chips + (i ^ masks[core]))
        for core in range(groups)
        for i in range(chips)
    ]
    return lax.ppermute(value, ("dp", "expert"), pairs)


def total_over_devices(parts, first_beside, beside):
    value = add(exchange(parts, "dp", 1), "add_cores", after=[first_beside])
    groups, chips = lax.axis_size("dp"), lax.axis_size("expert")
    rounds = []
    bit = 1
    while bit < chips:
        rounds.append([bit, 2 * bit, 3 * bit] if 4 * bit <= chips else [bit])
        bit *= 4
    even = len(rounds[-1]) == 3
    for step in range(len(rounds)):
        of_core = [rounds[(step + even * core) % len(rounds)] for core in range(groups)]
        others = [across_chips(value, masks) for masks in zip(*of_core)]
        after = [beside.pop(0)(value)] if beside else []
        value = add([value, *others], "add_chips", after=after)
    return value, join(exchange([value] * len(parts), "dp", 1))


def local(tokens, router, weight_in, weight_out, cotangent):
    per = weight_in.shape[0]
    experts = router.shape[1]
    chips = experts // per
    groups = lax.axis_size("dp")
    tokens, cotangent = tokens[0], cotangent[0]
    width = tokens.shape[1]
    router_t = router.T

    def to_chips(rows):
        blocks = rows.reshape(chips, 2 * per, width)
        blocks = lax.all_to_all(blocks, "expert", split_axis=0, concat_axis=0, tiled=True)
        return blocks.reshape(rows.shape)

    rows, disp, comb, tokens, cotangent = front(per, tokens, router_t, cotangent)
    rows = to_chips(rows)
    first_weight = fetch(rows, weight_in)
    rows = exchange([rows] * groups, "dp", 1)
    back_rows, (slots, grads, hidden, grad_pre) = run_experts(
        rows, first_weight, weight_in, weight_out
    )
    back_rows = add(exchange(back_rows, "dp", -1), "add_groups", chips)
    outs = to_chips(back_rows)
    grad_second = outer(hidden, grads, back_rows, "grad_weight_out", (0, per))
    grad_first = outer(slots, grad_pre, back_rows, "grad_weight_in", (0, 1))
    parts, grad_logits = finish_logits(
        per, groups, tokens, cotangent, disp, comb, outs, grad_first, grad_second
    )
    mixed = finish_mixed(per, outs, comb)

    def piece(part, value):
        nonlocal grad_first
        grad_first = outer(slots, grad_pre, value, "grad_weight_in", part, grad_first)
        return grad_first

    cut = (per + 2) // 2
    beside = [functools.partial(piece, part) for part in ((1, cut), (cut, per))]
    value, total = total_over_devices(parts, mixed, beside)
    grad_tokens = finish_tokens(per, outs, disp, grad_logits, router_t, value)
    grad_router = total.T
    return (mixed[None], grad_tokens[None], grad_router, grad_first, grad_second)


def solution(mesh):
    return jax.shard_map(
        local,
        mesh=mesh,
        in_specs=(
            P(("dp", "expert"), None, None),
            P(),
            P("expert", None, "dp"),
            P("expert", "dp", None),
            P(("dp", "expert"), None, None),
        ),
        out_specs=(
            P(("dp", "expert"), None, None),
            P(("dp", "expert"), None, None),
            P(),
            P("expert", None, "dp"),
            P("expert", "dp", None),
        ),
        check_vma=False,
    )
```

```python
import functools
import math

import jax
import jax.numpy as jnp
from jax import lax
from jax.experimental import pallas as pl
from jax.experimental.pallas import tpu as pltpu
from jax.sharding import PartitionSpec as P

F32 = jnp.float32
BF16 = jnp.bfloat16
MIB = 1024 * 1024


def dot(left, right, left_dim=1, right_dim=0):
    return lax.dot_general(
        left, right, (((left_dim,), (right_dim,)), ((), ())), preferred_element_type=F32
    )


def iota(shape, dim):
    return lax.broadcasted_iota(jnp.int32, shape, dim)


def in_hbm(value):
    return pltpu.with_memory_space_constraint(value, pltpu.HBM)


def call(kernel, name, out_shape, limit, flops, moved, **more):
    return pl.pallas_call(
        kernel,
        out_shape=out_shape,
        compiler_params=pltpu.CompilerParams(vmem_limit_bytes=limit * MIB),
        cost_estimate=pl.CostEstimate(flops=flops, bytes_accessed=moved, transcendentals=0),
        name=name,
        **more,
    )


def picked_expert(per, rows):
    return (rows // (2 * per)) * per + rows % per


def spread(per, experts):
    shape = (2 * experts, experts)
    return (picked_expert(per, iota(shape, 0)) == iota(shape, 1)).astype(BF16)


def pick_first(per, experts):
    shape = (2 * experts, experts)
    row = iota(shape, 0)
    return ((picked_expert(per, row) == iota(shape, 1)) & (row % (2 * per) < per)).astype(BF16)


def first_half(per, shape):
    return iota(shape, 1) % (2 * per) < per


def front_kernel(
    per, tokens_hbm, router_hbm, cotangent_hbm, rows, disp, comb, tokens, cotangent, router_t, sems
):
    copies = [
        pltpu.make_async_copy(source, target, sems.at[index])
        for index, (source, target) in enumerate(
            ((router_hbm, router_t), (tokens_hbm, tokens), (cotangent_hbm, cotangent))
        )
    ]
    for copy in copies:
        copy.start()
    matrix = spread(per, router_t.shape[0])
    copies[0].wait()
    paired_router = dot(matrix, router_t[...]).astype(BF16)
    copies[1].wait()
    logits = dot(tokens[...], paired_router, 1, 1)
    first = first_half(per, logits.shape)
    down = jnp.exp(logits - jnp.max(logits, axis=0, keepdims=True))
    disp_prob = down / jnp.sum(down, axis=0, keepdims=True)
    across = jnp.exp(logits - jnp.max(logits, axis=1, keepdims=True))
    comb_prob = across / jnp.sum(jnp.where(first, across, 0.0), axis=1, keepdims=True)
    disp[...] = disp_prob
    comb[...] = comb_prob
    disp_cols = jnp.where(first, disp_prob, 0.0).astype(BF16)
    comb_cols = jnp.where(first, 0.0, comb_prob).astype(BF16)
    copies[2].wait()
    rows[...] = (
        dot(disp_cols, tokens[...], 0, 0) + dot(comb_cols, cotangent[...], 0, 0)
    ).astype(BF16)


def front(per, tokens, router_t, cotangent):
    seq, width = tokens.shape
    experts = router_t.shape[0]
    return call(
        functools.partial(front_kernel, per),
        "front",
        (
            pltpu.VMEM((2 * experts, width), BF16),
            pltpu.VMEM((seq, 2 * experts), F32),
            pltpu.VMEM((seq, 2 * experts), F32),
            pltpu.VMEM(tokens.shape, BF16),
            pltpu.VMEM(cotangent.shape, BF16),
        ),
        8,
        12 * seq * width * experts,
        6 * seq * width,
        in_specs=[pl.BlockSpec(memory_space=pltpu.HBM)] * 3,
        scratch_shapes=[pltpu.VMEM(router_t.shape, BF16), pltpu.SemaphoreType.DMA((3,))],
    )(in_hbm(tokens), in_hbm(router_t), in_hbm(cotangent))


def digits(chips):
    low = 1 << ((chips.bit_length() - 1) // 2)
    return low, chips // low


def swapped(core, chips):
    low, high = digits(chips)
    return core % 2 if low == high else 0


def away(first, second, core, chips):
    low, _ = digits(chips)
    usual = first + low * second
    return usual + swapped(core, chips) * (low * first + second - usual)


def across_chips(value, steps):
    groups, chips = lax.axis_size("dp"), lax.axis_size("expert")
    pairs = [
        (core * chips + i, core * chips + (i ^ away(*steps, core, chips)))
        for core in range(groups)
        for i in range(chips)
    ]
    return lax.ppermute(value, ("dp", "expert"), pairs)


def shifted(value, axis, by):
    size = lax.axis_size(axis)
    return lax.ppermute(value, axis, [(i, (i + by) % size) for i in range(size)])


def exchange(blocks, axis, sign):
    return [blocks[0]] + [shifted(block, axis, sign * k) for k, block in enumerate(blocks) if k]


def sort_matrix(images, wide):
    shape = (images * wide, images * wide)
    to, start = iota(shape, 0), iota(shape, 1)
    return ((to % images) * wide + to // images == start).astype(BF16)


def other_chip(first, second, chips):
    return lax.axis_index("expert") ^ away(first, second, lax.axis_index("dp"), chips)


def pair_sum(pieces):
    total = [piece[...].astype(F32) for piece in pieces]
    while len(total) > 1:
        total = [sum(total[index : index + 2]) for index in range(0, len(total), 2)]
    return total[0]


def add_kernel(count, *refs):
    refs[-1][...] = pair_sum(refs[:count]).astype(BF16)


def add(pieces, name, after=()):
    size = pieces[0].size
    return call(
        functools.partial(add_kernel, len(pieces)),
        name,
        pltpu.VMEM(pieces[0].shape, BF16),
        4,
        len(pieces) * size,
        4 * size,
        in_specs=[pl.BlockSpec(memory_space=pltpu.VMEM)] * len(pieces)
        + [pl.BlockSpec(memory_space=pltpu.HBM)] * len(after),
    )(*pieces, *map(in_hbm, after))


def groups_kernel(count, wide, *refs):
    pieces, outs = refs[:count], refs[count:]
    total = pair_sum(pieces).astype(BF16)
    chips = total.shape[0] // wide
    _, later = digits(chips)
    shape = (chips * wide, chips * wide)
    to, start = iota(shape, 0), iota(shape, 1)
    chip = other_chip(to // (later * wide), to // wide % later, chips)
    moved = dot((start == to % wide * chips + chip).astype(BF16), total)
    height = later * wide
    for part, out in enumerate(outs):
        out[...] = moved[part * height : (part + 1) * height, :].astype(BF16)


def add_groups(pieces, wide):
    total, width = pieces[0].shape
    first, _ = digits(total // wide)
    return call(
        functools.partial(groups_kernel, len(pieces), wide),
        "add_groups",
        [pltpu.VMEM((total // first, width), BF16)] * first,
        8,
        2 * total * total * width,
        4 * total * width,
    )(*pieces)


def regroup_kernel(count, wide, *refs):
    blocks, outs = [ref[...].astype(F32) for ref in refs[:count]], refs[count + 1 :]
    for part, out in enumerate(outs):
        rows = [block[part * wide : (part + 1) * wide, :] for block in blocks]
        out[...] = jnp.concatenate(rows).astype(BF16)


def regroup(blocks, wide, after):
    height, width = blocks[0].shape
    later = height // wide
    return call(
        functools.partial(regroup_kernel, len(blocks), wide),
        "regroup",
        [pltpu.VMEM((len(blocks) * wide, width), BF16)] * later,
        4,
        0,
        4 * height * width * len(blocks),
        in_specs=[pl.BlockSpec(memory_space=pltpu.VMEM)] * len(blocks)
        + [pl.BlockSpec(memory_space=pltpu.HBM)],
    )(*blocks, in_hbm(after))


def fetch_kernel(rows, source, target, sems):
    height = target.shape[0] // sems.shape[0]
    copies = [
        pltpu.make_async_copy(
            source.at[0, pl.ds(part * height, height)],
            target.at[pl.ds(part * height, height)],
            sems.at[part],
        )
        for part in range(sems.shape[0])
    ]
    for copy in copies:
        copy.start()
    for copy in copies:
        copy.wait()


def fetch(after, weight):
    return call(
        fetch_kernel,
        "fetch_first",
        pltpu.VMEM(weight.shape[1:], BF16),
        2,
        0,
        4 * weight[0].size,
        in_specs=[pl.BlockSpec(memory_space=pl.ANY), pl.BlockSpec(memory_space=pltpu.HBM)],
        scratch_shapes=[pltpu.SemaphoreType.DMA((2,))],
    )(after, in_hbm(weight))


def experts_kernel(per, groups, *refs):
    rows, refs = refs[:groups], refs[groups:]
    first_weight, *weights_hbm = refs[:3]
    refs = refs[3:]
    back_rows, refs = refs[:groups], refs[groups:]
    slots_out, grads_out, hidden_out, pre_out, w_first, w_second, sems = refs
    wide = 2 * per
    size = rows[0].shape[0] // wide
    span = lambda j: slice(j * size, (j + 1) * size)
    def copy(k, index):
        target = (w_first, w_second)[index]
        return pltpu.make_async_copy(weights_hbm[index].at[k], target.at[k], sems.at[index, k])

    copy_first = [None] + [copy(k, 0) for k in range(1, per)]
    copy_second = [copy(k, 1) for k in range(per)]
    order = [copy for pair in zip(copy_first, copy_second) for copy in pair][1:]
    order[0].start()
    matrix = sort_matrix(size, wide)
    for part in range(groups):
        moved = dot(matrix, rows[part][...]).astype(BF16)
        for k in range(per):
            slots_out[k, span(part), :] = moved[span(k), :]
            grads_out[k, span(part), :] = moved[span(per + k), :]
    ahead = 3
    for copy in order[1:ahead]:
        copy.start()

    def wait(index):
        order[index].wait()
        if index + ahead < len(order):
            order[index + ahead].start()

    for k in range(per):
        if k:
            wait(2 * k - 1)
        first = w_first.at[k] if k else first_weight
        pre_act = dot(slots_out[k], first[...])
        phi = 0.5 * (1.0 + lax.erf(pre_act * math.sqrt(0.5)))
        density = jnp.exp(pre_act * pre_act * -0.5) * (1.0 / math.sqrt(2.0 * math.pi))
        hidden = (pre_act * phi).astype(BF16)
        hidden_out[k] = hidden
        wait(2 * k)
        grad_hidden = dot(grads_out[k], w_second[k], 1, 1)
        out = dot(hidden, w_second[k]).astype(BF16)
        grad_pre = ((phi + pre_act * density) * grad_hidden).astype(BF16)
        pre_out[k] = grad_pre
        grad_slot = dot(grad_pre, first[...], 1, 1).astype(BF16)
        for part, target in enumerate(back_rows):
            target[span(k), :] = out[span(part), :]
            target[span(per + k), :] = grad_slot[span(part), :]


def run_experts(rows, first_weight, w_first, w_second):
    per, width, units = w_first.shape
    groups = len(rows)
    total = rows[0].shape[0]
    images = groups * total // (2 * per)
    results = call(
        functools.partial(experts_kernel, per, groups),
        "experts",
        [pltpu.VMEM((total, width), BF16)] * groups
        + [pltpu.VMEM((per, images, width), BF16)] * 2
        + [pltpu.VMEM((per, images, units), BF16)] * 2,
        32,
        8 * per * images * width * units,
        4 * per * width * units,
        in_specs=[pl.BlockSpec(memory_space=pltpu.VMEM)] * (groups + 1)
        + [pl.BlockSpec(memory_space=pltpu.HBM)] * 2,
        scratch_shapes=[
            pltpu.VMEM(w_first.shape, BF16),
            pltpu.VMEM(w_second.shape, BF16),
            pltpu.SemaphoreType.DMA((2, per)),
        ],
    )(*rows, first_weight, in_hbm(w_first), in_hbm(w_second))
    return results[:groups], results[groups:]


def outer_kernel(left, right, *refs):
    refs[-1][0] = dot(left[0], right[0], 0, 0).astype(BF16)


def outer(left, right, after, name, part, into=None):
    per, images, height = left.shape
    units = right.shape[2]
    begin, end = part
    per_expert = lambda a, b: pl.BlockSpec((1, a, b), lambda k: (k + begin, 0, 0))
    more = () if into is None else (in_hbm(into),)
    return call(
        outer_kernel,
        name,
        jax.ShapeDtypeStruct((per, height, units), BF16),
        16,
        2 * (end - begin) * images * height * units,
        2 * (end - begin) * height * units,
        grid=(end - begin,),
        in_specs=[
            per_expert(images, height),
            per_expert(images, units),
            pl.BlockSpec(memory_space=pl.ANY),
        ]
        + [pl.BlockSpec(memory_space=pltpu.HBM)] * len(more),
        out_specs=per_expert(height, units),
        input_output_aliases={3: 0} if more else {},
    )(left, right, after, *more)


def logits_kernel(per, groups, tokens, cotangent, disp, comb, after, *refs):
    *blocks, outs, grad_logits, terms = refs
    blocks, parts = blocks[:-groups], blocks[-groups:]
    moved = jnp.concatenate([block[...].astype(F32) for block in blocks]).astype(BF16)
    wide = 2 * per
    shape = (moved.shape[0], moved.shape[0])
    chips = shape[0] // wide
    to, start = iota(shape, 0), iota(shape, 1)
    earlier, _ = digits(chips)
    chip = other_chip(start // wide % earlier, start // (earlier * wide), chips)
    rows = dot((to == chip * wide + start % wide).astype(BF16), moved).astype(BF16)
    outs[...] = rows
    disp_prob = disp[...]
    comb_prob = comb[...]
    first = first_half(per, disp_prob.shape)
    grad_comb = dot(cotangent[...], rows, 1, 1)
    grad_disp = dot(tokens[...], rows, 1, 1)
    part_disp = disp_prob * (
        grad_disp - jnp.sum(disp_prob * grad_disp, axis=0, keepdims=True)
    )
    comb_sum = jnp.sum(jnp.where(first, comb_prob * grad_comb, 0.0), axis=1, keepdims=True)
    part_comb = comb_prob * (grad_comb - comb_sum)
    both = jnp.where(first, part_comb, part_disp)
    cols = both.shape[1]
    other = jnp.where(first, pltpu.roll(both, cols - per, 1), pltpu.roll(both, per, 1))
    paired = (both + other).astype(BF16)
    grad_logits[...] = jnp.where(first, paired.astype(F32), 0.0).astype(BF16)
    one_each = dot(paired, pick_first(per, cols // 2)).astype(BF16)
    term = dot(one_each, tokens[...], 0, 0)
    height = terms.shape[1]
    for part in range(groups):
        terms[part] = term[part * height : (part + 1) * height, :].astype(BF16)
    me = lax.axis_index("dp")
    for part, out in enumerate(parts):
        out[...] = terms[lax.rem(me + part, groups)]


def finish_logits(per, groups, tokens, cotangent, disp, comb, blocks, after):
    seq, width = tokens.shape
    cols = disp.shape[1]
    height = cols // 2 // groups
    results = call(
        functools.partial(logits_kernel, per, groups),
        "grad_logits",
        [pltpu.VMEM((height, width), BF16)] * groups
        + [pltpu.VMEM((cols, width), BF16), pltpu.VMEM((seq, cols), BF16)],
        12,
        6 * seq * width * cols,
        6 * seq * width,
        in_specs=[pl.BlockSpec(memory_space=pltpu.VMEM)] * 4
        + [pl.BlockSpec(memory_space=pltpu.HBM)]
        + [pl.BlockSpec(memory_space=pltpu.VMEM)] * len(blocks),
        scratch_shapes=[pltpu.VMEM((groups, height, width), BF16)],
    )(tokens, cotangent, disp, comb, in_hbm(after), *blocks)
    return results[:groups], *results[groups:]


def mixed_kernel(per, outs, comb, mixed):
    first = first_half(per, comb.shape)
    mixed[...] = dot(jnp.where(first, comb[...], 0.0).astype(BF16), outs[...]).astype(BF16)


def finish_mixed(per, outs, comb):
    seq, cols = comb.shape
    width = outs.shape[1]
    return call(
        functools.partial(mixed_kernel, per),
        "mixed",
        jax.ShapeDtypeStruct((seq, width), BF16),
        8,
        2 * seq * width * cols,
        2 * seq * width,
    )(outs, comb)


def tokens_kernel(per, outs, disp, grad_logits, router_t, after, grad_tokens):
    first = first_half(per, disp.shape)
    disp_cols = jnp.where(first, 0.0, disp[...]).astype(BF16)
    paired_router = dot(spread(per, router_t.shape[0]), router_t[...]).astype(BF16)
    grad_tokens[...] = (
        dot(disp_cols, outs[...]) + dot(grad_logits[...], paired_router)
    ).astype(BF16)


def finish_tokens(per, outs, disp, grad_logits, router_t, after):
    seq, cols = disp.shape
    width = outs.shape[1]
    return call(
        functools.partial(tokens_kernel, per),
        "grad_tokens",
        jax.ShapeDtypeStruct((seq, width), BF16),
        8,
        4 * seq * width * cols,
        2 * seq * width,
        in_specs=[pl.BlockSpec(memory_space=pltpu.VMEM)] * 4 + [pl.BlockSpec(memory_space=pl.ANY)],
    )(outs, disp, grad_logits, router_t, after)


def join_kernel(*refs):
    *parts, out = refs
    groups = len(parts)
    me = lax.axis_index("dp")
    for part, ref in enumerate(parts):
        out[lax.rem(me - part + groups, groups)] = ref[...].astype(F32)


def join(parts):
    height, width = parts[0].shape
    return call(
        join_kernel,
        "join",
        jax.ShapeDtypeStruct((len(parts), height, width), F32),
        4,
        0,
        6 * height * width,
    )(*parts).reshape(-1, width)


def total_over_devices(parts, first_beside, beside):
    value = add(exchange(parts, "dp", 1), "add_cores", after=[first_beside])
    for step, size in enumerate(digits(lax.axis_size("expert"))):
        steps = [(0, m) if step else (m, 0) for m in range(1, size)]
        others = [across_chips(value, away_by) for away_by in steps]
        value = add([value, *others], "add_chips", after=[beside.pop(0)(value)])
    return value, join(exchange([value] * len(parts), "dp", 1))


def local(tokens, router, weight_in, weight_out, cotangent):
    per = weight_in.shape[0]
    experts = router.shape[1]
    chips = experts // per
    groups = lax.axis_size("dp")
    tokens, cotangent = tokens[0], cotangent[0]
    width = tokens.shape[1]
    router_t = router.T

    rows, disp, comb, tokens, cotangent = front(per, tokens, router_t, cotangent)
    rows = rows.reshape(chips, 2 * per, width)
    rows = lax.all_to_all(rows, "expert", split_axis=0, concat_axis=0, tiled=True)
    rows = rows.reshape(2 * experts, width)
    first_weight = fetch(rows, weight_in)
    rows = exchange([rows] * groups, "dp", 1)
    back_rows, (slots, grads, hidden, grad_pre) = run_experts(
        rows, first_weight, weight_in, weight_out
    )

    def first_grad(part, after, into=None):
        return outer(slots, grad_pre, after, "grad_weight_in", part, into)

    def second_grad(part, after, into=None):
        return outer(hidden, grads, after, "grad_weight_out", part, into)

    early, late = (0, per // 2), (per // 2, per)
    blocks = add_groups(exchange(back_rows, "dp", -1), 2 * per)
    grad_second = second_grad(early, blocks[0])
    blocks = [across_chips(block, (m, 0)) if m else block for m, block in enumerate(blocks)]
    blocks = regroup(blocks, 2 * per, grad_second)
    grad_second = second_grad(late, blocks[0], grad_second)
    blocks = [across_chips(block, (0, m)) if m else block for m, block in enumerate(blocks)]
    parts, outs, grad_logits = finish_logits(
        per, groups, tokens, cotangent, disp, comb, blocks, grad_second
    )
    mixed = finish_mixed(per, outs, comb)
    grad_first = None

    def piece(part, value):
        nonlocal grad_first
        grad_first = first_grad(part, value, grad_first)
        return grad_first

    beside = [functools.partial(piece, part) for part in (early, late)]
    value, total = total_over_devices(parts, mixed, beside)
    grad_tokens = finish_tokens(per, outs, disp, grad_logits, router_t, value)
    grad_router = total.T
    return (mixed[None], grad_tokens[None], grad_router, grad_first, grad_second)


def solution(mesh):
    return jax.shard_map(
        local,
        mesh=mesh,
        in_specs=(
            P(("dp", "expert"), None, None),
            P(),
            P("expert", None, "dp"),
            P("expert", "dp", None),
            P(("dp", "expert"), None, None),
        ),
        out_specs=(
            P(("dp", "expert"), None, None),
            P(("dp", "expert"), None, None),
            P(),
            P("expert", None, "dp"),
            P("expert", "dp", None),
        ),
        check_vma=False,
    )
```

```python
import functools
import math

import jax
import jax.numpy as jnp
from jax import lax
from jax.experimental import pallas as pl
from jax.experimental.pallas import tpu as pltpu
from jax.sharding import PartitionSpec as P

F32 = jnp.float32
BF16 = jnp.bfloat16
MIB = 1024 * 1024


def dot(left, right, left_dim=1, right_dim=0):
    return lax.dot_general(
        left, right, (((left_dim,), (right_dim,)), ((), ())), preferred_element_type=F32
    )


def iota(shape, dim):
    return lax.broadcasted_iota(jnp.int32, shape, dim)


def in_hbm(value):
    return pltpu.with_memory_space_constraint(value, pltpu.HBM)


def call(kernel, name, out_shape, limit, flops, moved, **more):
    return pl.pallas_call(
        kernel,
        out_shape=out_shape,
        compiler_params=pltpu.CompilerParams(vmem_limit_bytes=limit * MIB),
        cost_estimate=pl.CostEstimate(flops=flops, bytes_accessed=moved, transcendentals=0),
        name=name,
        **more,
    )


def picked_expert(per, rows):
    return (rows // (2 * per)) * per + rows % per


def spread(per, experts):
    shape = (2 * experts, experts)
    return (picked_expert(per, iota(shape, 0)) == iota(shape, 1)).astype(BF16)


def pick_first(per, experts):
    shape = (2 * experts, experts)
    row = iota(shape, 0)
    return ((picked_expert(per, row) == iota(shape, 1)) & (row % (2 * per) < per)).astype(BF16)


def first_half(per, shape):
    return iota(shape, 1) % (2 * per) < per


def front_kernel(per, tokens_hbm, router_hbm, cotangent_hbm, weight_hbm, *refs):
    rows, disp, comb, tokens, cotangent, weight, router_t, sems = refs
    copies = [
        pltpu.make_async_copy(source, target, sems.at[index])
        for index, (source, target) in enumerate(
            (
                (router_hbm, router_t),
                (tokens_hbm, tokens),
                (cotangent_hbm, cotangent),
                (weight_hbm.at[0], weight),
            )
        )
    ]
    for copy in copies:
        copy.start()
    matrix = spread(per, router_t.shape[0])
    copies[0].wait()
    paired_router = dot(matrix, router_t[...]).astype(BF16)
    copies[1].wait()
    logits = dot(tokens[...], paired_router, 1, 1)
    first = first_half(per, logits.shape)
    down = jnp.exp(logits - jnp.max(logits, axis=0, keepdims=True))
    disp_prob = down / jnp.sum(down, axis=0, keepdims=True)
    across = jnp.exp(logits - jnp.max(logits, axis=1, keepdims=True))
    comb_prob = across / jnp.sum(jnp.where(first, across, 0.0), axis=1, keepdims=True)
    disp[...] = disp_prob
    comb[...] = comb_prob
    disp_cols = jnp.where(first, disp_prob, 0.0).astype(BF16)
    comb_cols = jnp.where(first, 0.0, comb_prob).astype(BF16)
    copies[2].wait()
    rows[...] = (
        dot(disp_cols, tokens[...], 0, 0) + dot(comb_cols, cotangent[...], 0, 0)
    ).astype(BF16)
    copies[3].wait()


def front(per, tokens, router_t, cotangent, weight):
    seq, width = tokens.shape
    experts = router_t.shape[0]
    return call(
        functools.partial(front_kernel, per),
        "front",
        (
            pltpu.VMEM((2 * experts, width), BF16),
            pltpu.VMEM((seq, 2 * experts), F32),
            pltpu.VMEM((seq, 2 * experts), F32),
            pltpu.VMEM(tokens.shape, BF16),
            pltpu.VMEM(cotangent.shape, BF16),
            pltpu.VMEM(weight.shape[1:], BF16),
        ),
        8,
        12 * seq * width * experts,
        6 * seq * width,
        in_specs=[pl.BlockSpec(memory_space=pltpu.HBM)] * 4,
        scratch_shapes=[pltpu.VMEM(router_t.shape, BF16), pltpu.SemaphoreType.DMA((4,))],
    )(in_hbm(tokens), in_hbm(router_t), in_hbm(cotangent), in_hbm(weight))


def shifted(value, axis, by):
    size = lax.axis_size(axis)
    return lax.ppermute(value, axis, [(i, (i + by) % size) for i in range(size)])


def exchange(blocks, axis, sign):
    return [blocks[0]] + [shifted(block, axis, sign * k) for k, block in enumerate(blocks) if k]


def sort_matrix(images, wide, transposed):
    shape = (images * wide, images * wide)
    to, start = (iota(shape, 1), iota(shape, 0)) if transposed else (iota(shape, 0), iota(shape, 1))
    return ((to % images) * wide + to // images == start).astype(BF16)


def add_kernel(images, count, *refs):
    pieces, out = refs[:count], refs[-1]
    total = [piece[...].astype(F32) for piece in pieces]
    while len(total) > 1:
        total = [sum(total[index : index + 2]) for index in range(0, len(total), 2)]
    total = total[0].astype(BF16)
    if images:
        total = dot(sort_matrix(images, total.shape[0] // images, True), total).astype(BF16)
    out[...] = total


def add(pieces, name, images=0, after=()):
    size = pieces[0].size
    return call(
        functools.partial(add_kernel, images, len(pieces)),
        name,
        pltpu.VMEM(pieces[0].shape, BF16),
        4,
        len(pieces) * size,
        4 * size,
        in_specs=[pl.BlockSpec(memory_space=pltpu.VMEM)] * len(pieces)
        + [pl.BlockSpec(memory_space=pltpu.HBM)] * len(after),
    )(*pieces, *map(in_hbm, after))


def fetch_kernel(rows, source, target, sems):
    height = target.shape[0] // sems.shape[0]
    copies = [
        pltpu.make_async_copy(
            source.at[0, pl.ds(part * height, height)],
            target.at[pl.ds(part * height, height)],
            sems.at[part],
        )
        for part in range(sems.shape[0])
    ]
    for copy in copies:
        copy.start()
    for copy in copies:
        copy.wait()


def fetch(after, weight):
    return call(
        fetch_kernel,
        "fetch_first",
        pltpu.VMEM(weight.shape[1:], BF16),
        2,
        0,
        4 * weight[0].size,
        in_specs=[pl.BlockSpec(memory_space=pl.ANY), pl.BlockSpec(memory_space=pltpu.HBM)],
        scratch_shapes=[pltpu.SemaphoreType.DMA((2,))],
    )(after, in_hbm(weight))


def experts_kernel(per, groups, *refs):
    rows, refs = refs[:groups], refs[groups:]
    resident, weights_hbm, refs = refs[:2], refs[2:4], refs[4:]
    back_rows, refs = refs[:groups], refs[groups:]
    slots_out, grads_out, hidden_out, pre_out, w_first, w_second, sems = refs
    wide = 2 * per
    size = rows[0].shape[0] // wide
    span = lambda j: slice(j * size, (j + 1) * size)
    def copy(k, index):
        target = (w_first, w_second)[index]
        return pltpu.make_async_copy(weights_hbm[index].at[k], target.at[k], sems.at[index, k])

    copies = [None] + [(copy(k, 0), copy(k, 1)) for k in range(1, per)]

    def start(k):
        for one in copies[k] if k < per else ():
            one.start()

    start(1)
    matrix = sort_matrix(size, wide, False)
    for part in range(groups):
        moved = dot(matrix, rows[part][...]).astype(BF16)
        for k in range(per):
            slots_out[k, span(part), :] = moved[span(k), :]
            grads_out[k, span(part), :] = moved[span(per + k), :]
    for k in range(per):
        for one in copies[k] if k else ():
            one.wait()
        start(k + 2)
        first, second = (w_first.at[k], w_second.at[k]) if k else resident
        pre_act = dot(slots_out[k], first[...])
        grad_hidden = dot(grads_out[k], second[...], 1, 1)
        phi = 0.5 * (1.0 + lax.erf(pre_act * math.sqrt(0.5)))
        density = jnp.exp(pre_act * pre_act * -0.5) * (1.0 / math.sqrt(2.0 * math.pi))
        hidden = (pre_act * phi).astype(BF16)
        hidden_out[k] = hidden
        out = dot(hidden, second[...]).astype(BF16)
        grad_pre = ((phi + pre_act * density) * grad_hidden).astype(BF16)
        pre_out[k] = grad_pre
        grad_slot = dot(grad_pre, first[...], 1, 1).astype(BF16)
        for part, target in enumerate(back_rows):
            target[span(k), :] = out[span(part), :]
            target[span(per + k), :] = grad_slot[span(part), :]


def run_experts(rows, weights, w_first, w_second):
    per, width, units = w_first.shape
    groups = len(rows)
    total = rows[0].shape[0]
    images = groups * total // (2 * per)
    results = call(
        functools.partial(experts_kernel, per, groups),
        "experts",
        [pltpu.VMEM((total, width), BF16)] * groups
        + [pltpu.VMEM((per, images, width), BF16)] * 2
        + [pltpu.VMEM((per, images, units), BF16)] * 2,
        32,
        8 * per * images * width * units,
        4 * per * width * units,
        in_specs=[pl.BlockSpec(memory_space=pltpu.VMEM)] * (groups + 2)
        + [pl.BlockSpec(memory_space=pltpu.HBM)] * 2,
        scratch_shapes=[
            pltpu.VMEM(w_first.shape, BF16),
            pltpu.VMEM(w_second.shape, BF16),
            pltpu.SemaphoreType.DMA((2, per)),
        ],
    )(*rows, *weights, in_hbm(w_first), in_hbm(w_second))
    return results[:groups], results[groups:]


def outer_kernel(left, right, *refs):
    refs[-1][0] = dot(left[0], right[0], 0, 0).astype(BF16)


def outer(left, right, after, name, part, into=None):
    per, images, height = left.shape
    units = right.shape[2]
    begin, end = part
    per_expert = lambda a, b: pl.BlockSpec((1, a, b), lambda k: (k + begin, 0, 0))
    more = () if into is None else (in_hbm(into),)
    return call(
        outer_kernel,
        name,
        jax.ShapeDtypeStruct((per, height, units), BF16),
        16,
        2 * (end - begin) * images * height * units,
        2 * (end - begin) * height * units,
        grid=(end - begin,),
        in_specs=[
            per_expert(images, height),
            per_expert(images, units),
            pl.BlockSpec(memory_space=pl.ANY),
        ]
        + [pl.BlockSpec(memory_space=pltpu.HBM)] * len(more),
        out_specs=per_expert(height, units),
        input_output_aliases={3: 0} if more else {},
    )(left, right, after, *more)


def logits_kernel(per, groups, tokens, cotangent, disp, comb, outs, after1, after2, *refs):
    *parts, grad_logits, terms = refs
    rows = outs[...]
    disp_prob = disp[...]
    comb_prob = comb[...]
    first = first_half(per, disp_prob.shape)
    grad_comb = dot(cotangent[...], rows, 1, 1)
    grad_disp = dot(tokens[...], rows, 1, 1)
    part_disp = disp_prob * (
        grad_disp - jnp.sum(disp_prob * grad_disp, axis=0, keepdims=True)
    )
    comb_sum = jnp.sum(jnp.where(first, comb_prob * grad_comb, 0.0), axis=1, keepdims=True)
    part_comb = comb_prob * (grad_comb - comb_sum)
    both = jnp.where(first, part_comb, part_disp)
    cols = both.shape[1]
    other = jnp.where(first, pltpu.roll(both, cols - per, 1), pltpu.roll(both, per, 1))
    paired = (both + other).astype(BF16)
    grad_logits[...] = jnp.where(first, paired.astype(F32), 0.0).astype(BF16)
    one_each = dot(paired, pick_first(per, cols // 2)).astype(BF16)
    term = dot(one_each, tokens[...], 0, 0)
    height = terms.shape[1]
    for part in range(groups):
        terms[part] = term[part * height : (part + 1) * height, :].astype(BF16)
    me = lax.axis_index("dp")
    for part, out in enumerate(parts):
        out[...] = terms[lax.rem(me + part, groups)]


def finish_logits(per, groups, tokens, cotangent, disp, comb, outs, after1, after2):
    seq, width = tokens.shape
    cols = disp.shape[1]
    height = cols // 2 // groups
    results = call(
        functools.partial(logits_kernel, per, groups),
        "grad_logits",
        [pltpu.VMEM((height, width), BF16)] * groups + [pltpu.VMEM((seq, cols), BF16)],
        8,
        6 * seq * width * cols,
        6 * seq * width,
        in_specs=[pl.BlockSpec(memory_space=pltpu.VMEM)] * 5
        + [pl.BlockSpec(memory_space=pltpu.HBM)] * 2,
        scratch_shapes=[pltpu.VMEM((groups, height, width), BF16)],
    )(tokens, cotangent, disp, comb, outs, in_hbm(after1), in_hbm(after2))
    return results[:groups], results[groups]


def mixed_kernel(per, outs, comb, mixed):
    first = first_half(per, comb.shape)
    mixed[...] = dot(jnp.where(first, comb[...], 0.0).astype(BF16), outs[...]).astype(BF16)


def finish_mixed(per, outs, comb):
    seq, cols = comb.shape
    width = outs.shape[1]
    return call(
        functools.partial(mixed_kernel, per),
        "mixed",
        jax.ShapeDtypeStruct((seq, width), BF16),
        8,
        2 * seq * width * cols,
        2 * seq * width,
    )(outs, comb)


def tokens_kernel(per, outs, disp, grad_logits, router_t, after, grad_tokens):
    first = first_half(per, disp.shape)
    disp_cols = jnp.where(first, 0.0, disp[...]).astype(BF16)
    paired_router = dot(spread(per, router_t.shape[0]), router_t[...]).astype(BF16)
    grad_tokens[...] = (
        dot(disp_cols, outs[...]) + dot(grad_logits[...], paired_router)
    ).astype(BF16)


def finish_tokens(per, outs, disp, grad_logits, router_t, after):
    seq, cols = disp.shape
    width = outs.shape[1]
    return call(
        functools.partial(tokens_kernel, per),
        "grad_tokens",
        jax.ShapeDtypeStruct((seq, width), BF16),
        8,
        4 * seq * width * cols,
        2 * seq * width,
        in_specs=[pl.BlockSpec(memory_space=pltpu.VMEM)] * 4 + [pl.BlockSpec(memory_space=pl.ANY)],
    )(outs, disp, grad_logits, router_t, after)


def join_kernel(*refs):
    *parts, out = refs
    groups = len(parts)
    me = lax.axis_index("dp")
    for part, ref in enumerate(parts):
        out[lax.rem(me - part + groups, groups)] = ref[...].astype(F32)


def join(parts):
    height, width = parts[0].shape
    return call(
        join_kernel,
        "join",
        jax.ShapeDtypeStruct((len(parts), height, width), F32),
        4,
        0,
        6 * height * width,
    )(*parts).reshape(-1, width)


def across_chips(value, masks):
    groups, chips = lax.axis_size("dp"), lax.axis_size("expert")
    pairs = [
        (core * chips + i, core * chips + (i ^ masks[core]))
        for core in range(groups)
        for i in range(chips)
    ]
    return lax.ppermute(value, ("dp", "expert"), pairs)


def total_over_devices(parts, first_beside, beside):
    value = add(exchange(parts, "dp", 1), "add_cores", after=[first_beside])
    groups, chips = lax.axis_size("dp"), lax.axis_size("expert")
    rounds = []
    bit = 1
    while bit < chips:
        rounds.append([bit, 2 * bit, 3 * bit] if 4 * bit <= chips else [bit])
        bit *= 4
    even = len(rounds[-1]) == 3
    for step in range(len(rounds)):
        of_core = [rounds[(step + even * core) % len(rounds)] for core in range(groups)]
        others = [across_chips(value, masks) for masks in zip(*of_core)]
        after = [beside.pop(0)(value)] if beside else []
        value = add([value, *others], "add_chips", after=after)
    return value, join(exchange([value] * len(parts), "dp", 1))


def local(tokens, router, weight_in, weight_out, cotangent):
    per = weight_in.shape[0]
    experts = router.shape[1]
    chips = experts // per
    groups = lax.axis_size("dp")
    tokens, cotangent = tokens[0], cotangent[0]
    width = tokens.shape[1]
    router_t = router.T

    def to_chips(rows):
        blocks = rows.reshape(chips, 2 * per, width)
        blocks = lax.all_to_all(blocks, "expert", split_axis=0, concat_axis=0, tiled=True)
        return blocks.reshape(rows.shape)

    rows, disp, comb, tokens, cotangent, second_weight = front(
        per, tokens, router_t, cotangent, weight_out
    )
    rows = to_chips(rows)
    first_weight = fetch(rows, weight_in)
    rows = exchange([rows] * groups, "dp", 1)
    back_rows, (slots, grads, hidden, grad_pre) = run_experts(
        rows, (first_weight, second_weight), weight_in, weight_out
    )
    back_rows = add(exchange(back_rows, "dp", -1), "add_groups", chips)
    outs = to_chips(back_rows)
    grad_second = outer(hidden, grads, back_rows, "grad_weight_out", (0, per))
    grad_first = outer(slots, grad_pre, back_rows, "grad_weight_in", (0, 1))
    parts, grad_logits = finish_logits(
        per, groups, tokens, cotangent, disp, comb, outs, grad_first, grad_second
    )
    mixed = finish_mixed(per, outs, comb)

    def piece(part, value):
        nonlocal grad_first
        grad_first = outer(slots, grad_pre, value, "grad_weight_in", part, grad_first)
        return grad_first

    cut = (per + 2) // 2
    beside = [functools.partial(piece, part) for part in ((1, cut), (cut, per))]
    value, total = total_over_devices(parts, mixed, beside)
    grad_tokens = finish_tokens(per, outs, disp, grad_logits, router_t, value)
    grad_router = total.T
    return (mixed[None], grad_tokens[None], grad_router, grad_first, grad_second)


def solution(mesh):
    return jax.shard_map(
        local,
        mesh=mesh,
        in_specs=(
            P(("dp", "expert"), None, None),
            P(),
            P("expert", None, "dp"),
            P("expert", "dp", None),
            P(("dp", "expert"), None, None),
        ),
        out_specs=(
            P(("dp", "expert"), None, None),
            P(("dp", "expert"), None, None),
            P(),
            P("expert", None, "dp"),
            P("expert", "dp", None),
        ),
        check_vma=False,
    )
```

```python
import functools
import math

import jax
import jax.numpy as jnp
from jax import lax
from jax.experimental import pallas as pl
from jax.experimental.pallas import tpu as pltpu
from jax.sharding import PartitionSpec as P

F32 = jnp.float32
BF16 = jnp.bfloat16
MIB = 1024 * 1024


def dot(left, right, left_dim=1, right_dim=0):
    return lax.dot_general(
        left, right, (((left_dim,), (right_dim,)), ((), ())), preferred_element_type=F32
    )


def iota(shape, dim):
    return lax.broadcasted_iota(jnp.int32, shape, dim)


def in_hbm(value):
    return pltpu.with_memory_space_constraint(value, pltpu.HBM)


def call(kernel, name, out_shape, limit, flops, moved, **more):
    return pl.pallas_call(
        kernel,
        out_shape=out_shape,
        compiler_params=pltpu.CompilerParams(vmem_limit_bytes=limit * MIB),
        cost_estimate=pl.CostEstimate(flops=flops, bytes_accessed=moved, transcendentals=0),
        name=name,
        **more,
    )


def picked_expert(per, rows):
    return (rows // (2 * per)) * per + rows % per


def spread(per, experts):
    shape = (2 * experts, experts)
    return (picked_expert(per, iota(shape, 0)) == iota(shape, 1)).astype(BF16)


def pick_first(per, experts):
    shape = (2 * experts, experts)
    row = iota(shape, 0)
    return ((picked_expert(per, row) == iota(shape, 1)) & (row % (2 * per) < per)).astype(BF16)


def first_half(per, shape):
    return iota(shape, 1) % (2 * per) < per


def front_kernel(per, tokens_hbm, router_hbm, cotangent_hbm, weight_hbm, *refs):
    rows, disp, comb, tokens, cotangent, weight, router_t, sems = refs
    copies = [
        pltpu.make_async_copy(source, target, sems.at[index])
        for index, (source, target) in enumerate(
            (
                (router_hbm, router_t),
                (tokens_hbm, tokens),
                (cotangent_hbm, cotangent),
                (weight_hbm.at[0], weight),
            )
        )
    ]
    for copy in copies:
        copy.start()
    matrix = spread(per, router_t.shape[0])
    copies[0].wait()
    paired_router = dot(matrix, router_t[...]).astype(BF16)
    copies[1].wait()
    logits = dot(tokens[...], paired_router, 1, 1)
    first = first_half(per, logits.shape)
    down = jnp.exp(logits - jnp.max(logits, axis=0, keepdims=True))
    disp_prob = down / jnp.sum(down, axis=0, keepdims=True)
    across = jnp.exp(logits - jnp.max(logits, axis=1, keepdims=True))
    comb_prob = across / jnp.sum(jnp.where(first, across, 0.0), axis=1, keepdims=True)
    disp[...] = disp_prob
    comb[...] = comb_prob
    disp_cols = jnp.where(first, disp_prob, 0.0).astype(BF16)
    comb_cols = jnp.where(first, 0.0, comb_prob).astype(BF16)
    copies[2].wait()
    total = dot(disp_cols, tokens[...], 0, 0) + dot(comb_cols, cotangent[...], 0, 0)
    wide = 2 * per
    chips = router_t.shape[0] // per
    shape = (chips * wide, chips * wide)
    to, start = iota(shape, 0), iota(shape, 1)
    low, _ = digits(chips)
    block = to // wide
    chip = chip_of(block // low, block % low, lax.axis_index("dp"), chips)
    matrix = (start == chip * wide + to % wide).astype(BF16)
    rows[...] = dot(matrix, total.astype(BF16)).astype(BF16)
    copies[3].wait()


def front(per, tokens, router_t, cotangent, weight):
    seq, width = tokens.shape
    experts = router_t.shape[0]
    return call(
        functools.partial(front_kernel, per),
        "front",
        (
            pltpu.VMEM((2 * experts, width), BF16),
            pltpu.VMEM((seq, 2 * experts), F32),
            pltpu.VMEM((seq, 2 * experts), F32),
            pltpu.VMEM(tokens.shape, BF16),
            pltpu.VMEM(cotangent.shape, BF16),
            pltpu.VMEM(weight.shape[1:], BF16),
        ),
        8,
        12 * seq * width * experts,
        6 * seq * width,
        in_specs=[pl.BlockSpec(memory_space=pltpu.HBM)] * 4,
        scratch_shapes=[pltpu.VMEM(router_t.shape, BF16), pltpu.SemaphoreType.DMA((4,))],
    )(in_hbm(tokens), in_hbm(router_t), in_hbm(cotangent), in_hbm(weight))


def digits(chips):
    low = 1 << ((chips.bit_length() - 1) // 2)
    return low, chips // low


def chip_of(first, second, core, chips):
    low, high = digits(chips)
    usual = first * low + second
    return usual + (core % 2 if low == high else 0) * (second * low + first - usual)


def exchange_digit(rows, step):
    groups, chips = lax.axis_size("dp"), lax.axis_size("expert")
    low, high = digits(chips)
    size, others = (low, high) if step else (high, low)
    among = [
        [
            core * chips + (chip_of(other, k, core, chips) if step else chip_of(k, other, core, chips))
            for k in range(size)
        ]
        for core in range(groups)
        for other in range(others)
    ]
    blocks = rows.reshape(size, rows.shape[0] // size, rows.shape[1])
    blocks = lax.all_to_all(
        blocks, ("dp", "expert"), split_axis=0, concat_axis=0, axis_index_groups=among, tiled=True
    )
    return blocks.reshape(rows.shape)


def regroup_kernel(inner, wide, rows, out):
    outer = rows.shape[0] // (inner * wide)
    blocks = rows[...].astype(F32).reshape(outer, inner, wide, rows.shape[1])
    order = [blocks[i, j] for j in range(inner) for i in range(outer)]
    out[...] = jnp.concatenate(order).astype(BF16)


def regroup(rows, inner, wide):
    return call(
        functools.partial(regroup_kernel, inner, wide),
        "regroup",
        pltpu.VMEM(rows.shape, BF16),
        4,
        0,
        4 * rows.size,
    )(rows)


def shifted(value, axis, by):
    size = lax.axis_size(axis)
    return lax.ppermute(value, axis, [(i, (i + by) % size) for i in range(size)])


def exchange(blocks, axis, sign):
    return [blocks[0]] + [shifted(block, axis, sign * k) for k, block in enumerate(blocks) if k]


def unsort_matrix(images, wide):
    shape = (images * wide, images * wide)
    to, start = iota(shape, 0), iota(shape, 1)
    return (start == to % wide * images + to // wide).astype(BF16)


def add_kernel(images, count, *refs):
    pieces, out = refs[:count], refs[-1]
    total = [piece[...].astype(F32) for piece in pieces]
    while len(total) > 1:
        total = [sum(total[index : index + 2]) for index in range(0, len(total), 2)]
    total = total[0].astype(BF16)
    if images:
        total = dot(unsort_matrix(images, total.shape[0] // images), total).astype(BF16)
    out[...] = total


def add(pieces, name, images=0, after=()):
    size = pieces[0].size
    return call(
        functools.partial(add_kernel, images, len(pieces)),
        name,
        pltpu.VMEM(pieces[0].shape, BF16),
        4,
        len(pieces) * size,
        4 * size,
        in_specs=[pl.BlockSpec(memory_space=pltpu.VMEM)] * len(pieces)
        + [pl.BlockSpec(memory_space=pltpu.HBM)] * len(after),
    )(*pieces, *map(in_hbm, after))


def fetch_kernel(rows, source, target, sems):
    height = target.shape[0] // sems.shape[0]
    copies = [
        pltpu.make_async_copy(
            source.at[0, pl.ds(part * height, height)],
            target.at[pl.ds(part * height, height)],
            sems.at[part],
        )
        for part in range(sems.shape[0])
    ]
    for copy in copies:
        copy.start()
    for copy in copies:
        copy.wait()


def fetch(after, weight):
    return call(
        fetch_kernel,
        "fetch_first",
        pltpu.VMEM(weight.shape[1:], BF16),
        2,
        0,
        4 * weight[0].size,
        in_specs=[pl.BlockSpec(memory_space=pl.ANY), pl.BlockSpec(memory_space=pltpu.HBM)],
        scratch_shapes=[pltpu.SemaphoreType.DMA((2,))],
    )(after, in_hbm(weight))


def experts_kernel(per, groups, *refs):
    rows, refs = refs[:groups], refs[groups:]
    resident, weights_hbm, refs = refs[:2], refs[2:4], refs[4:]
    back_rows, refs = refs[:groups], refs[groups:]
    slots_out, grads_out, hidden_out, pre_out, w_first, w_second, sems = refs
    wide = 2 * per
    size = rows[0].shape[0] // wide
    span = lambda j: slice(j * size, (j + 1) * size)
    def copy(k, index):
        target = (w_first, w_second)[index]
        return pltpu.make_async_copy(weights_hbm[index].at[k], target.at[k], sems.at[index, k])

    copies = [None] + [(copy(k, 0), copy(k, 1)) for k in range(1, per)]

    def start(k):
        for one in copies[k] if k < per else ():
            one.start()

    start(1)
    shape = (size * wide, size * wide)
    to, origin = iota(shape, 0), iota(shape, 1)
    low, high = digits(size)
    block = origin // wide
    for part in range(groups):
        core = lax.rem(lax.axis_index("dp") - part + groups, groups)
        chip = chip_of(block % high, block // high, core, size)
        matrix = (to == origin % wide * size + chip).astype(BF16)
        moved = dot(matrix, rows[part][...]).astype(BF16)
        for k in range(per):
            slots_out[k, span(part), :] = moved[span(k), :]
            grads_out[k, span(part), :] = moved[span(per + k), :]
    for k in range(per):
        for one in copies[k] if k else ():
            one.wait()
        start(k + 2)
        first, second = (w_first.at[k], w_second.at[k]) if k else resident
        pre_act = dot(slots_out[k], first[...])
        grad_hidden = dot(grads_out[k], second[...], 1, 1)
        phi = 0.5 * (1.0 + lax.erf(pre_act * math.sqrt(0.5)))
        density = jnp.exp(pre_act * pre_act * -0.5) * (1.0 / math.sqrt(2.0 * math.pi))
        hidden = (pre_act * phi).astype(BF16)
        hidden_out[k] = hidden
        out = dot(hidden, second[...]).astype(BF16)
        grad_pre = ((phi + pre_act * density) * grad_hidden).astype(BF16)
        pre_out[k] = grad_pre
        grad_slot = dot(grad_pre, first[...], 1, 1).astype(BF16)
        for part, target in enumerate(back_rows):
            target[span(k), :] = out[span(part), :]
            target[span(per + k), :] = grad_slot[span(part), :]


def run_experts(rows, weights, w_first, w_second):
    per, width, units = w_first.shape
    groups = len(rows)
    total = rows[0].shape[0]
    images = groups * total // (2 * per)
    results = call(
        functools.partial(experts_kernel, per, groups),
        "experts",
        [pltpu.VMEM((total, width), BF16)] * groups
        + [pltpu.VMEM((per, images, width), BF16)] * 2
        + [pltpu.VMEM((per, images, units), BF16)] * 2,
        32,
        8 * per * images * width * units,
        4 * per * width * units,
        in_specs=[pl.BlockSpec(memory_space=pltpu.VMEM)] * (groups + 2)
        + [pl.BlockSpec(memory_space=pltpu.HBM)] * 2,
        scratch_shapes=[
            pltpu.VMEM(w_first.shape, BF16),
            pltpu.VMEM(w_second.shape, BF16),
            pltpu.SemaphoreType.DMA((2, per)),
        ],
    )(*rows, *weights, in_hbm(w_first), in_hbm(w_second))
    return results[:groups], results[groups:]


def outer_kernel(left, right, *refs):
    refs[-1][0] = dot(left[0], right[0], 0, 0).astype(BF16)


def outer(left, right, after, name, part, into=None):
    per, images, height = left.shape
    units = right.shape[2]
    begin, end = part
    per_expert = lambda a, b: pl.BlockSpec((1, a, b), lambda k: (k + begin, 0, 0))
    more = () if into is None else (in_hbm(into),)
    return call(
        outer_kernel,
        name,
        jax.ShapeDtypeStruct((per, height, units), BF16),
        16,
        2 * (end - begin) * images * height * units,
        2 * (end - begin) * height * units,
        grid=(end - begin,),
        in_specs=[
            per_expert(images, height),
            per_expert(images, units),
            pl.BlockSpec(memory_space=pl.ANY),
        ]
        + [pl.BlockSpec(memory_space=pltpu.HBM)] * len(more),
        out_specs=per_expert(height, units),
        input_output_aliases={3: 0} if more else {},
    )(left, right, after, *more)


def logits_kernel(per, groups, tokens, cotangent, disp, comb, outs, after1, after2, *refs):
    *parts, grad_logits, terms = refs
    rows = outs[...]
    disp_prob = disp[...]
    comb_prob = comb[...]
    first = first_half(per, disp_prob.shape)
    grad_comb = dot(cotangent[...], rows, 1, 1)
    grad_disp = dot(tokens[...], rows, 1, 1)
    part_disp = disp_prob * (
        grad_disp - jnp.sum(disp_prob * grad_disp, axis=0, keepdims=True)
    )
    comb_sum = jnp.sum(jnp.where(first, comb_prob * grad_comb, 0.0), axis=1, keepdims=True)
    part_comb = comb_prob * (grad_comb - comb_sum)
    both = jnp.where(first, part_comb, part_disp)
    cols = both.shape[1]
    other = jnp.where(first, pltpu.roll(both, cols - per, 1), pltpu.roll(both, per, 1))
    paired = (both + other).astype(BF16)
    grad_logits[...] = jnp.where(first, paired.astype(F32), 0.0).astype(BF16)
    one_each = dot(paired, pick_first(per, cols // 2)).astype(BF16)
    term = dot(one_each, tokens[...], 0, 0)
    height = terms.shape[1]
    for part in range(groups):
        terms[part] = term[part * height : (part + 1) * height, :].astype(BF16)
    me = lax.axis_index("dp")
    for part, out in enumerate(parts):
        out[...] = terms[lax.rem(me + part, groups)]


def finish_logits(per, groups, tokens, cotangent, disp, comb, outs, after1, after2):
    seq, width = tokens.shape
    cols = disp.shape[1]
    height = cols // 2 // groups
    results = call(
        functools.partial(logits_kernel, per, groups),
        "grad_logits",
        [pltpu.VMEM((height, width), BF16)] * groups + [pltpu.VMEM((seq, cols), BF16)],
        8,
        6 * seq * width * cols,
        6 * seq * width,
        in_specs=[pl.BlockSpec(memory_space=pltpu.VMEM)] * 5
        + [pl.BlockSpec(memory_space=pltpu.HBM)] * 2,
        scratch_shapes=[pltpu.VMEM((groups, height, width), BF16)],
    )(tokens, cotangent, disp, comb, outs, in_hbm(after1), in_hbm(after2))
    return results[:groups], results[groups]


def mixed_kernel(per, outs, comb, mixed):
    first = first_half(per, comb.shape)
    mixed[...] = dot(jnp.where(first, comb[...], 0.0).astype(BF16), outs[...]).astype(BF16)


def finish_mixed(per, outs, comb):
    seq, cols = comb.shape
    width = outs.shape[1]
    return call(
        functools.partial(mixed_kernel, per),
        "mixed",
        jax.ShapeDtypeStruct((seq, width), BF16),
        8,
        2 * seq * width * cols,
        2 * seq * width,
    )(outs, comb)


def tokens_kernel(per, outs, disp, grad_logits, router_t, after, grad_tokens):
    first = first_half(per, disp.shape)
    disp_cols = jnp.where(first, 0.0, disp[...]).astype(BF16)
    paired_router = dot(spread(per, router_t.shape[0]), router_t[...]).astype(BF16)
    grad_tokens[...] = (
        dot(disp_cols, outs[...]) + dot(grad_logits[...], paired_router)
    ).astype(BF16)


def finish_tokens(per, outs, disp, grad_logits, router_t, after):
    seq, cols = disp.shape
    width = outs.shape[1]
    return call(
        functools.partial(tokens_kernel, per),
        "grad_tokens",
        jax.ShapeDtypeStruct((seq, width), BF16),
        8,
        4 * seq * width * cols,
        2 * seq * width,
        in_specs=[pl.BlockSpec(memory_space=pltpu.VMEM)] * 4 + [pl.BlockSpec(memory_space=pl.ANY)],
    )(outs, disp, grad_logits, router_t, after)


def join_kernel(*refs):
    *parts, out = refs
    groups = len(parts)
    me = lax.axis_index("dp")
    for part, ref in enumerate(parts):
        out[lax.rem(me - part + groups, groups)] = ref[...].astype(F32)


def join(parts):
    height, width = parts[0].shape
    return call(
        join_kernel,
        "join",
        jax.ShapeDtypeStruct((len(parts), height, width), F32),
        4,
        0,
        6 * height * width,
    )(*parts).reshape(-1, width)


def across_chips(value, masks):
    groups, chips = lax.axis_size("dp"), lax.axis_size("expert")
    pairs = [
        (core * chips + i, core * chips + (i ^ masks[core]))
        for core in range(groups)
        for i in range(chips)
    ]
    return lax.ppermute(value, ("dp", "expert"), pairs)


def total_over_devices(parts, first_beside, beside):
    value = add(exchange(parts, "dp", 1), "add_cores", after=[first_beside])
    groups, chips = lax.axis_size("dp"), lax.axis_size("expert")
    rounds = []
    bit = 1
    while bit < chips:
        rounds.append([bit, 2 * bit, 3 * bit] if 4 * bit <= chips else [bit])
        bit *= 4
    even = len(rounds[-1]) == 3
    for step in range(len(rounds)):
        of_core = [rounds[(step + even * core) % len(rounds)] for core in range(groups)]
        others = [across_chips(value, masks) for masks in zip(*of_core)]
        after = [beside.pop(0)(value)] if beside else []
        value = add([value, *others], "add_chips", after=after)
    return value, join(exchange([value] * len(parts), "dp", 1))


def local(tokens, router, weight_in, weight_out, cotangent):
    per = weight_in.shape[0]
    experts = router.shape[1]
    chips = experts // per
    groups = lax.axis_size("dp")
    tokens, cotangent = tokens[0], cotangent[0]
    width = tokens.shape[1]
    router_t = router.T

    def to_chips(rows):
        blocks = rows.reshape(chips, 2 * per, width)
        blocks = lax.all_to_all(blocks, "expert", split_axis=0, concat_axis=0, tiled=True)
        return blocks.reshape(rows.shape)

    rows, disp, comb, tokens, cotangent, second_weight = front(
        per, tokens, router_t, cotangent, weight_out
    )
    low, _ = digits(chips)
    rows = regroup(exchange_digit(rows, 0), low, 2 * per)
    rows = exchange_digit(rows, 1)
    first_weight = fetch(rows, weight_in)
    rows = exchange([rows] * groups, "dp", 1)
    back_rows, (slots, grads, hidden, grad_pre) = run_experts(
        rows, (first_weight, second_weight), weight_in, weight_out
    )
    back_rows = add(exchange(back_rows, "dp", -1), "add_groups", chips)
    outs = to_chips(back_rows)
    grad_second = outer(hidden, grads, back_rows, "grad_weight_out", (0, per))
    grad_first = outer(slots, grad_pre, back_rows, "grad_weight_in", (0, 1))
    parts, grad_logits = finish_logits(
        per, groups, tokens, cotangent, disp, comb, outs, grad_first, grad_second
    )
    mixed = finish_mixed(per, outs, comb)

    def piece(part, value):
        nonlocal grad_first
        grad_first = outer(slots, grad_pre, value, "grad_weight_in", part, grad_first)
        return grad_first

    cut = (per + 2) // 2
    beside = [functools.partial(piece, part) for part in ((1, cut), (cut, per))]
    value, total = total_over_devices(parts, mixed, beside)
    grad_tokens = finish_tokens(per, outs, disp, grad_logits, router_t, value)
    grad_router = total.T
    return (mixed[None], grad_tokens[None], grad_router, grad_first, grad_second)


def solution(mesh):
    return jax.shard_map(
        local,
        mesh=mesh,
        in_specs=(
            P(("dp", "expert"), None, None),
            P(),
            P("expert", None, "dp"),
            P("expert", "dp", None),
            P(("dp", "expert"), None, None),
        ),
        out_specs=(
            P(("dp", "expert"), None, None),
            P(("dp", "expert"), None, None),
            P(),
            P("expert", None, "dp"),
            P("expert", "dp", None),
        ),
        check_vma=False,
    )
```

```python
import functools
import math

import jax
import jax.numpy as jnp
from jax import lax
from jax.experimental import pallas as pl
from jax.experimental.pallas import tpu as pltpu
from jax.sharding import PartitionSpec as P

F32 = jnp.float32
BF16 = jnp.bfloat16
MIB = 1024 * 1024


def dot(left, right, left_dim=1, right_dim=0):
    return lax.dot_general(
        left, right, (((left_dim,), (right_dim,)), ((), ())), preferred_element_type=F32
    )


def iota(shape, dim):
    return lax.broadcasted_iota(jnp.int32, shape, dim)


def in_hbm(value):
    return pltpu.with_memory_space_constraint(value, pltpu.HBM)


def call(kernel, name, out_shape, limit, flops, moved, **more):
    return pl.pallas_call(
        kernel,
        out_shape=out_shape,
        compiler_params=pltpu.CompilerParams(vmem_limit_bytes=limit * MIB),
        cost_estimate=pl.CostEstimate(flops=flops, bytes_accessed=moved, transcendentals=0),
        name=name,
        **more,
    )


def picked_expert(per, rows):
    return (rows // (2 * per)) * per + rows % per


def spread(per, experts):
    shape = (2 * experts, experts)
    return (picked_expert(per, iota(shape, 0)) == iota(shape, 1)).astype(BF16)


def pick_first(per, experts):
    shape = (2 * experts, experts)
    row = iota(shape, 0)
    return ((picked_expert(per, row) == iota(shape, 1)) & (row % (2 * per) < per)).astype(BF16)


def first_half(per, shape):
    return iota(shape, 1) % (2 * per) < per


def front_kernel(per, tokens_hbm, router_hbm, cotangent_hbm, weight_hbm, *refs):
    rows, disp, comb, tokens, cotangent, weight, router_t, sems = refs
    copies = [
        pltpu.make_async_copy(source, target, sems.at[index])
        for index, (source, target) in enumerate(
            (
                (router_hbm, router_t),
                (tokens_hbm, tokens),
                (cotangent_hbm, cotangent),
                (weight_hbm.at[0], weight),
            )
        )
    ]
    for copy in copies:
        copy.start()
    matrix = spread(per, router_t.shape[0])
    copies[0].wait()
    paired_router = dot(matrix, router_t[...]).astype(BF16)
    copies[1].wait()
    logits = dot(tokens[...], paired_router, 1, 1)
    first = first_half(per, logits.shape)
    down = jnp.exp(logits - jnp.max(logits, axis=0, keepdims=True))
    disp_prob = down / jnp.sum(down, axis=0, keepdims=True)
    across = jnp.exp(logits - jnp.max(logits, axis=1, keepdims=True))
    comb_prob = across / jnp.sum(jnp.where(first, across, 0.0), axis=1, keepdims=True)
    disp[...] = disp_prob
    comb[...] = comb_prob
    disp_cols = jnp.where(first, disp_prob, 0.0).astype(BF16)
    comb_cols = jnp.where(first, 0.0, comb_prob).astype(BF16)
    copies[2].wait()
    rows[...] = (
        dot(disp_cols, tokens[...], 0, 0) + dot(comb_cols, cotangent[...], 0, 0)
    ).astype(BF16)
    copies[3].wait()


def front(per, tokens, router_t, cotangent, weight):
    seq, width = tokens.shape
    experts = router_t.shape[0]
    return call(
        functools.partial(front_kernel, per),
        "front",
        (
            pltpu.VMEM((2 * experts, width), BF16),
            pltpu.VMEM((seq, 2 * experts), F32),
            pltpu.VMEM((seq, 2 * experts), F32),
            pltpu.VMEM(tokens.shape, BF16),
            pltpu.VMEM(cotangent.shape, BF16),
            pltpu.VMEM(weight.shape[1:], BF16),
        ),
        8,
        12 * seq * width * experts,
        6 * seq * width,
        in_specs=[pl.BlockSpec(memory_space=pltpu.HBM)] * 4,
        scratch_shapes=[pltpu.VMEM(router_t.shape, BF16), pltpu.SemaphoreType.DMA((4,))],
    )(in_hbm(tokens), in_hbm(router_t), in_hbm(cotangent), in_hbm(weight))


def digits(chips):
    low = 1 << ((chips.bit_length() - 1) // 2)
    return low, chips // low


def chip_of(first, second, core, chips):
    low, high = digits(chips)
    if core % 2 and low == high:
        first, second = second, first
    return first * low + second


def exchange_digit(blocks, digit):
    groups, chips = lax.axis_size("dp"), lax.axis_size("expert")
    low, high = digits(chips)
    size, others = (low, high) if digit else (high, low)
    among = [
        [
            core * chips + (chip_of(other, k, core, chips) if digit else chip_of(k, other, core, chips))
            for k in range(size)
        ]
        for core in range(groups)
        for other in range(others)
    ]
    return lax.all_to_all(
        blocks, ("dp", "expert"), split_axis=0, concat_axis=0, axis_index_groups=among, tiled=True
    )


def sum_kernel(parts, out):
    total = jnp.sum(parts[...].astype(F32), axis=0, keepdims=True)
    out[...] = jnp.broadcast_to(total, out.shape).astype(BF16)


def sum_blocks(parts, copies):
    return call(
        sum_kernel,
        "sum_blocks",
        pltpu.VMEM((copies, *parts.shape[1:]), BF16),
        4,
        parts.size,
        4 * parts.size,
    )(parts)


def shifted(value, axis, by):
    size = lax.axis_size(axis)
    return lax.ppermute(value, axis, [(i, (i + by) % size) for i in range(size)])


def exchange(blocks, axis, sign):
    return [blocks[0]] + [shifted(block, axis, sign * k) for k, block in enumerate(blocks) if k]


def sort_matrix(images, wide, transposed):
    shape = (images * wide, images * wide)
    to, start = (iota(shape, 1), iota(shape, 0)) if transposed else (iota(shape, 0), iota(shape, 1))
    return ((to % images) * wide + to // images == start).astype(BF16)


def add_kernel(images, count, *refs):
    pieces, out = refs[:count], refs[-1]
    total = [piece[...].astype(F32) for piece in pieces]
    while len(total) > 1:
        total = [sum(total[index : index + 2]) for index in range(0, len(total), 2)]
    total = total[0].astype(BF16)
    if images:
        total = dot(sort_matrix(images, total.shape[0] // images, True), total).astype(BF16)
    out[...] = total


def add(pieces, name, images=0, after=()):
    size = pieces[0].size
    return call(
        functools.partial(add_kernel, images, len(pieces)),
        name,
        pltpu.VMEM(pieces[0].shape, BF16),
        4,
        len(pieces) * size,
        4 * size,
        in_specs=[pl.BlockSpec(memory_space=pltpu.VMEM)] * len(pieces)
        + [pl.BlockSpec(memory_space=pltpu.HBM)] * len(after),
    )(*pieces, *map(in_hbm, after))


def fetch_kernel(rows, source, target, sems):
    height = target.shape[0] // sems.shape[0]
    copies = [
        pltpu.make_async_copy(
            source.at[0, pl.ds(part * height, height)],
            target.at[pl.ds(part * height, height)],
            sems.at[part],
        )
        for part in range(sems.shape[0])
    ]
    for copy in copies:
        copy.start()
    for copy in copies:
        copy.wait()


def fetch(after, weight):
    return call(
        fetch_kernel,
        "fetch_first",
        pltpu.VMEM(weight.shape[1:], BF16),
        2,
        0,
        4 * weight[0].size,
        in_specs=[pl.BlockSpec(memory_space=pl.ANY), pl.BlockSpec(memory_space=pltpu.HBM)],
        scratch_shapes=[pltpu.SemaphoreType.DMA((2,))],
    )(after, in_hbm(weight))


def experts_kernel(per, groups, *refs):
    rows, refs = refs[:groups], refs[groups:]
    resident, weights_hbm, refs = refs[:2], refs[2:4], refs[4:]
    back_rows, refs = refs[:groups], refs[groups:]
    slots_out, grads_out, hidden_out, pre_out, w_first, w_second, sems = refs
    wide = 2 * per
    size = rows[0].shape[0] // wide
    span = lambda j: slice(j * size, (j + 1) * size)
    def copy(k, index):
        target = (w_first, w_second)[index]
        return pltpu.make_async_copy(weights_hbm[index].at[k], target.at[k], sems.at[index, k])

    copies = [None] + [(copy(k, 0), copy(k, 1)) for k in range(1, per)]

    def start(k):
        for one in copies[k] if k < per else ():
            one.start()

    start(1)
    matrix = sort_matrix(size, wide, False)
    for part in range(groups):
        moved = dot(matrix, rows[part][...]).astype(BF16)
        for k in range(per):
            slots_out[k, span(part), :] = moved[span(k), :]
            grads_out[k, span(part), :] = moved[span(per + k), :]
    for k in range(per):
        for one in copies[k] if k else ():
            one.wait()
        start(k + 2)
        first, second = (w_first.at[k], w_second.at[k]) if k else resident
        pre_act = dot(slots_out[k], first[...])
        grad_hidden = dot(grads_out[k], second[...], 1, 1)
        phi = 0.5 * (1.0 + lax.erf(pre_act * math.sqrt(0.5)))
        density = jnp.exp(pre_act * pre_act * -0.5) * (1.0 / math.sqrt(2.0 * math.pi))
        hidden = (pre_act * phi).astype(BF16)
        hidden_out[k] = hidden
        out = dot(hidden, second[...]).astype(BF16)
        grad_pre = ((phi + pre_act * density) * grad_hidden).astype(BF16)
        pre_out[k] = grad_pre
        grad_slot = dot(grad_pre, first[...], 1, 1).astype(BF16)
        for part, target in enumerate(back_rows):
            target[span(k), :] = out[span(part), :]
            target[span(per + k), :] = grad_slot[span(part), :]


def run_experts(rows, weights, w_first, w_second):
    per, width, units = w_first.shape
    groups = len(rows)
    total = rows[0].shape[0]
    images = groups * total // (2 * per)
    results = call(
        functools.partial(experts_kernel, per, groups),
        "experts",
        [pltpu.VMEM((total, width), BF16)] * groups
        + [pltpu.VMEM((per, images, width), BF16)] * 2
        + [pltpu.VMEM((per, images, units), BF16)] * 2,
        32,
        8 * per * images * width * units,
        4 * per * width * units,
        in_specs=[pl.BlockSpec(memory_space=pltpu.VMEM)] * (groups + 2)
        + [pl.BlockSpec(memory_space=pltpu.HBM)] * 2,
        scratch_shapes=[
            pltpu.VMEM(w_first.shape, BF16),
            pltpu.VMEM(w_second.shape, BF16),
            pltpu.SemaphoreType.DMA((2, per)),
        ],
    )(*rows, *weights, in_hbm(w_first), in_hbm(w_second))
    return results[:groups], results[groups:]


def outer_kernel(slots, grad_pre, hidden, grads, after, grad_first, grad_second):
    for left, right, out in ((slots, grad_pre, grad_first), (hidden, grads, grad_second)):
        height = out.shape[1]
        piece = math.gcd(height, 128)
        for top in range(0, height, piece):
            rows = slice(top, top + piece)
            out[0, rows, :] = dot(left[0, :, rows], right[0], 0, 0).astype(BF16)


def weight_grads(slots, grads, hidden, grad_pre, after):
    per, images, width = slots.shape
    units = hidden.shape[2]
    parts = 2 if units % 256 == 0 and width % 256 == 0 else 1
    lefts = lambda size: pl.BlockSpec((1, images, size // parts), lambda k, part: (k, 0, part))
    rights = lambda size: pl.BlockSpec((1, images, size), lambda k, part: (k, 0, 0))
    results = lambda a, b: pl.BlockSpec((1, a // parts, b), lambda k, part: (k, part, 0))
    return call(
        outer_kernel,
        "weight_grads",
        (
            jax.ShapeDtypeStruct((per, width, units), BF16),
            jax.ShapeDtypeStruct((per, units, width), BF16),
        ),
        16,
        4 * per * images * width * units,
        4 * per * width * units,
        grid=(per, parts),
        in_specs=[
            lefts(width),
            rights(units),
            lefts(units),
            rights(width),
            pl.BlockSpec(memory_space=pl.ANY),
        ],
        out_specs=[results(width, units), results(units, width)],
    )(slots, grad_pre, hidden, grads, after)


def logits_kernel(per, groups, tokens, cotangent, disp, comb, outs, after1, after2, *refs):
    *parts, grad_logits, terms = refs
    rows = outs[...]
    disp_prob = disp[...]
    comb_prob = comb[...]
    first = first_half(per, disp_prob.shape)
    grad_comb = dot(cotangent[...], rows, 1, 1)
    grad_disp = dot(tokens[...], rows, 1, 1)
    part_disp = disp_prob * (
        grad_disp - jnp.sum(disp_prob * grad_disp, axis=0, keepdims=True)
    )
    comb_sum = jnp.sum(jnp.where(first, comb_prob * grad_comb, 0.0), axis=1, keepdims=True)
    part_comb = comb_prob * (grad_comb - comb_sum)
    both = jnp.where(first, part_comb, part_disp)
    cols = both.shape[1]
    other = jnp.where(first, pltpu.roll(both, cols - per, 1), pltpu.roll(both, per, 1))
    paired = (both + other).astype(BF16)
    one_each = dot(paired, pick_first(per, cols // 2)).astype(BF16)
    grad_logits[...] = one_each
    term = dot(one_each, tokens[...], 0, 0)
    height = terms.shape[1]
    for part in range(groups):
        terms[part] = term[part * height : (part + 1) * height, :].astype(BF16)
    me = lax.axis_index("dp")
    for part, out in enumerate(parts):
        out[...] = terms[lax.rem(me + part, groups)]


def finish_logits(per, groups, tokens, cotangent, disp, comb, outs, after1, after2):
    seq, width = tokens.shape
    cols = disp.shape[1]
    height = cols // 2 // groups
    results = call(
        functools.partial(logits_kernel, per, groups),
        "grad_logits",
        [pltpu.VMEM((height, width), BF16)] * groups + [pltpu.VMEM((seq, cols // 2), BF16)],
        8,
        6 * seq * width * cols,
        6 * seq * width,
        in_specs=[pl.BlockSpec(memory_space=pltpu.VMEM)] * 5
        + [pl.BlockSpec(memory_space=pltpu.HBM)] * 2,
        scratch_shapes=[pltpu.VMEM((groups, height, width), BF16)],
    )(tokens, cotangent, disp, comb, outs, in_hbm(after1), in_hbm(after2))
    return results[:groups], results[groups]


def mixed_kernel(per, outs, comb, mixed):
    first = first_half(per, comb.shape)
    mixed[...] = dot(jnp.where(first, comb[...], 0.0).astype(BF16), outs[...]).astype(BF16)


def finish_mixed(per, outs, comb):
    seq, cols = comb.shape
    width = outs.shape[1]
    return call(
        functools.partial(mixed_kernel, per),
        "mixed",
        jax.ShapeDtypeStruct((seq, width), BF16),
        8,
        2 * seq * width * cols,
        2 * seq * width,
    )(outs, comb)


def tokens_kernel(per, outs, disp, grad_logits, router_t, after, grad_tokens):
    first = first_half(per, disp.shape)
    disp_cols = jnp.where(first, 0.0, disp[...]).astype(BF16)
    grad_tokens[...] = (
        dot(disp_cols, outs[...]) + dot(grad_logits[...], router_t[...])
    ).astype(BF16)


def finish_tokens(per, outs, disp, grad_logits, router_t, after):
    seq, cols = disp.shape
    width = outs.shape[1]
    return call(
        functools.partial(tokens_kernel, per),
        "grad_tokens",
        jax.ShapeDtypeStruct((seq, width), BF16),
        8,
        4 * seq * width * cols,
        2 * seq * width,
        in_specs=[pl.BlockSpec(memory_space=pltpu.VMEM)] * 4 + [pl.BlockSpec(memory_space=pl.ANY)],
    )(outs, disp, grad_logits, router_t, after)


def join_kernel(*refs):
    *parts, out = refs
    groups = len(parts)
    me = lax.axis_index("dp")
    for part, ref in enumerate(parts):
        out[lax.rem(me - part + groups, groups)] = ref[...].astype(F32)


def join(parts):
    height, width = parts[0].shape
    return call(
        join_kernel,
        "join",
        jax.ShapeDtypeStruct((len(parts), height, width), F32),
        4,
        0,
        6 * height * width,
    )(*parts).reshape(-1, width)


def total_over_devices(parts, beside):
    value = add(exchange(parts, "dp", 1), "add_cores", after=[beside])
    low, high = digits(lax.axis_size("expert"))
    height, width = value.shape
    shares = exchange_digit(value.reshape(low, height // low, width), 1)
    shares = exchange_digit(sum_blocks(shares, high), 0)
    value = exchange_digit(sum_blocks(shares, low), 1).reshape(height, width)
    return value, join(exchange([value] * len(parts), "dp", 1))


def local(tokens, router, weight_in, weight_out, cotangent):
    per = weight_in.shape[0]
    experts = router.shape[1]
    chips = experts // per
    groups = lax.axis_size("dp")
    tokens, cotangent = tokens[0], cotangent[0]
    width = tokens.shape[1]
    router_t = router.T

    def to_chips(rows):
        blocks = rows.reshape(chips, 2 * per, width)
        blocks = lax.all_to_all(blocks, "expert", split_axis=0, concat_axis=0, tiled=True)
        return blocks.reshape(rows.shape)

    rows, disp, comb, tokens, cotangent, second_weight = front(
        per, tokens, router_t, cotangent, weight_out
    )
    rows = to_chips(rows)
    first_weight = fetch(rows, weight_in)
    rows = exchange([rows] * groups, "dp", 1)
    back_rows, (slots, grads, hidden, grad_pre) = run_experts(
        rows, (first_weight, second_weight), weight_in, weight_out
    )
    back_rows = add(exchange(back_rows, "dp", -1), "add_groups", chips)
    outs = to_chips(back_rows)
    grad_first, grad_second = weight_grads(slots, grads, hidden, grad_pre, back_rows)
    parts, grad_logits = finish_logits(
        per, groups, tokens, cotangent, disp, comb, outs, grad_first, grad_second
    )
    mixed = finish_mixed(per, outs, comb)
    value, total = total_over_devices(parts, mixed)
    grad_tokens = finish_tokens(per, outs, disp, grad_logits, router_t, value)
    grad_router = total.T
    return (mixed[None], grad_tokens[None], grad_router, grad_first, grad_second)


def solution(mesh):
    return jax.shard_map(
        local,
        mesh=mesh,
        in_specs=(
            P(("dp", "expert"), None, None),
            P(),
            P("expert", None, "dp"),
            P("expert", "dp", None),
            P(("dp", "expert"), None, None),
        ),
        out_specs=(
            P(("dp", "expert"), None, None),
            P(("dp", "expert"), None, None),
            P(),
            P("expert", None, "dp"),
            P("expert", "dp", None),
        ),
        check_vma=False,
    )
```

```python
import functools
import math

import jax
import jax.numpy as jnp
from jax import lax
from jax.experimental import pallas as pl
from jax.experimental.pallas import tpu as pltpu
from jax.sharding import PartitionSpec as P

F32 = jnp.float32
BF16 = jnp.bfloat16
MIB = 1024 * 1024


def dot(left, right, left_dim=1, right_dim=0):
    return lax.dot_general(
        left, right, (((left_dim,), (right_dim,)), ((), ())), preferred_element_type=F32
    )


def iota(shape, dim):
    return lax.broadcasted_iota(jnp.int32, shape, dim)


def in_hbm(value):
    return pltpu.with_memory_space_constraint(value, pltpu.HBM)


def call(kernel, name, out_shape, limit, flops, moved, **more):
    return pl.pallas_call(
        kernel,
        out_shape=out_shape,
        compiler_params=pltpu.CompilerParams(vmem_limit_bytes=limit * MIB),
        cost_estimate=pl.CostEstimate(flops=flops, bytes_accessed=moved, transcendentals=0),
        name=name,
        **more,
    )


def picked_expert(per, rows):
    return (rows // (2 * per)) * per + rows % per


def spread(per, experts):
    shape = (2 * experts, experts)
    return (picked_expert(per, iota(shape, 0)) == iota(shape, 1)).astype(BF16)


def pick_first(per, experts):
    shape = (2 * experts, experts)
    row = iota(shape, 0)
    return ((picked_expert(per, row) == iota(shape, 1)) & (row % (2 * per) < per)).astype(BF16)


def first_half(per, shape):
    return iota(shape, 1) % (2 * per) < per


def front_kernel(per, tokens_hbm, router_hbm, cotangent_hbm, weight_hbm, *refs):
    rows, disp, comb, tokens, cotangent, weight, router_t, sems = refs
    copies = [
        pltpu.make_async_copy(source, target, sems.at[index])
        for index, (source, target) in enumerate(
            (
                (router_hbm, router_t),
                (tokens_hbm, tokens),
                (cotangent_hbm, cotangent),
                (weight_hbm.at[0], weight),
            )
        )
    ]
    for copy in copies:
        copy.start()
    matrix = spread(per, router_t.shape[0])
    copies[0].wait()
    paired_router = dot(matrix, router_t[...]).astype(BF16)
    copies[1].wait()
    logits = dot(tokens[...], paired_router, 1, 1)
    first = first_half(per, logits.shape)
    down = jnp.exp(logits - jnp.max(logits, axis=0, keepdims=True))
    disp_prob = down / jnp.sum(down, axis=0, keepdims=True)
    across = jnp.exp(logits - jnp.max(logits, axis=1, keepdims=True))
    comb_prob = across / jnp.sum(jnp.where(first, across, 0.0), axis=1, keepdims=True)
    disp[...] = disp_prob
    comb[...] = comb_prob
    disp_cols = jnp.where(first, disp_prob, 0.0).astype(BF16)
    comb_cols = jnp.where(first, 0.0, comb_prob).astype(BF16)
    copies[2].wait()
    rows[...] = (
        dot(disp_cols, tokens[...], 0, 0) + dot(comb_cols, cotangent[...], 0, 0)
    ).astype(BF16)
    copies[3].wait()


def front(per, tokens, router_t, cotangent, weight):
    seq, width = tokens.shape
    experts = router_t.shape[0]
    return call(
        functools.partial(front_kernel, per),
        "front",
        (
            pltpu.VMEM((2 * experts, width), BF16),
            pltpu.VMEM((seq, 2 * experts), F32),
            pltpu.VMEM((seq, 2 * experts), F32),
            pltpu.VMEM(tokens.shape, BF16),
            pltpu.VMEM(cotangent.shape, BF16),
            pltpu.VMEM(weight.shape[1:], BF16),
        ),
        8,
        12 * seq * width * experts,
        6 * seq * width,
        in_specs=[pl.BlockSpec(memory_space=pltpu.HBM)] * 4,
        scratch_shapes=[pltpu.VMEM(router_t.shape, BF16), pltpu.SemaphoreType.DMA((4,))],
    )(in_hbm(tokens), in_hbm(router_t), in_hbm(cotangent), in_hbm(weight))


def digits(chips):
    low = 1 << ((chips.bit_length() - 1) // 2)
    return low, chips // low


def chip_of(first, second, core, chips):
    low, high = digits(chips)
    if core % 2 and low == high:
        first, second = second, first
    return first * low + second


def across_chips(value, digit):
    groups, chips = lax.axis_size("dp"), lax.axis_size("expert")
    low, high = digits(chips)
    others = []
    for step in range(1, low if digit else high):
        away = [
            chip_of(0, step, core, chips) if digit else chip_of(step, 0, core, chips)
            for core in range(groups)
        ]
        pairs = [
            (core * chips + i, core * chips + (i ^ away[core]))
            for core in range(groups)
            for i in range(chips)
        ]
        others.append(lax.ppermute(value, ("dp", "expert"), pairs))
    return others


def shifted(value, axis, by):
    size = lax.axis_size(axis)
    return lax.ppermute(value, axis, [(i, (i + by) % size) for i in range(size)])


def exchange(blocks, axis, sign):
    return [blocks[0]] + [shifted(block, axis, sign * k) for k, block in enumerate(blocks) if k]


def sort_matrix(images, wide, transposed):
    shape = (images * wide, images * wide)
    to, start = (iota(shape, 1), iota(shape, 0)) if transposed else (iota(shape, 0), iota(shape, 1))
    return ((to % images) * wide + to // images == start).astype(BF16)


def add_kernel(images, count, *refs):
    pieces, out = refs[:count], refs[-1]
    total = [piece[...].astype(F32) for piece in pieces]
    while len(total) > 1:
        total = [sum(total[index : index + 2]) for index in range(0, len(total), 2)]
    total = total[0].astype(BF16)
    if images:
        total = dot(sort_matrix(images, total.shape[0] // images, True), total).astype(BF16)
    out[...] = total


def add(pieces, name, images=0, after=()):
    size = pieces[0].size
    return call(
        functools.partial(add_kernel, images, len(pieces)),
        name,
        pltpu.VMEM(pieces[0].shape, BF16),
        4,
        len(pieces) * size,
        4 * size,
        in_specs=[pl.BlockSpec(memory_space=pltpu.VMEM)] * len(pieces)
        + [pl.BlockSpec(memory_space=pltpu.HBM)] * len(after),
    )(*pieces, *map(in_hbm, after))


def fetch_kernel(rows, source, target, sems):
    height = target.shape[0] // sems.shape[0]
    copies = [
        pltpu.make_async_copy(
            source.at[0, pl.ds(part * height, height)],
            target.at[pl.ds(part * height, height)],
            sems.at[part],
        )
        for part in range(sems.shape[0])
    ]
    for copy in copies:
        copy.start()
    for copy in copies:
        copy.wait()


def fetch(after, weight):
    return call(
        fetch_kernel,
        "fetch_first",
        pltpu.VMEM(weight.shape[1:], BF16),
        2,
        0,
        4 * weight[0].size,
        in_specs=[pl.BlockSpec(memory_space=pl.ANY), pl.BlockSpec(memory_space=pltpu.HBM)],
        scratch_shapes=[pltpu.SemaphoreType.DMA((2,))],
    )(after, in_hbm(weight))


def experts_kernel(per, groups, *refs):
    rows, refs = refs[:groups], refs[groups:]
    resident, weights_hbm, refs = refs[:2], refs[2:4], refs[4:]
    back_rows, refs = refs[:groups], refs[groups:]
    slots_out, grads_out, hidden_out, pre_out, w_first, w_second, sems = refs
    wide = 2 * per
    size = rows[0].shape[0] // wide
    span = lambda j: slice(j * size, (j + 1) * size)
    def copy(k, index):
        target = (w_first, w_second)[index]
        return pltpu.make_async_copy(weights_hbm[index].at[k], target.at[k], sems.at[index, k])

    copies = [None] + [(copy(k, 0), copy(k, 1)) for k in range(1, per)]

    def start(k):
        for one in copies[k] if k < per else ():
            one.start()

    start(1)
    matrix = sort_matrix(size, wide, False)
    for part in range(groups):
        moved = dot(matrix, rows[part][...]).astype(BF16)
        for k in range(per):
            slots_out[k, span(part), :] = moved[span(k), :]
            grads_out[k, span(part), :] = moved[span(per + k), :]
    for k in range(per):
        for one in copies[k] if k else ():
            one.wait()
        start(k + 2)
        first, second = (w_first.at[k], w_second.at[k]) if k else resident
        pre_act = dot(slots_out[k], first[...])
        grad_hidden = dot(grads_out[k], second[...], 1, 1)
        phi = 0.5 * (1.0 + lax.erf(pre_act * math.sqrt(0.5)))
        density = jnp.exp(pre_act * pre_act * -0.5) * (1.0 / math.sqrt(2.0 * math.pi))
        hidden = (pre_act * phi).astype(BF16)
        hidden_out[k] = hidden
        out = dot(hidden, second[...]).astype(BF16)
        grad_pre = ((phi + pre_act * density) * grad_hidden).astype(BF16)
        pre_out[k] = grad_pre
        grad_slot = dot(grad_pre, first[...], 1, 1).astype(BF16)
        for part, target in enumerate(back_rows):
            target[span(k), :] = out[span(part), :]
            target[span(per + k), :] = grad_slot[span(part), :]


def run_experts(rows, weights, w_first, w_second):
    per, width, units = w_first.shape
    groups = len(rows)
    total = rows[0].shape[0]
    images = groups * total // (2 * per)
    results = call(
        functools.partial(experts_kernel, per, groups),
        "experts",
        [pltpu.VMEM((total, width), BF16)] * groups
        + [pltpu.VMEM((per, images, width), BF16)] * 2
        + [pltpu.VMEM((per, images, units), BF16)] * 2,
        32,
        8 * per * images * width * units,
        4 * per * width * units,
        in_specs=[pl.BlockSpec(memory_space=pltpu.VMEM)] * (groups + 2)
        + [pl.BlockSpec(memory_space=pltpu.HBM)] * 2,
        scratch_shapes=[
            pltpu.VMEM(w_first.shape, BF16),
            pltpu.VMEM(w_second.shape, BF16),
            pltpu.SemaphoreType.DMA((2, per)),
        ],
    )(*rows, *weights, in_hbm(w_first), in_hbm(w_second))
    return results[:groups], results[groups:]


def outer_kernel(slots, grad_pre, hidden, grads, after, grad_first, grad_second):
    for left, right, out in ((slots, grad_pre, grad_first), (hidden, grads, grad_second)):
        height = out.shape[1]
        piece = math.gcd(height, 128)
        for top in range(0, height, piece):
            rows = slice(top, top + piece)
            out[0, rows, :] = dot(left[0, :, rows], right[0], 0, 0).astype(BF16)


def weight_grads(slots, grads, hidden, grad_pre, after):
    per, images, width = slots.shape
    units = hidden.shape[2]
    parts = 2 if units % 256 == 0 and width % 256 == 0 else 1
    lefts = lambda size: pl.BlockSpec((1, images, size // parts), lambda k, part: (k, 0, part))
    rights = lambda size: pl.BlockSpec((1, images, size), lambda k, part: (k, 0, 0))
    results = lambda a, b: pl.BlockSpec((1, a // parts, b), lambda k, part: (k, part, 0))
    return call(
        outer_kernel,
        "weight_grads",
        (
            jax.ShapeDtypeStruct((per, width, units), BF16),
            jax.ShapeDtypeStruct((per, units, width), BF16),
        ),
        16,
        4 * per * images * width * units,
        4 * per * width * units,
        grid=(per, parts),
        in_specs=[
            lefts(width),
            rights(units),
            lefts(units),
            rights(width),
            pl.BlockSpec(memory_space=pl.ANY),
        ],
        out_specs=[results(width, units), results(units, width)],
    )(slots, grad_pre, hidden, grads, after)


def logits_kernel(per, groups, tokens, cotangent, disp, comb, outs, after1, after2, *refs):
    *parts, grad_logits, terms = refs
    rows = outs[...]
    disp_prob = disp[...]
    comb_prob = comb[...]
    first = first_half(per, disp_prob.shape)
    grad_comb = dot(cotangent[...], rows, 1, 1)
    grad_disp = dot(tokens[...], rows, 1, 1)
    part_disp = disp_prob * (
        grad_disp - jnp.sum(disp_prob * grad_disp, axis=0, keepdims=True)
    )
    comb_sum = jnp.sum(jnp.where(first, comb_prob * grad_comb, 0.0), axis=1, keepdims=True)
    part_comb = comb_prob * (grad_comb - comb_sum)
    both = jnp.where(first, part_comb, part_disp)
    cols = both.shape[1]
    other = jnp.where(first, pltpu.roll(both, cols - per, 1), pltpu.roll(both, per, 1))
    paired = (both + other).astype(BF16)
    one_each = dot(paired, pick_first(per, cols // 2)).astype(BF16)
    grad_logits[...] = one_each
    term = dot(one_each, tokens[...], 0, 0)
    height = terms.shape[1]
    for part in range(groups):
        terms[part] = term[part * height : (part + 1) * height, :].astype(BF16)
    me = lax.axis_index("dp")
    for part, out in enumerate(parts):
        out[...] = terms[lax.rem(me + part, groups)]


def finish_logits(per, groups, tokens, cotangent, disp, comb, outs, after1, after2):
    seq, width = tokens.shape
    cols = disp.shape[1]
    height = cols // 2 // groups
    results = call(
        functools.partial(logits_kernel, per, groups),
        "grad_logits",
        [pltpu.VMEM((height, width), BF16)] * groups + [pltpu.VMEM((seq, cols // 2), BF16)],
        8,
        6 * seq * width * cols,
        6 * seq * width,
        in_specs=[pl.BlockSpec(memory_space=pltpu.VMEM)] * 5
        + [pl.BlockSpec(memory_space=pltpu.HBM)] * 2,
        scratch_shapes=[pltpu.VMEM((groups, height, width), BF16)],
    )(tokens, cotangent, disp, comb, outs, in_hbm(after1), in_hbm(after2))
    return results[:groups], results[groups]


def mixed_kernel(per, outs, comb, mixed):
    first = first_half(per, comb.shape)
    mixed[...] = dot(jnp.where(first, comb[...], 0.0).astype(BF16), outs[...]).astype(BF16)


def finish_mixed(per, outs, comb):
    seq, cols = comb.shape
    width = outs.shape[1]
    return call(
        functools.partial(mixed_kernel, per),
        "mixed",
        jax.ShapeDtypeStruct((seq, width), BF16),
        8,
        2 * seq * width * cols,
        2 * seq * width,
    )(outs, comb)


def tokens_kernel(per, outs, disp, grad_logits, router_t, after, grad_tokens):
    first = first_half(per, disp.shape)
    disp_cols = jnp.where(first, 0.0, disp[...]).astype(BF16)
    grad_tokens[...] = (
        dot(disp_cols, outs[...]) + dot(grad_logits[...], router_t[...])
    ).astype(BF16)


def finish_tokens(per, outs, disp, grad_logits, router_t, after):
    seq, cols = disp.shape
    width = outs.shape[1]
    return call(
        functools.partial(tokens_kernel, per),
        "grad_tokens",
        jax.ShapeDtypeStruct((seq, width), BF16),
        8,
        4 * seq * width * cols,
        2 * seq * width,
        in_specs=[pl.BlockSpec(memory_space=pltpu.VMEM)] * 4 + [pl.BlockSpec(memory_space=pl.ANY)],
    )(outs, disp, grad_logits, router_t, after)


def join_kernel(*refs):
    *parts, out = refs
    groups = len(parts)
    me = lax.axis_index("dp")
    for part, ref in enumerate(parts):
        out[lax.rem(me - part + groups, groups)] = ref[...].astype(F32)


def join(parts):
    height, width = parts[0].shape
    return call(
        join_kernel,
        "join",
        jax.ShapeDtypeStruct((len(parts), height, width), F32),
        4,
        0,
        6 * height * width,
    )(*parts).reshape(-1, width)


def total_over_devices(parts, beside):
    value = add(exchange(parts, "dp", 1), "add_cores", after=[beside[0](parts[0])])
    for digit in (1, 0):
        after = [beside[1](value)] if digit else []
        value = add([value, *across_chips(value, digit)], "add_chips", after=after)
    return join(exchange([value] * len(parts), "dp", 1))


def local(tokens, router, weight_in, weight_out, cotangent):
    per = weight_in.shape[0]
    experts = router.shape[1]
    chips = experts // per
    groups = lax.axis_size("dp")
    tokens, cotangent = tokens[0], cotangent[0]
    width = tokens.shape[1]
    router_t = router.T

    def to_chips(rows):
        blocks = rows.reshape(chips, 2 * per, width)
        blocks = lax.all_to_all(blocks, "expert", split_axis=0, concat_axis=0, tiled=True)
        return blocks.reshape(rows.shape)

    rows, disp, comb, tokens, cotangent, second_weight = front(
        per, tokens, router_t, cotangent, weight_out
    )
    rows = to_chips(rows)
    first_weight = fetch(rows, weight_in)
    rows = exchange([rows] * groups, "dp", 1)
    back_rows, (slots, grads, hidden, grad_pre) = run_experts(
        rows, (first_weight, second_weight), weight_in, weight_out
    )
    back_rows = add(exchange(back_rows, "dp", -1), "add_groups", chips)
    outs = to_chips(back_rows)
    grad_first, grad_second = weight_grads(slots, grads, hidden, grad_pre, back_rows)
    parts, grad_logits = finish_logits(
        per, groups, tokens, cotangent, disp, comb, outs, grad_first, grad_second
    )
    mixed = finish_mixed(per, outs, comb)
    images = [mixed]

    def finish(value):
        images.append(finish_tokens(per, outs, disp, grad_logits, router_t, value))
        return images[1]

    grad_router = total_over_devices(parts, [lambda value: mixed, finish]).T
    grad_tokens = images[1]
    return (mixed[None], grad_tokens[None], grad_router, grad_first, grad_second)


def solution(mesh):
    return jax.shard_map(
        local,
        mesh=mesh,
        in_specs=(
            P(("dp", "expert"), None, None),
            P(),
            P("expert", None, "dp"),
            P("expert", "dp", None),
            P(("dp", "expert"), None, None),
        ),
        out_specs=(
            P(("dp", "expert"), None, None),
            P(("dp", "expert"), None, None),
            P(),
            P("expert", None, "dp"),
            P("expert", "dp", None),
        ),
        check_vma=False,
    )
```

```python
import functools
import math

import jax
import jax.numpy as jnp
from jax import lax
from jax.experimental import pallas as pl
from jax.experimental.pallas import tpu as pltpu
from jax.sharding import PartitionSpec as P

F32 = jnp.float32
BF16 = jnp.bfloat16
MIB = 1024 * 1024


def dot(left, right, left_dim=1, right_dim=0):
    return lax.dot_general(
        left, right, (((left_dim,), (right_dim,)), ((), ())), preferred_element_type=F32
    )


def iota(shape, dim):
    return lax.broadcasted_iota(jnp.int32, shape, dim)


def in_hbm(value):
    return pltpu.with_memory_space_constraint(value, pltpu.HBM)


def call(kernel, name, out_shape, limit, flops, moved, **more):
    return pl.pallas_call(
        kernel,
        out_shape=out_shape,
        compiler_params=pltpu.CompilerParams(vmem_limit_bytes=limit * MIB),
        cost_estimate=pl.CostEstimate(flops=flops, bytes_accessed=moved, transcendentals=0),
        name=name,
        **more,
    )


def picked_expert(per, rows):
    return (rows // (2 * per)) * per + rows % per


def spread(per, experts):
    shape = (2 * experts, experts)
    return (picked_expert(per, iota(shape, 0)) == iota(shape, 1)).astype(BF16)


def pick_first(per, experts):
    shape = (2 * experts, experts)
    row = iota(shape, 0)
    return ((picked_expert(per, row) == iota(shape, 1)) & (row % (2 * per) < per)).astype(BF16)


def first_half(per, shape):
    return iota(shape, 1) % (2 * per) < per


def front_kernel(per, tokens_hbm, router_hbm, cotangent_hbm, weight_hbm, *refs):
    rows, disp, comb, tokens, cotangent, weight, router_t, sems = refs
    copies = [
        pltpu.make_async_copy(source, target, sems.at[index])
        for index, (source, target) in enumerate(
            (
                (router_hbm, router_t),
                (tokens_hbm, tokens),
                (cotangent_hbm, cotangent),
                (weight_hbm.at[0], weight),
            )
        )
    ]
    for copy in copies:
        copy.start()
    matrix = spread(per, router_t.shape[0])
    copies[0].wait()
    paired_router = dot(matrix, router_t[...]).astype(BF16)
    copies[1].wait()
    logits = dot(tokens[...], paired_router, 1, 1)
    first = first_half(per, logits.shape)
    down = jnp.exp(logits - jnp.max(logits, axis=0, keepdims=True))
    disp_prob = down / jnp.sum(down, axis=0, keepdims=True)
    across = jnp.exp(logits - jnp.max(logits, axis=1, keepdims=True))
    comb_prob = across / jnp.sum(jnp.where(first, across, 0.0), axis=1, keepdims=True)
    disp[...] = disp_prob
    comb[...] = comb_prob
    disp_cols = jnp.where(first, disp_prob, 0.0).astype(BF16)
    comb_cols = jnp.where(first, 0.0, comb_prob).astype(BF16)
    copies[2].wait()
    rows[...] = (
        dot(disp_cols, tokens[...], 0, 0) + dot(comb_cols, cotangent[...], 0, 0)
    ).astype(BF16)
    copies[3].wait()


def front(per, tokens, router_t, cotangent, weight):
    seq, width = tokens.shape
    experts = router_t.shape[0]
    return call(
        functools.partial(front_kernel, per),
        "front",
        (
            pltpu.VMEM((2 * experts, width), BF16),
            pltpu.VMEM((seq, 2 * experts), F32),
            pltpu.VMEM((seq, 2 * experts), F32),
            pltpu.VMEM(tokens.shape, BF16),
            pltpu.VMEM(cotangent.shape, BF16),
            pltpu.VMEM(weight.shape[1:], BF16),
        ),
        8,
        12 * seq * width * experts,
        6 * seq * width,
        in_specs=[pl.BlockSpec(memory_space=pltpu.HBM)] * 4,
        scratch_shapes=[pltpu.VMEM(router_t.shape, BF16), pltpu.SemaphoreType.DMA((4,))],
    )(in_hbm(tokens), in_hbm(router_t), in_hbm(cotangent), in_hbm(weight))


def digits(chips):
    low = 1 << ((chips.bit_length() - 1) // 2)
    return low, chips // low


def chip_of(first, second, core, chips):
    low, high = digits(chips)
    if core % 2 and low == high:
        first, second = second, first
    return first * low + second


def across_chips(value, digit):
    groups, chips = lax.axis_size("dp"), lax.axis_size("expert")
    low, high = digits(chips)
    others = []
    for step in reversed(range(1, low if digit else high)):
        away = [
            chip_of(0, step, core, chips) if digit else chip_of(step, 0, core, chips)
            for core in range(groups)
        ]
        pairs = [
            (core * chips + i, core * chips + (i ^ away[core]))
            for core in range(groups)
            for i in range(chips)
        ]
        others.append(lax.ppermute(value, ("dp", "expert"), pairs))
    return others[::-1]


def shifted(value, axis, by):
    size = lax.axis_size(axis)
    return lax.ppermute(value, axis, [(i, (i + by) % size) for i in range(size)])


def exchange(blocks, axis, sign):
    return [blocks[0]] + [shifted(block, axis, sign * k) for k, block in enumerate(blocks) if k]


def sort_matrix(images, wide, transposed):
    shape = (images * wide, images * wide)
    to, start = (iota(shape, 1), iota(shape, 0)) if transposed else (iota(shape, 0), iota(shape, 1))
    return ((to % images) * wide + to // images == start).astype(BF16)


def add_kernel(images, count, *refs):
    pieces, out = refs[:count], refs[-1]
    total = [piece[...].astype(F32) for piece in pieces]
    while len(total) > 1:
        total = [sum(total[index : index + 2]) for index in range(0, len(total), 2)]
    total = total[0].astype(BF16)
    if images:
        total = dot(sort_matrix(images, total.shape[0] // images, True), total).astype(BF16)
    out[...] = total


def add(pieces, name, images=0, after=()):
    size = pieces[0].size
    return call(
        functools.partial(add_kernel, images, len(pieces)),
        name,
        pltpu.VMEM(pieces[0].shape, BF16),
        4,
        len(pieces) * size,
        4 * size,
        in_specs=[pl.BlockSpec(memory_space=pltpu.VMEM)] * len(pieces)
        + [pl.BlockSpec(memory_space=pltpu.HBM)] * len(after),
    )(*pieces, *map(in_hbm, after))


def fetch_kernel(rows, source, target, sems):
    height = target.shape[0] // sems.shape[0]
    copies = [
        pltpu.make_async_copy(
            source.at[0, pl.ds(part * height, height)],
            target.at[pl.ds(part * height, height)],
            sems.at[part],
        )
        for part in range(sems.shape[0])
    ]
    for copy in copies:
        copy.start()
    for copy in copies:
        copy.wait()


def fetch(after, weight):
    return call(
        fetch_kernel,
        "fetch_first",
        pltpu.VMEM(weight.shape[1:], BF16),
        2,
        0,
        4 * weight[0].size,
        in_specs=[pl.BlockSpec(memory_space=pl.ANY), pl.BlockSpec(memory_space=pltpu.HBM)],
        scratch_shapes=[pltpu.SemaphoreType.DMA((2,))],
    )(after, in_hbm(weight))


def experts_kernel(per, groups, *refs):
    rows, refs = refs[:groups], refs[groups:]
    resident, weights_hbm, refs = refs[:2], refs[2:4], refs[4:]
    back_rows, refs = refs[:groups], refs[groups:]
    slots_out, grads_out, hidden_out, pre_out, w_first, w_second, sems = refs
    wide = 2 * per
    size = rows[0].shape[0] // wide
    span = lambda j: slice(j * size, (j + 1) * size)
    def copy(k, index):
        target = (w_first, w_second)[index]
        return pltpu.make_async_copy(weights_hbm[index].at[k], target.at[k], sems.at[index, k])

    copies = [None] + [(copy(k, 0), copy(k, 1)) for k in range(1, per)]

    def start(k):
        for one in copies[k] if k < per else ():
            one.start()

    start(1)
    matrix = sort_matrix(size, wide, False)
    for part in range(groups):
        moved = dot(matrix, rows[part][...]).astype(BF16)
        for k in range(per):
            slots_out[k, span(part), :] = moved[span(k), :]
            grads_out[k, span(part), :] = moved[span(per + k), :]
    for k in range(per):
        for one in copies[k] if k else ():
            one.wait()
        start(k + 2)
        first, second = (w_first.at[k], w_second.at[k]) if k else resident
        pre_act = dot(slots_out[k], first[...])
        grad_hidden = dot(grads_out[k], second[...], 1, 1)
        phi = 0.5 * (1.0 + lax.erf(pre_act * math.sqrt(0.5)))
        density = jnp.exp(pre_act * pre_act * -0.5) * (1.0 / math.sqrt(2.0 * math.pi))
        hidden = (pre_act * phi).astype(BF16)
        hidden_out[k] = hidden
        out = dot(hidden, second[...]).astype(BF16)
        grad_pre = ((phi + pre_act * density) * grad_hidden).astype(BF16)
        pre_out[k] = grad_pre
        grad_slot = dot(grad_pre, first[...], 1, 1).astype(BF16)
        for part, target in enumerate(back_rows):
            target[span(k), :] = out[span(part), :]
            target[span(per + k), :] = grad_slot[span(part), :]


def run_experts(rows, weights, w_first, w_second):
    per, width, units = w_first.shape
    groups = len(rows)
    total = rows[0].shape[0]
    images = groups * total // (2 * per)
    results = call(
        functools.partial(experts_kernel, per, groups),
        "experts",
        [pltpu.VMEM((total, width), BF16)] * groups
        + [pltpu.VMEM((per, images, width), BF16)] * 2
        + [pltpu.VMEM((per, images, units), BF16)] * 2,
        32,
        8 * per * images * width * units,
        4 * per * width * units,
        in_specs=[pl.BlockSpec(memory_space=pltpu.VMEM)] * (groups + 2)
        + [pl.BlockSpec(memory_space=pltpu.HBM)] * 2,
        scratch_shapes=[
            pltpu.VMEM(w_first.shape, BF16),
            pltpu.VMEM(w_second.shape, BF16),
            pltpu.SemaphoreType.DMA((2, per)),
        ],
    )(*rows, *weights, in_hbm(w_first), in_hbm(w_second))
    return results[:groups], results[groups:]


def outer_kernel(slots, grad_pre, hidden, grads, after, grad_first, grad_second):
    for left, right, out in ((slots, grad_pre, grad_first), (hidden, grads, grad_second)):
        height = out.shape[1]
        piece = math.gcd(height, 128)
        for top in range(0, height, piece):
            rows = slice(top, top + piece)
            out[0, rows, :] = dot(left[0, :, rows], right[0], 0, 0).astype(BF16)


def weight_grads(slots, grads, hidden, grad_pre, after):
    per, images, width = slots.shape
    units = hidden.shape[2]
    parts = 2 if units % 256 == 0 and width % 256 == 0 else 1
    lefts = lambda size: pl.BlockSpec((1, images, size // parts), lambda k, part: (k, 0, part))
    rights = lambda size: pl.BlockSpec((1, images, size), lambda k, part: (k, 0, 0))
    results = lambda a, b: pl.BlockSpec((1, a // parts, b), lambda k, part: (k, part, 0))
    return call(
        outer_kernel,
        "weight_grads",
        (
            jax.ShapeDtypeStruct((per, width, units), BF16),
            jax.ShapeDtypeStruct((per, units, width), BF16),
        ),
        16,
        4 * per * images * width * units,
        4 * per * width * units,
        grid=(per, parts),
        in_specs=[
            lefts(width),
            rights(units),
            lefts(units),
            rights(width),
            pl.BlockSpec(memory_space=pl.ANY),
        ],
        out_specs=[results(width, units), results(units, width)],
    )(slots, grad_pre, hidden, grads, after)


def logits_kernel(per, groups, tokens, cotangent, disp, comb, outs, after1, after2, *refs):
    *parts, grad_logits, terms = refs
    rows = outs[...]
    disp_prob = disp[...]
    comb_prob = comb[...]
    first = first_half(per, disp_prob.shape)
    grad_comb = dot(cotangent[...], rows, 1, 1)
    grad_disp = dot(tokens[...], rows, 1, 1)
    part_disp = disp_prob * (
        grad_disp - jnp.sum(disp_prob * grad_disp, axis=0, keepdims=True)
    )
    comb_sum = jnp.sum(jnp.where(first, comb_prob * grad_comb, 0.0), axis=1, keepdims=True)
    part_comb = comb_prob * (grad_comb - comb_sum)
    both = jnp.where(first, part_comb, part_disp)
    cols = both.shape[1]
    other = jnp.where(first, pltpu.roll(both, cols - per, 1), pltpu.roll(both, per, 1))
    paired = (both + other).astype(BF16)
    one_each = dot(paired, pick_first(per, cols // 2)).astype(BF16)
    grad_logits[...] = one_each
    term = dot(one_each, tokens[...], 0, 0)
    height = terms.shape[1]
    for part in range(groups):
        terms[part] = term[part * height : (part + 1) * height, :].astype(BF16)
    me = lax.axis_index("dp")
    for part, out in enumerate(parts):
        out[...] = terms[lax.rem(me + part, groups)]


def finish_logits(per, groups, tokens, cotangent, disp, comb, outs, after1, after2):
    seq, width = tokens.shape
    cols = disp.shape[1]
    height = cols // 2 // groups
    results = call(
        functools.partial(logits_kernel, per, groups),
        "grad_logits",
        [pltpu.VMEM((height, width), BF16)] * groups + [pltpu.VMEM((seq, cols // 2), BF16)],
        8,
        6 * seq * width * cols,
        6 * seq * width,
        in_specs=[pl.BlockSpec(memory_space=pltpu.VMEM)] * 5
        + [pl.BlockSpec(memory_space=pltpu.HBM)] * 2,
        scratch_shapes=[pltpu.VMEM((groups, height, width), BF16)],
    )(tokens, cotangent, disp, comb, outs, in_hbm(after1), in_hbm(after2))
    return results[:groups], results[groups]


def mixed_kernel(per, outs, comb, mixed):
    first = first_half(per, comb.shape)
    mixed[...] = dot(jnp.where(first, comb[...], 0.0).astype(BF16), outs[...]).astype(BF16)


def finish_mixed(per, outs, comb):
    seq, cols = comb.shape
    width = outs.shape[1]
    return call(
        functools.partial(mixed_kernel, per),
        "mixed",
        jax.ShapeDtypeStruct((seq, width), BF16),
        8,
        2 * seq * width * cols,
        2 * seq * width,
    )(outs, comb)


def tokens_kernel(per, outs, disp, grad_logits, router_t, after, grad_tokens):
    first = first_half(per, disp.shape)
    disp_cols = jnp.where(first, 0.0, disp[...]).astype(BF16)
    grad_tokens[...] = (
        dot(disp_cols, outs[...]) + dot(grad_logits[...], router_t[...])
    ).astype(BF16)


def finish_tokens(per, outs, disp, grad_logits, router_t, after):
    seq, cols = disp.shape
    width = outs.shape[1]
    return call(
        functools.partial(tokens_kernel, per),
        "grad_tokens",
        jax.ShapeDtypeStruct((seq, width), BF16),
        8,
        4 * seq * width * cols,
        2 * seq * width,
        in_specs=[pl.BlockSpec(memory_space=pltpu.VMEM)] * 4 + [pl.BlockSpec(memory_space=pl.ANY)],
    )(outs, disp, grad_logits, router_t, after)


def join_kernel(*refs):
    *parts, out = refs
    groups = len(parts)
    me = lax.axis_index("dp")
    for part, ref in enumerate(parts):
        out[lax.rem(me - part + groups, groups)] = ref[...].astype(F32)


def join(parts):
    height, width = parts[0].shape
    return call(
        join_kernel,
        "join",
        jax.ShapeDtypeStruct((len(parts), height, width), F32),
        4,
        0,
        6 * height * width,
    )(*parts).reshape(-1, width)


def total_over_devices(parts, beside):
    value = add(exchange(parts, "dp", 1), "add_cores", after=[beside[0](parts[0])])
    for digit in (1, 0):
        after = [beside[1](value)] if digit else []
        value = add([value, *across_chips(value, digit)], "add_chips", after=after)
    return join(exchange([value] * len(parts), "dp", 1))


def local(tokens, router, weight_in, weight_out, cotangent):
    per = weight_in.shape[0]
    experts = router.shape[1]
    chips = experts // per
    groups = lax.axis_size("dp")
    tokens, cotangent = tokens[0], cotangent[0]
    width = tokens.shape[1]
    router_t = router.T

    def to_chips(rows):
        blocks = rows.reshape(chips, 2 * per, width)
        blocks = lax.all_to_all(blocks, "expert", split_axis=0, concat_axis=0, tiled=True)
        return blocks.reshape(rows.shape)

    rows, disp, comb, tokens, cotangent, second_weight = front(
        per, tokens, router_t, cotangent, weight_out
    )
    rows = to_chips(rows)
    first_weight = fetch(rows, weight_in)
    rows = exchange([rows] * groups, "dp", 1)
    back_rows, (slots, grads, hidden, grad_pre) = run_experts(
        rows, (first_weight, second_weight), weight_in, weight_out
    )
    back_rows = add(exchange(back_rows, "dp", -1), "add_groups", chips)
    outs = to_chips(back_rows)
    grad_first, grad_second = weight_grads(slots, grads, hidden, grad_pre, back_rows)
    parts, grad_logits = finish_logits(
        per, groups, tokens, cotangent, disp, comb, outs, grad_first, grad_second
    )
    mixed = finish_mixed(per, outs, comb)
    images = [mixed]

    def finish(value):
        images.append(finish_tokens(per, outs, disp, grad_logits, router_t, value))
        return images[1]

    grad_router = total_over_devices(parts, [lambda value: mixed, finish]).T
    grad_tokens = images[1]
    return (mixed[None], grad_tokens[None], grad_router, grad_first, grad_second)


def solution(mesh):
    return jax.shard_map(
        local,
        mesh=mesh,
        in_specs=(
            P(("dp", "expert"), None, None),
            P(),
            P("expert", None, "dp"),
            P("expert", "dp", None),
            P(("dp", "expert"), None, None),
        ),
        out_specs=(
            P(("dp", "expert"), None, None),
            P(("dp", "expert"), None, None),
            P(),
            P("expert", None, "dp"),
            P("expert", "dp", None),
        ),
        check_vma=False,
    )
```

```python
import functools
import math

import jax
import jax.numpy as jnp
from jax import lax
from jax.experimental import pallas as pl
from jax.experimental.pallas import tpu as pltpu
from jax.sharding import PartitionSpec as P

F32 = jnp.float32
BF16 = jnp.bfloat16
MIB = 1024 * 1024


def dot(left, right, left_dim=1, right_dim=0):
    return lax.dot_general(
        left, right, (((left_dim,), (right_dim,)), ((), ())), preferred_element_type=F32
    )


def iota(shape, dim):
    return lax.broadcasted_iota(jnp.int32, shape, dim)


def in_hbm(value):
    return pltpu.with_memory_space_constraint(value, pltpu.HBM)


def call(kernel, name, out_shape, limit, flops, moved, **more):
    return pl.pallas_call(
        kernel,
        out_shape=out_shape,
        compiler_params=pltpu.CompilerParams(vmem_limit_bytes=limit * MIB),
        cost_estimate=pl.CostEstimate(flops=flops, bytes_accessed=moved, transcendentals=0),
        name=name,
        **more,
    )


def picked_expert(per, rows):
    return (rows // (2 * per)) * per + rows % per


def spread(per, experts):
    shape = (2 * experts, experts)
    return (picked_expert(per, iota(shape, 0)) == iota(shape, 1)).astype(BF16)


def pick_first(per, experts):
    shape = (2 * experts, experts)
    row = iota(shape, 0)
    return ((picked_expert(per, row) == iota(shape, 1)) & (row % (2 * per) < per)).astype(BF16)


def first_half(per, shape):
    return iota(shape, 1) % (2 * per) < per


def front_kernel(per, tokens_hbm, router_hbm, cotangent_hbm, weight_hbm, *refs):
    rows, disp, comb, tokens, cotangent, weight, router_t, sems = refs
    copies = [
        pltpu.make_async_copy(source, target, sems.at[index])
        for index, (source, target) in enumerate(
            (
                (router_hbm, router_t),
                (tokens_hbm, tokens),
                (cotangent_hbm, cotangent),
                (weight_hbm.at[0], weight),
            )
        )
    ]
    for copy in copies:
        copy.start()
    matrix = spread(per, router_t.shape[0])
    copies[0].wait()
    paired_router = dot(matrix, router_t[...]).astype(BF16)
    copies[1].wait()
    logits = dot(tokens[...], paired_router, 1, 1)
    first = first_half(per, logits.shape)
    down = jnp.exp(logits - jnp.max(logits, axis=0, keepdims=True))
    disp_prob = down / jnp.sum(down, axis=0, keepdims=True)
    across = jnp.exp(logits - jnp.max(logits, axis=1, keepdims=True))
    comb_prob = across / jnp.sum(jnp.where(first, across, 0.0), axis=1, keepdims=True)
    disp[...] = disp_prob
    comb[...] = comb_prob
    disp_cols = jnp.where(first, disp_prob, 0.0).astype(BF16)
    comb_cols = jnp.where(first, 0.0, comb_prob).astype(BF16)
    copies[2].wait()
    rows[...] = (
        dot(disp_cols, tokens[...], 0, 0) + dot(comb_cols, cotangent[...], 0, 0)
    ).astype(BF16)
    copies[3].wait()


def front(per, tokens, router_t, cotangent, weight):
    seq, width = tokens.shape
    experts = router_t.shape[0]
    return call(
        functools.partial(front_kernel, per),
        "front",
        (
            pltpu.VMEM((2 * experts, width), BF16),
            pltpu.VMEM((seq, 2 * experts), F32),
            pltpu.VMEM((seq, 2 * experts), F32),
            pltpu.VMEM(tokens.shape, BF16),
            pltpu.VMEM(cotangent.shape, BF16),
            pltpu.VMEM(weight.shape[1:], BF16),
        ),
        8,
        12 * seq * width * experts,
        6 * seq * width,
        in_specs=[pl.BlockSpec(memory_space=pltpu.HBM)] * 4,
        scratch_shapes=[pltpu.VMEM(router_t.shape, BF16), pltpu.SemaphoreType.DMA((4,))],
    )(in_hbm(tokens), in_hbm(router_t), in_hbm(cotangent), in_hbm(weight))


def digits(chips):
    low = 1 << ((chips.bit_length() - 1) // 2)
    return low, chips // low


def chip_of(first, second, core, chips):
    low, high = digits(chips)
    if core % 2 and low == high:
        first, second = second, first
    return first * low + second


def across_chips(value, digit):
    groups, chips = lax.axis_size("dp"), lax.axis_size("expert")
    low, high = digits(chips)
    others = []
    for step in reversed(range(1, low if digit else high)):
        away = [
            chip_of(0, step, core, chips) if digit else chip_of(step, 0, core, chips)
            for core in range(groups)
        ]
        pairs = [
            (core * chips + i, core * chips + (i ^ away[core]))
            for core in range(groups)
            for i in range(chips)
        ]
        others.append(lax.ppermute(value, ("dp", "expert"), pairs))
    return others[::-1]


def shifted(value, axis, by):
    size = lax.axis_size(axis)
    return lax.ppermute(value, axis, [(i, (i + by) % size) for i in range(size)])


def exchange(blocks, axis, sign):
    return [blocks[0]] + [shifted(block, axis, sign * k) for k, block in enumerate(blocks) if k]


def sort_matrix(images, wide, transposed):
    shape = (images * wide, images * wide)
    to, start = (iota(shape, 1), iota(shape, 0)) if transposed else (iota(shape, 0), iota(shape, 1))
    return ((to % images) * wide + to // images == start).astype(BF16)


def add_kernel(images, count, *refs):
    pieces, out = refs[count - 1 :: -1], refs[-1]
    total = [piece[...].astype(F32) for piece in pieces]
    while len(total) > 1:
        total = [sum(total[index : index + 2]) for index in range(0, len(total), 2)]
    total = total[0].astype(BF16)
    if images:
        total = dot(sort_matrix(images, total.shape[0] // images, True), total).astype(BF16)
    out[...] = total


def add(pieces, name, images=0, after=()):
    size = pieces[0].size
    return call(
        functools.partial(add_kernel, images, len(pieces)),
        name,
        pltpu.VMEM(pieces[0].shape, BF16),
        4,
        len(pieces) * size,
        4 * size,
        in_specs=[pl.BlockSpec(memory_space=pltpu.VMEM)] * len(pieces)
        + [pl.BlockSpec(memory_space=pltpu.HBM)] * len(after),
    )(*pieces[::-1], *map(in_hbm, after))


def fetch_kernel(rows, source, target, sems):
    height = target.shape[0] // sems.shape[0]
    copies = [
        pltpu.make_async_copy(
            source.at[0, pl.ds(part * height, height)],
            target.at[pl.ds(part * height, height)],
            sems.at[part],
        )
        for part in range(sems.shape[0])
    ]
    for copy in copies:
        copy.start()
    for copy in copies:
        copy.wait()


def fetch(after, weight):
    return call(
        fetch_kernel,
        "fetch_first",
        pltpu.VMEM(weight.shape[1:], BF16),
        2,
        0,
        4 * weight[0].size,
        in_specs=[pl.BlockSpec(memory_space=pl.ANY), pl.BlockSpec(memory_space=pltpu.HBM)],
        scratch_shapes=[pltpu.SemaphoreType.DMA((2,))],
    )(after, in_hbm(weight))


def experts_kernel(per, groups, *refs):
    rows, refs = refs[:groups], refs[groups:]
    resident, weights_hbm, refs = refs[:2], refs[2:4], refs[4:]
    back_rows, refs = refs[:groups], refs[groups:]
    slots_out, grads_out, hidden_out, pre_out, w_first, w_second, sems = refs
    wide = 2 * per
    size = rows[0].shape[0] // wide
    span = lambda j: slice(j * size, (j + 1) * size)
    def copy(k, index):
        target = (w_first, w_second)[index]
        return pltpu.make_async_copy(weights_hbm[index].at[k], target.at[k], sems.at[index, k])

    copies = [None] + [(copy(k, 0), copy(k, 1)) for k in range(1, per)]

    def start(k):
        for one in copies[k] if k < per else ():
            one.start()

    start(1)
    matrix = sort_matrix(size, wide, False)
    for part in range(groups):
        moved = dot(matrix, rows[part][...]).astype(BF16)
        for k in range(per):
            slots_out[k, span(part), :] = moved[span(k), :]
            grads_out[k, span(part), :] = moved[span(per + k), :]
    for k in range(per):
        for one in copies[k] if k else ():
            one.wait()
        start(k + 2)
        first, second = (w_first.at[k], w_second.at[k]) if k else resident
        pre_act = dot(slots_out[k], first[...])
        grad_hidden = dot(grads_out[k], second[...], 1, 1)
        phi = 0.5 * (1.0 + lax.erf(pre_act * math.sqrt(0.5)))
        density = jnp.exp(pre_act * pre_act * -0.5) * (1.0 / math.sqrt(2.0 * math.pi))
        hidden = (pre_act * phi).astype(BF16)
        hidden_out[k] = hidden
        out = dot(hidden, second[...]).astype(BF16)
        grad_pre = ((phi + pre_act * density) * grad_hidden).astype(BF16)
        pre_out[k] = grad_pre
        grad_slot = dot(grad_pre, first[...], 1, 1).astype(BF16)
        for part, target in enumerate(back_rows):
            target[span(k), :] = out[span(part), :]
            target[span(per + k), :] = grad_slot[span(part), :]


def run_experts(rows, weights, w_first, w_second):
    per, width, units = w_first.shape
    groups = len(rows)
    total = rows[0].shape[0]
    images = groups * total // (2 * per)
    results = call(
        functools.partial(experts_kernel, per, groups),
        "experts",
        [pltpu.VMEM((total, width), BF16)] * groups
        + [pltpu.VMEM((per, images, width), BF16)] * 2
        + [pltpu.VMEM((per, images, units), BF16)] * 2,
        32,
        8 * per * images * width * units,
        4 * per * width * units,
        in_specs=[pl.BlockSpec(memory_space=pltpu.VMEM)] * (groups + 2)
        + [pl.BlockSpec(memory_space=pltpu.HBM)] * 2,
        scratch_shapes=[
            pltpu.VMEM(w_first.shape, BF16),
            pltpu.VMEM(w_second.shape, BF16),
            pltpu.SemaphoreType.DMA((2, per)),
        ],
    )(*rows, *weights, in_hbm(w_first), in_hbm(w_second))
    return results[:groups], results[groups:]


def outer_kernel(slots, grad_pre, hidden, grads, after, grad_first, grad_second):
    for left, right, out in ((slots, grad_pre, grad_first), (hidden, grads, grad_second)):
        height = out.shape[1]
        piece = math.gcd(height, 128)
        for top in range(0, height, piece):
            rows = slice(top, top + piece)
            out[0, rows, :] = dot(left[0, :, rows], right[0], 0, 0).astype(BF16)


def weight_grads(slots, grads, hidden, grad_pre, after):
    per, images, width = slots.shape
    units = hidden.shape[2]
    parts = 2 if units % 256 == 0 and width % 256 == 0 else 1
    lefts = lambda size: pl.BlockSpec((1, images, size // parts), lambda k, part: (k, 0, part))
    rights = lambda size: pl.BlockSpec((1, images, size), lambda k, part: (k, 0, 0))
    results = lambda a, b: pl.BlockSpec((1, a // parts, b), lambda k, part: (k, part, 0))
    return call(
        outer_kernel,
        "weight_grads",
        (
            jax.ShapeDtypeStruct((per, width, units), BF16),
            jax.ShapeDtypeStruct((per, units, width), BF16),
        ),
        16,
        4 * per * images * width * units,
        4 * per * width * units,
        grid=(per, parts),
        in_specs=[
            lefts(width),
            rights(units),
            lefts(units),
            rights(width),
            pl.BlockSpec(memory_space=pl.ANY),
        ],
        out_specs=[results(width, units), results(units, width)],
    )(slots, grad_pre, hidden, grads, after)


def logits_kernel(per, groups, tokens, cotangent, disp, comb, outs, after1, after2, *refs):
    *parts, grad_logits, terms = refs
    rows = outs[...]
    disp_prob = disp[...]
    comb_prob = comb[...]
    first = first_half(per, disp_prob.shape)
    grad_comb = dot(cotangent[...], rows, 1, 1)
    grad_disp = dot(tokens[...], rows, 1, 1)
    part_disp = disp_prob * (
        grad_disp - jnp.sum(disp_prob * grad_disp, axis=0, keepdims=True)
    )
    comb_sum = jnp.sum(jnp.where(first, comb_prob * grad_comb, 0.0), axis=1, keepdims=True)
    part_comb = comb_prob * (grad_comb - comb_sum)
    both = jnp.where(first, part_comb, part_disp)
    cols = both.shape[1]
    other = jnp.where(first, pltpu.roll(both, cols - per, 1), pltpu.roll(both, per, 1))
    paired = (both + other).astype(BF16)
    one_each = dot(paired, pick_first(per, cols // 2)).astype(BF16)
    grad_logits[...] = one_each
    term = dot(one_each, tokens[...], 0, 0)
    height = terms.shape[1]
    for part in range(groups):
        terms[part] = term[part * height : (part + 1) * height, :].astype(BF16)
    me = lax.axis_index("dp")
    for part, out in enumerate(parts):
        out[...] = terms[lax.rem(me + part, groups)]


def finish_logits(per, groups, tokens, cotangent, disp, comb, outs, after1, after2):
    seq, width = tokens.shape
    cols = disp.shape[1]
    height = cols // 2 // groups
    results = call(
        functools.partial(logits_kernel, per, groups),
        "grad_logits",
        [pltpu.VMEM((height, width), BF16)] * groups + [pltpu.VMEM((seq, cols // 2), BF16)],
        8,
        6 * seq * width * cols,
        6 * seq * width,
        in_specs=[pl.BlockSpec(memory_space=pltpu.VMEM)] * 5
        + [pl.BlockSpec(memory_space=pltpu.HBM)] * 2,
        scratch_shapes=[pltpu.VMEM((groups, height, width), BF16)],
    )(tokens, cotangent, disp, comb, outs, in_hbm(after1), in_hbm(after2))
    return results[:groups], results[groups]


def mixed_kernel(per, outs, comb, mixed):
    first = first_half(per, comb.shape)
    mixed[...] = dot(jnp.where(first, comb[...], 0.0).astype(BF16), outs[...]).astype(BF16)


def finish_mixed(per, outs, comb):
    seq, cols = comb.shape
    width = outs.shape[1]
    return call(
        functools.partial(mixed_kernel, per),
        "mixed",
        jax.ShapeDtypeStruct((seq, width), BF16),
        8,
        2 * seq * width * cols,
        2 * seq * width,
    )(outs, comb)


def tokens_kernel(per, outs, disp, grad_logits, router_t, after, grad_tokens):
    first = first_half(per, disp.shape)
    disp_cols = jnp.where(first, 0.0, disp[...]).astype(BF16)
    grad_tokens[...] = (
        dot(disp_cols, outs[...]) + dot(grad_logits[...], router_t[...])
    ).astype(BF16)


def finish_tokens(per, outs, disp, grad_logits, router_t, after):
    seq, cols = disp.shape
    width = outs.shape[1]
    return call(
        functools.partial(tokens_kernel, per),
        "grad_tokens",
        jax.ShapeDtypeStruct((seq, width), BF16),
        8,
        4 * seq * width * cols,
        2 * seq * width,
        in_specs=[pl.BlockSpec(memory_space=pltpu.VMEM)] * 4 + [pl.BlockSpec(memory_space=pl.ANY)],
    )(outs, disp, grad_logits, router_t, after)


def join_kernel(*refs):
    *parts, out = refs
    groups = len(parts)
    me = lax.axis_index("dp")
    for part, ref in enumerate(parts):
        out[lax.rem(me - part + groups, groups)] = ref[...].astype(F32)


def join(parts):
    height, width = parts[0].shape
    return call(
        join_kernel,
        "join",
        jax.ShapeDtypeStruct((len(parts), height, width), F32),
        4,
        0,
        6 * height * width,
    )(*parts).reshape(-1, width)


def total_over_devices(parts, beside):
    value = add(exchange(parts, "dp", 1), "add_cores", after=[beside[0](parts[0])])
    for digit in (1, 0):
        after = [beside[1](value)] if digit else []
        value = add([value, *across_chips(value, digit)], "add_chips", after=after)
    return join(exchange([value] * len(parts), "dp", 1))


def local(tokens, router, weight_in, weight_out, cotangent):
    per = weight_in.shape[0]
    experts = router.shape[1]
    chips = experts // per
    groups = lax.axis_size("dp")
    tokens, cotangent = tokens[0], cotangent[0]
    width = tokens.shape[1]
    router_t = router.T

    def to_chips(rows):
        blocks = rows.reshape(chips, 2 * per, width)
        blocks = lax.all_to_all(blocks, "expert", split_axis=0, concat_axis=0, tiled=True)
        return blocks.reshape(rows.shape)

    rows, disp, comb, tokens, cotangent, second_weight = front(
        per, tokens, router_t, cotangent, weight_out
    )
    rows = to_chips(rows)
    first_weight = fetch(rows, weight_in)
    rows = exchange([rows] * groups, "dp", 1)
    back_rows, (slots, grads, hidden, grad_pre) = run_experts(
        rows, (first_weight, second_weight), weight_in, weight_out
    )
    back_rows = add(exchange(back_rows, "dp", -1), "add_groups", chips)
    outs = to_chips(back_rows)
    grad_first, grad_second = weight_grads(slots, grads, hidden, grad_pre, back_rows)
    parts, grad_logits = finish_logits(
        per, groups, tokens, cotangent, disp, comb, outs, grad_first, grad_second
    )
    mixed = finish_mixed(per, outs, comb)
    images = [mixed]

    def finish(value):
        images.append(finish_tokens(per, outs, disp, grad_logits, router_t, value))
        return images[1]

    grad_router = total_over_devices(parts, [lambda value: mixed, finish]).T
    grad_tokens = images[1]
    return (mixed[None], grad_tokens[None], grad_router, grad_first, grad_second)


def solution(mesh):
    return jax.shard_map(
        local,
        mesh=mesh,
        in_specs=(
            P(("dp", "expert"), None, None),
            P(),
            P("expert", None, "dp"),
            P("expert", "dp", None),
            P(("dp", "expert"), None, None),
        ),
        out_specs=(
            P(("dp", "expert"), None, None),
            P(("dp", "expert"), None, None),
            P(),
            P("expert", None, "dp"),
            P("expert", "dp", None),
        ),
        check_vma=False,
    )
```

```python
import functools
import math

import jax
import jax.numpy as jnp
from jax import lax
from jax.experimental import pallas as pl
from jax.experimental.pallas import tpu as pltpu
from jax.sharding import PartitionSpec as P

F32 = jnp.float32
BF16 = jnp.bfloat16
MIB = 1024 * 1024


def dot(left, right, left_dim=1, right_dim=0):
    return lax.dot_general(
        left, right, (((left_dim,), (right_dim,)), ((), ())), preferred_element_type=F32
    )


def iota(shape, dim):
    return lax.broadcasted_iota(jnp.int32, shape, dim)


def in_hbm(value):
    return pltpu.with_memory_space_constraint(value, pltpu.HBM)


def call(kernel, name, out_shape, limit, flops, moved, **more):
    return pl.pallas_call(
        kernel,
        out_shape=out_shape,
        compiler_params=pltpu.CompilerParams(vmem_limit_bytes=limit * MIB),
        cost_estimate=pl.CostEstimate(flops=flops, bytes_accessed=moved, transcendentals=0),
        name=name,
        **more,
    )


def picked_expert(per, rows):
    return (rows // (2 * per)) * per + rows % per


def spread(per, experts):
    shape = (2 * experts, experts)
    return (picked_expert(per, iota(shape, 0)) == iota(shape, 1)).astype(BF16)


def pick_first(per, experts):
    shape = (2 * experts, experts)
    row = iota(shape, 0)
    return ((picked_expert(per, row) == iota(shape, 1)) & (row % (2 * per) < per)).astype(BF16)


def first_half(per, shape):
    return iota(shape, 1) % (2 * per) < per


def front_kernel(per, tokens_hbm, router_hbm, cotangent_hbm, weight_hbm, *refs):
    rows, disp, comb, tokens, cotangent, weight, router_t, sems = refs
    copies = [
        pltpu.make_async_copy(source, target, sems.at[index])
        for index, (source, target) in enumerate(
            (
                (router_hbm, router_t),
                (tokens_hbm, tokens),
                (cotangent_hbm, cotangent),
                (weight_hbm.at[0], weight),
            )
        )
    ]
    for copy in copies:
        copy.start()
    matrix = spread(per, router_t.shape[0])
    copies[0].wait()
    paired_router = dot(matrix, router_t[...]).astype(BF16)
    copies[1].wait()
    logits = dot(tokens[...], paired_router, 1, 1)
    first = first_half(per, logits.shape)
    down = jnp.exp(logits - jnp.max(logits, axis=0, keepdims=True))
    disp_prob = down / jnp.sum(down, axis=0, keepdims=True)
    across = jnp.exp(logits - jnp.max(logits, axis=1, keepdims=True))
    comb_prob = across / jnp.sum(jnp.where(first, across, 0.0), axis=1, keepdims=True)
    disp[...] = disp_prob
    comb[...] = comb_prob
    disp_cols = jnp.where(first, disp_prob, 0.0).astype(BF16)
    comb_cols = jnp.where(first, 0.0, comb_prob).astype(BF16)
    copies[2].wait()
    rows[...] = (
        dot(disp_cols, tokens[...], 0, 0) + dot(comb_cols, cotangent[...], 0, 0)
    ).astype(BF16)
    copies[3].wait()


def front(per, tokens, router_t, cotangent, weight):
    seq, width = tokens.shape
    experts = router_t.shape[0]
    return call(
        functools.partial(front_kernel, per),
        "front",
        (
            pltpu.VMEM((2 * experts, width), BF16),
            pltpu.VMEM((seq, 2 * experts), F32),
            pltpu.VMEM((seq, 2 * experts), F32),
            pltpu.VMEM(tokens.shape, BF16),
            pltpu.VMEM(cotangent.shape, BF16),
            pltpu.VMEM(weight.shape[1:], BF16),
        ),
        8,
        12 * seq * width * experts,
        6 * seq * width,
        in_specs=[pl.BlockSpec(memory_space=pltpu.HBM)] * 4,
        scratch_shapes=[pltpu.VMEM(router_t.shape, BF16), pltpu.SemaphoreType.DMA((4,))],
    )(in_hbm(tokens), in_hbm(router_t), in_hbm(cotangent), in_hbm(weight))


def digits(chips):
    low = 1 << ((chips.bit_length() - 1) // 2)
    return low, chips // low


def chip_of(first, second, core, chips):
    low, high = digits(chips)
    usual = first * low + second
    return usual + (core % 2 if low == high else 0) * (second * low + first - usual)


def away_chip(first, second, chips):
    return lax.axis_index("expert") ^ chip_of(first, second, lax.axis_index("dp"), chips)


def across_chips(values, digit):
    groups, chips = lax.axis_size("dp"), lax.axis_size("expert")
    got = [values[0]]
    for step in range(1, len(values)):
        away = [
            chip_of(0, step, core, chips) if digit else chip_of(step, 0, core, chips)
            for core in range(groups)
        ]
        pairs = [
            (core * chips + i, core * chips + (i ^ away[core]))
            for core in range(groups)
            for i in range(chips)
        ]
        got.append(lax.ppermute(values[step], ("dp", "expert"), pairs))
    return got


def shifted(value, axis, by):
    size = lax.axis_size(axis)
    return lax.ppermute(value, axis, [(i, (i + by) % size) for i in range(size)])


def exchange(blocks, axis, sign):
    return [blocks[0]] + [shifted(block, axis, sign * k) for k, block in enumerate(blocks) if k]


def sort_matrix(images, wide):
    shape = (images * wide, images * wide)
    to, start = iota(shape, 0), iota(shape, 1)
    return ((to % images) * wide + to // images == start).astype(BF16)


def pair_sum(pieces):
    total = [piece[...].astype(F32) for piece in pieces]
    while len(total) > 1:
        total = [sum(total[index : index + 2]) for index in range(0, len(total), 2)]
    return total[0]


def add_kernel(count, *refs):
    refs[-1][...] = pair_sum(refs[:count]).astype(BF16)


def add(pieces, name, after=()):
    size = pieces[0].size
    return call(
        functools.partial(add_kernel, len(pieces)),
        name,
        pltpu.VMEM(pieces[0].shape, BF16),
        4,
        len(pieces) * size,
        4 * size,
        in_specs=[pl.BlockSpec(memory_space=pltpu.VMEM)] * len(pieces)
        + [pl.BlockSpec(memory_space=pltpu.HBM)] * len(after),
    )(*pieces, *map(in_hbm, after))


def groups_kernel(count, wide, *refs):
    pieces, outs = refs[:count], refs[count:]
    total = pair_sum(pieces).astype(BF16)
    chips = total.shape[0] // wide
    _, high = digits(chips)
    shape = (chips * wide, chips * wide)
    to, start = iota(shape, 0), iota(shape, 1)
    chip = away_chip(to // wide % high, to // (high * wide), chips)
    moved = dot((start == to % wide * chips + chip).astype(BF16), total)
    height = high * wide
    for part, out in enumerate(outs):
        out[...] = moved[part * height : (part + 1) * height, :].astype(BF16)


def add_groups(pieces, wide):
    total, width = pieces[0].shape
    low, _ = digits(total // wide)
    return call(
        functools.partial(groups_kernel, len(pieces), wide),
        "add_groups",
        [pltpu.VMEM((total // low, width), BF16)] * low,
        8,
        2 * total * total * width,
        4 * total * width,
    )(*pieces)


def regroup_kernel(count, wide, *refs):
    blocks, outs = [ref[...].astype(F32) for ref in refs[count - 1 :: -1]], refs[count + 1 :]
    for part, out in enumerate(outs):
        rows = [block[part * wide : (part + 1) * wide, :] for block in blocks]
        out[...] = jnp.concatenate(rows).astype(BF16)


def regroup(blocks, wide, after):
    height, width = blocks[0].shape
    return call(
        functools.partial(regroup_kernel, len(blocks), wide),
        "regroup",
        [pltpu.VMEM((len(blocks) * wide, width), BF16)] * (height // wide),
        4,
        0,
        4 * height * width * len(blocks),
        in_specs=[pl.BlockSpec(memory_space=pltpu.VMEM)] * len(blocks)
        + [pl.BlockSpec(memory_space=pltpu.HBM)],
    )(*blocks[::-1], in_hbm(after))


def fetch_kernel(rows, source, target, sems):
    height = target.shape[0] // sems.shape[0]
    copies = [
        pltpu.make_async_copy(
            source.at[0, pl.ds(part * height, height)],
            target.at[pl.ds(part * height, height)],
            sems.at[part],
        )
        for part in range(sems.shape[0])
    ]
    for copy in copies:
        copy.start()
    for copy in copies:
        copy.wait()


def fetch(after, weight):
    return call(
        fetch_kernel,
        "fetch_first",
        pltpu.VMEM(weight.shape[1:], BF16),
        2,
        0,
        4 * weight[0].size,
        in_specs=[pl.BlockSpec(memory_space=pl.ANY), pl.BlockSpec(memory_space=pltpu.HBM)],
        scratch_shapes=[pltpu.SemaphoreType.DMA((2,))],
    )(after, in_hbm(weight))


def experts_kernel(per, groups, *refs):
    rows, refs = refs[:groups], refs[groups:]
    resident, weights_hbm, refs = refs[:2], refs[2:4], refs[4:]
    back_rows, refs = refs[:groups], refs[groups:]
    slots_out, grads_out, hidden_out, pre_out, w_first, w_second, sems = refs
    wide = 2 * per
    size = rows[0].shape[0] // wide
    span = lambda j: slice(j * size, (j + 1) * size)
    def copy(k, index):
        target = (w_first, w_second)[index]
        return pltpu.make_async_copy(weights_hbm[index].at[k], target.at[k], sems.at[index, k])

    copies = [None] + [(copy(k, 0), copy(k, 1)) for k in range(1, per)]

    def start(k):
        for one in copies[k] if k < per else ():
            one.start()

    start(1)
    matrix = sort_matrix(size, wide)
    for part in range(groups):
        moved = dot(matrix, rows[part][...]).astype(BF16)
        for k in range(per):
            slots_out[k, span(part), :] = moved[span(k), :]
            grads_out[k, span(part), :] = moved[span(per + k), :]
    for k in range(per):
        for one in copies[k] if k else ():
            one.wait()
        start(k + 2)
        first, second = (w_first.at[k], w_second.at[k]) if k else resident
        pre_act = dot(slots_out[k], first[...])
        grad_hidden = dot(grads_out[k], second[...], 1, 1)
        phi = 0.5 * (1.0 + lax.erf(pre_act * math.sqrt(0.5)))
        density = jnp.exp(pre_act * pre_act * -0.5) * (1.0 / math.sqrt(2.0 * math.pi))
        hidden = (pre_act * phi).astype(BF16)
        hidden_out[k] = hidden
        out = dot(hidden, second[...]).astype(BF16)
        grad_pre = ((phi + pre_act * density) * grad_hidden).astype(BF16)
        pre_out[k] = grad_pre
        grad_slot = dot(grad_pre, first[...], 1, 1).astype(BF16)
        for part, target in enumerate(back_rows):
            target[span(k), :] = out[span(part), :]
            target[span(per + k), :] = grad_slot[span(part), :]


def run_experts(rows, weights, w_first, w_second):
    per, width, units = w_first.shape
    groups = len(rows)
    total = rows[0].shape[0]
    images = groups * total // (2 * per)
    results = call(
        functools.partial(experts_kernel, per, groups),
        "experts",
        [pltpu.VMEM((total, width), BF16)] * groups
        + [pltpu.VMEM((per, images, width), BF16)] * 2
        + [pltpu.VMEM((per, images, units), BF16)] * 2,
        32,
        8 * per * images * width * units,
        4 * per * width * units,
        in_specs=[pl.BlockSpec(memory_space=pltpu.VMEM)] * (groups + 2)
        + [pl.BlockSpec(memory_space=pltpu.HBM)] * 2,
        scratch_shapes=[
            pltpu.VMEM(w_first.shape, BF16),
            pltpu.VMEM(w_second.shape, BF16),
            pltpu.SemaphoreType.DMA((2, per)),
        ],
    )(*rows, *weights, in_hbm(w_first), in_hbm(w_second))
    return results[:groups], results[groups:]


def outer_kernel(slots, grad_pre, hidden, grads, *refs):
    for left, right, out in ((slots, grad_pre, refs[-2]), (hidden, grads, refs[-1])):
        height = out.shape[1]
        piece = math.gcd(height, 128)
        for top in range(0, height, piece):
            rows = slice(top, top + piece)
            out[0, rows, :] = dot(left[0, :, rows], right[0], 0, 0).astype(BF16)


def weight_grads(slots, grads, hidden, grad_pre, after, quarter, into):
    per, images, width = slots.shape
    units = hidden.shape[2]
    begin, end = per * quarter // 4, per * (quarter + 1) // 4
    parts = 2 if units % 256 == 0 and width % 256 == 0 else 1
    lefts = lambda size: pl.BlockSpec(
        (1, images, size // parts), lambda k, part: (begin + k, 0, part)
    )
    rights = lambda size: pl.BlockSpec((1, images, size), lambda k, part: (begin + k, 0, 0))
    results = lambda a, b: pl.BlockSpec(
        (1, a // parts, b), lambda k, part: (begin + k, part, 0)
    )
    return call(
        outer_kernel,
        "weight_grads",
        (
            jax.ShapeDtypeStruct((per, width, units), BF16),
            jax.ShapeDtypeStruct((per, units, width), BF16),
        ),
        16,
        4 * (end - begin) * images * width * units,
        4 * (end - begin) * width * units,
        grid=(end - begin, parts),
        in_specs=[
            lefts(width),
            rights(units),
            lefts(units),
            rights(width),
            pl.BlockSpec(memory_space=pl.ANY),
        ]
        + [pl.BlockSpec(memory_space=pltpu.HBM)] * len(into),
        out_specs=[results(width, units), results(units, width)],
        input_output_aliases={5: 0, 6: 1} if into else {},
    )(slots, grad_pre, hidden, grads, after, *map(in_hbm, into))


def logits_kernel(per, groups, count, tokens, cotangent, disp, comb, after, *refs):
    blocks, parts, refs = refs[count - 1 :: -1], refs[count : count + groups], refs[count + groups :]
    outs, grad_logits, terms = refs
    moved = jnp.concatenate([block[...].astype(F32) for block in blocks]).astype(BF16)
    wide = 2 * per
    shape = (moved.shape[0], moved.shape[0])
    chips = shape[0] // wide
    to, start = iota(shape, 0), iota(shape, 1)
    low, _ = digits(chips)
    chip = away_chip(start // (low * wide), start // wide % low, chips)
    rows = dot((to == chip * wide + start % wide).astype(BF16), moved).astype(BF16)
    outs[...] = rows
    disp_prob = disp[...]
    comb_prob = comb[...]
    first = first_half(per, disp_prob.shape)
    grad_comb = dot(cotangent[...], rows, 1, 1)
    grad_disp = dot(tokens[...], rows, 1, 1)
    part_disp = disp_prob * (
        grad_disp - jnp.sum(disp_prob * grad_disp, axis=0, keepdims=True)
    )
    comb_sum = jnp.sum(jnp.where(first, comb_prob * grad_comb, 0.0), axis=1, keepdims=True)
    part_comb = comb_prob * (grad_comb - comb_sum)
    both = jnp.where(first, part_comb, part_disp)
    cols = both.shape[1]
    other = jnp.where(first, pltpu.roll(both, cols - per, 1), pltpu.roll(both, per, 1))
    paired = (both + other).astype(BF16)
    one_each = dot(paired, pick_first(per, cols // 2)).astype(BF16)
    grad_logits[...] = one_each
    term = dot(one_each, tokens[...], 0, 0)
    height = terms.shape[1]
    for part in range(groups):
        terms[part] = term[part * height : (part + 1) * height, :].astype(BF16)
    me = lax.axis_index("dp")
    for part, out in enumerate(parts):
        out[...] = terms[lax.rem(me + part, groups)]


def finish_logits(per, groups, tokens, cotangent, disp, comb, blocks, after):
    seq, width = tokens.shape
    cols = disp.shape[1]
    height = cols // 2 // groups
    results = call(
        functools.partial(logits_kernel, per, groups, len(blocks)),
        "grad_logits",
        [pltpu.VMEM((height, width), BF16)] * groups
        + [pltpu.VMEM((cols, width), BF16), pltpu.VMEM((seq, cols // 2), BF16)],
        12,
        6 * seq * width * cols,
        6 * seq * width,
        in_specs=[pl.BlockSpec(memory_space=pltpu.VMEM)] * 4
        + [pl.BlockSpec(memory_space=pltpu.HBM)]
        + [pl.BlockSpec(memory_space=pltpu.VMEM)] * len(blocks),
        scratch_shapes=[pltpu.VMEM((groups, height, width), BF16)],
    )(tokens, cotangent, disp, comb, in_hbm(after), *blocks[::-1])
    return results[:groups], *results[groups:]


def mixed_kernel(per, outs, comb, mixed):
    first = first_half(per, comb.shape)
    mixed[...] = dot(jnp.where(first, comb[...], 0.0).astype(BF16), outs[...]).astype(BF16)


def finish_mixed(per, outs, comb):
    seq, cols = comb.shape
    width = outs.shape[1]
    return call(
        functools.partial(mixed_kernel, per),
        "mixed",
        jax.ShapeDtypeStruct((seq, width), BF16),
        8,
        2 * seq * width * cols,
        2 * seq * width,
    )(outs, comb)


def tokens_kernel(per, outs, disp, grad_logits, router_t, after, grad_tokens):
    first = first_half(per, disp.shape)
    disp_cols = jnp.where(first, 0.0, disp[...]).astype(BF16)
    grad_tokens[...] = (
        dot(disp_cols, outs[...]) + dot(grad_logits[...], router_t[...])
    ).astype(BF16)


def finish_tokens(per, outs, disp, grad_logits, router_t, after):
    seq, cols = disp.shape
    width = outs.shape[1]
    return call(
        functools.partial(tokens_kernel, per),
        "grad_tokens",
        jax.ShapeDtypeStruct((seq, width), BF16),
        8,
        4 * seq * width * cols,
        2 * seq * width,
        in_specs=[pl.BlockSpec(memory_space=pltpu.VMEM)] * 4 + [pl.BlockSpec(memory_space=pl.ANY)],
    )(outs, disp, grad_logits, router_t, after)


def join_kernel(*refs):
    *parts, out = refs
    groups = len(parts)
    me = lax.axis_index("dp")
    for part, ref in enumerate(parts):
        out[lax.rem(me - part + groups, groups)] = ref[...].astype(F32)


def join(parts):
    height, width = parts[0].shape
    return call(
        join_kernel,
        "join",
        jax.ShapeDtypeStruct((len(parts), height, width), F32),
        4,
        0,
        6 * height * width,
    )(*parts).reshape(-1, width)


def total_over_devices(parts, mixed, beside):
    value = add(exchange(parts, "dp", 1), "add_cores", after=[mixed])
    for digit, size in zip((1, 0), digits(lax.axis_size("expert"))):
        value = add(across_chips([value] * size, digit), "add_chips", after=[beside(value)])
    return value, join(exchange([value] * len(parts), "dp", 1))


def local(tokens, router, weight_in, weight_out, cotangent):
    per = weight_in.shape[0]
    experts = router.shape[1]
    chips = experts // per
    groups = lax.axis_size("dp")
    tokens, cotangent = tokens[0], cotangent[0]
    width = tokens.shape[1]
    router_t = router.T

    rows, disp, comb, tokens, cotangent, second_weight = front(
        per, tokens, router_t, cotangent, weight_out
    )
    rows = rows.reshape(chips, 2 * per, width)
    rows = lax.all_to_all(rows, "expert", split_axis=0, concat_axis=0, tiled=True)
    rows = rows.reshape(2 * experts, width)
    first_weight = fetch(rows, weight_in)
    rows = exchange([rows] * groups, "dp", 1)
    back_rows, (slots, grads, hidden, grad_pre) = run_experts(
        rows, (first_weight, second_weight), weight_in, weight_out
    )
    done, weight_results = 0, ()

    def next_weight_grads(after):
        nonlocal done, weight_results
        weight_results = weight_grads(slots, grads, hidden, grad_pre, after, done, weight_results)
        done += 1
        return weight_results[0]

    blocks = add_groups(exchange(back_rows, "dp", -1), 2 * per)
    blocks = regroup(across_chips(blocks, 1), 2 * per, next_weight_grads(blocks[0]))
    beside = next_weight_grads(blocks[0])
    parts, outs, grad_logits = finish_logits(
        per, groups, tokens, cotangent, disp, comb, across_chips(blocks, 0), beside
    )
    mixed = finish_mixed(per, outs, comb)
    value, total = total_over_devices(parts, mixed, next_weight_grads)
    grad_tokens = finish_tokens(per, outs, disp, grad_logits, router_t, value)
    grad_router, (grad_first, grad_second) = total.T, weight_results
    return (mixed[None], grad_tokens[None], grad_router, grad_first, grad_second)


def solution(mesh):
    return jax.shard_map(
        local,
        mesh=mesh,
        in_specs=(
            P(("dp", "expert"), None, None),
            P(),
            P("expert", None, "dp"),
            P("expert", "dp", None),
            P(("dp", "expert"), None, None),
        ),
        out_specs=(
            P(("dp", "expert"), None, None),
            P(("dp", "expert"), None, None),
            P(),
            P("expert", None, "dp"),
            P("expert", "dp", None),
        ),
        check_vma=False,
    )
```

```python
import functools
import math

import jax
import jax.numpy as jnp
from jax import lax
from jax.experimental import pallas as pl
from jax.experimental.pallas import tpu as pltpu
from jax.sharding import PartitionSpec as P

F32 = jnp.float32
BF16 = jnp.bfloat16
MIB = 1024 * 1024


def dot(left, right, left_dim=1, right_dim=0):
    return lax.dot_general(
        left, right, (((left_dim,), (right_dim,)), ((), ())), preferred_element_type=F32
    )


def iota(shape, dim):
    return lax.broadcasted_iota(jnp.int32, shape, dim)


def in_hbm(value):
    return pltpu.with_memory_space_constraint(value, pltpu.HBM)


def call(kernel, name, out_shape, limit, flops, moved, **more):
    return pl.pallas_call(
        kernel,
        out_shape=out_shape,
        compiler_params=pltpu.CompilerParams(vmem_limit_bytes=limit * MIB),
        cost_estimate=pl.CostEstimate(flops=flops, bytes_accessed=moved, transcendentals=0),
        name=name,
        **more,
    )


def picked_expert(per, rows):
    return (rows // (2 * per)) * per + rows % per


def spread(per, experts):
    shape = (2 * experts, experts)
    return (picked_expert(per, iota(shape, 0)) == iota(shape, 1)).astype(BF16)


def pick_first(per, experts):
    shape = (2 * experts, experts)
    row = iota(shape, 0)
    return ((picked_expert(per, row) == iota(shape, 1)) & (row % (2 * per) < per)).astype(BF16)


def first_half(per, shape):
    return iota(shape, 1) % (2 * per) < per


def front_kernel(per, tokens_hbm, router_hbm, cotangent_hbm, first_hbm, second_hbm, *refs):
    rows, disp, comb, tokens, cotangent, router_t, first_top, second, sems = refs
    copies = [
        pltpu.make_async_copy(source, target, sems.at[index])
        for index, (source, target) in enumerate(
            (
                (router_hbm, router_t),
                (tokens_hbm, tokens),
                (cotangent_hbm, cotangent),
                (second_hbm.at[0], second),
                (first_hbm.at[0, pl.ds(0, first_top.shape[0])], first_top),
            )
        )
    ]
    for copy in copies:
        copy.start()
    matrix = spread(per, router_t.shape[0])
    copies[0].wait()
    paired_router = dot(matrix, router_t[...]).astype(BF16)
    copies[1].wait()
    logits = dot(tokens[...], paired_router, 1, 1)
    first = first_half(per, logits.shape)
    down = jnp.exp(logits - jnp.max(logits, axis=0, keepdims=True))
    disp_prob = down / jnp.sum(down, axis=0, keepdims=True)
    across = jnp.exp(logits - jnp.max(logits, axis=1, keepdims=True))
    comb_prob = across / jnp.sum(jnp.where(first, across, 0.0), axis=1, keepdims=True)
    disp[...] = disp_prob
    comb[...] = comb_prob
    disp_cols = jnp.where(first, disp_prob, 0.0).astype(BF16)
    comb_cols = jnp.where(first, 0.0, comb_prob).astype(BF16)
    copies[2].wait()
    rows[...] = (
        dot(disp_cols, tokens[...], 0, 0) + dot(comb_cols, cotangent[...], 0, 0)
    ).astype(BF16)
    copies[3].wait()
    copies[4].wait()


def front(per, tokens, router_t, cotangent, w_first, w_second):
    seq, width = tokens.shape
    experts = router_t.shape[0]
    return call(
        functools.partial(front_kernel, per),
        "front",
        (
            pltpu.VMEM((2 * experts, width), BF16),
            pltpu.VMEM((seq, 2 * experts), F32),
            pltpu.VMEM((seq, 2 * experts), F32),
            pltpu.VMEM(tokens.shape, BF16),
            pltpu.VMEM(cotangent.shape, BF16),
            pltpu.VMEM(router_t.shape, BF16),
            pltpu.VMEM((width // 4, w_first.shape[2]), BF16),
            pltpu.VMEM(w_second.shape[1:], BF16),
        ),
        8,
        12 * seq * width * experts,
        6 * seq * width,
        in_specs=[pl.BlockSpec(memory_space=pltpu.HBM)] * 5,
        scratch_shapes=[pltpu.SemaphoreType.DMA((5,))],
    )(*map(in_hbm, (tokens, router_t, cotangent, w_first, w_second)))


def digits(chips):
    low = 1 << ((chips.bit_length() - 1) // 2)
    return low, chips // low


def chip_of(first, second, core, chips):
    low, high = digits(chips)
    usual = first * low + second
    return usual + (core % 2 if low == high else 0) * (second * low + first - usual)


def away_chip(first, second, chips):
    return lax.axis_index("expert") ^ chip_of(first, second, lax.axis_index("dp"), chips)


def across_chips(values, digit):
    groups, chips = lax.axis_size("dp"), lax.axis_size("expert")
    got = [values[0]]
    for step in range(1, len(values)):
        away = [
            chip_of(0, step, core, chips) if digit else chip_of(step, 0, core, chips)
            for core in range(groups)
        ]
        pairs = [
            (core * chips + i, core * chips + (i ^ away[core]))
            for core in range(groups)
            for i in range(chips)
        ]
        got.append(lax.ppermute(values[step], ("dp", "expert"), pairs))
    return got


def shifted(value, axis, by):
    size = lax.axis_size(axis)
    return lax.ppermute(value, axis, [(i, (i + by) % size) for i in range(size)])


def exchange(blocks, axis, sign):
    return [blocks[0]] + [shifted(block, axis, sign * k) for k, block in enumerate(blocks) if k]


def sort_matrix(images, wide):
    shape = (images * wide, images * wide)
    to, start = iota(shape, 0), iota(shape, 1)
    return ((to % images) * wide + to // images == start).astype(BF16)


def pair_sum(pieces):
    total = [piece[...].astype(F32) for piece in pieces]
    while len(total) > 1:
        total = [sum(total[index : index + 2]) for index in range(0, len(total), 2)]
    return total[0]


def add_kernel(count, *refs):
    refs[-1][...] = pair_sum(refs[:count]).astype(BF16)


def add(pieces, name, after=()):
    size = pieces[0].size
    return call(
        functools.partial(add_kernel, len(pieces)),
        name,
        pltpu.VMEM(pieces[0].shape, BF16),
        4,
        len(pieces) * size,
        4 * size,
        in_specs=[pl.BlockSpec(memory_space=pltpu.VMEM)] * len(pieces)
        + [pl.BlockSpec(memory_space=pltpu.HBM)] * len(after),
    )(*pieces, *map(in_hbm, after))


def groups_kernel(count, wide, *refs):
    pieces, outs = refs[:count], refs[count:]
    total = pair_sum(pieces).astype(BF16)
    chips = total.shape[0] // wide
    _, high = digits(chips)
    shape = (chips * wide, chips * wide)
    to, start = iota(shape, 0), iota(shape, 1)
    chip = away_chip(to // wide % high, to // (high * wide), chips)
    moved = dot((start == to % wide * chips + chip).astype(BF16), total)
    height = high * wide
    for part, out in enumerate(outs):
        out[...] = moved[part * height : (part + 1) * height, :].astype(BF16)


def add_groups(pieces, wide):
    total, width = pieces[0].shape
    low, _ = digits(total // wide)
    return call(
        functools.partial(groups_kernel, len(pieces), wide),
        "add_groups",
        [pltpu.VMEM((total // low, width), BF16)] * low,
        8,
        2 * total * total * width,
        4 * total * width,
    )(*pieces)


def regroup_kernel(count, wide, *refs):
    blocks, outs = [ref[...].astype(F32) for ref in refs[count - 1 :: -1]], refs[count + 1 :]
    for part, out in enumerate(outs):
        rows = [block[part * wide : (part + 1) * wide, :] for block in blocks]
        out[...] = jnp.concatenate(rows).astype(BF16)


def regroup(blocks, wide, after):
    height, width = blocks[0].shape
    return call(
        functools.partial(regroup_kernel, len(blocks), wide),
        "regroup",
        [pltpu.VMEM((len(blocks) * wide, width), BF16)] * (height // wide),
        4,
        0,
        4 * height * width * len(blocks),
        in_specs=[pl.BlockSpec(memory_space=pltpu.VMEM)] * len(blocks)
        + [pl.BlockSpec(memory_space=pltpu.HBM)],
    )(*blocks[::-1], in_hbm(after))


def fetch_kernel(wide, rows, source, target, sorted_rows, sems):
    height = target.shape[0] // sems.shape[0]
    top = source.shape[1] - target.shape[0]
    copies = [
        pltpu.make_async_copy(
            source.at[0, pl.ds(top + part * height, height)],
            target.at[pl.ds(part * height, height)],
            sems.at[part],
        )
        for part in range(sems.shape[0])
    ]
    for copy in copies:
        copy.start()
    matrix = sort_matrix(rows.shape[0] // wide, wide)
    sorted_rows[...] = dot(matrix, rows[...]).astype(BF16)
    for copy in copies:
        copy.wait()


def fetch(wide, rows, weight):
    _, width, units = weight.shape
    return call(
        functools.partial(fetch_kernel, wide),
        "fetch_first",
        (pltpu.VMEM((width - width // 4, units), BF16), pltpu.VMEM(rows.shape, BF16)),
        4,
        0,
        4 * weight[0].size,
        in_specs=[
            pl.BlockSpec(memory_space=pltpu.VMEM),
            pl.BlockSpec(memory_space=pltpu.HBM),
        ],
        scratch_shapes=[pltpu.SemaphoreType.DMA((3,))],
    )(rows, in_hbm(weight))


def experts_kernel(per, groups, *refs):
    rows, refs = refs[:groups], refs[groups:]
    (first_top, first_rest, second_weight), weights_hbm, refs = refs[:3], refs[3:5], refs[5:]
    back_rows, refs = refs[:groups], refs[groups:]
    slots_out, grads_out, hidden_out, pre_out, w_first, w_second, sems = refs
    wide = 2 * per
    size = rows[0].shape[0] // wide
    span = lambda j: slice(j * size, (j + 1) * size)

    def copy(k, index):
        target = (w_first, w_second)[index]
        return pltpu.make_async_copy(weights_hbm[index].at[k], target.at[k], sems.at[index, k])

    copies = [None] + [(copy(k, 0), copy(k, 1)) for k in range(1, per)]

    def start(k):
        for one in copies[k] if k < per else ():
            one.start()

    start(1)
    matrix = sort_matrix(size, wide)
    for part in range(groups):
        moved = dot(matrix, rows[part][...]).astype(BF16) if part else rows[0][...]
        for k in range(per):
            slots_out[k, span(part), :] = moved[span(k), :]
            grads_out[k, span(part), :] = moved[span(per + k), :]
    for k in range(per):
        for one in copies[k] if k else ():
            one.wait()
        start(k + 2)
        firsts, second = ([w_first.at[k]], w_second.at[k]) if k else ([first_top, first_rest], second_weight)
        slots = slots_out[k]
        tops = [0, *(first.shape[0] for first in firsts)]
        cuts = [slice(tops[i], tops[i] + tops[i + 1]) for i in range(len(firsts))]
        pre_act = sum(dot(slots[:, cut], first[...]) for cut, first in zip(cuts, firsts))
        grad_hidden = dot(grads_out[k], second[...], 1, 1)
        phi = 0.5 * (1.0 + lax.erf(pre_act * math.sqrt(0.5)))
        density = jnp.exp(pre_act * pre_act * -0.5) * (1.0 / math.sqrt(2.0 * math.pi))
        hidden = (pre_act * phi).astype(BF16)
        hidden_out[k] = hidden
        out = dot(hidden, second[...]).astype(BF16)
        grad_pre = ((phi + pre_act * density) * grad_hidden).astype(BF16)
        pre_out[k] = grad_pre
        grad_slot = [dot(grad_pre, first[...], 1, 1).astype(BF16) for first in firsts]
        grad_slot = jnp.concatenate(grad_slot, axis=1) if len(firsts) > 1 else grad_slot[0]
        for part, target in enumerate(back_rows):
            target[span(k), :] = out[span(part), :]
            target[span(per + k), :] = grad_slot[span(part), :]


def run_experts(rows, weights, w_first, w_second):
    per, width, units = w_first.shape
    groups = len(rows)
    total = rows[0].shape[0]
    images = groups * total // (2 * per)
    results = call(
        functools.partial(experts_kernel, per, groups),
        "experts",
        [pltpu.VMEM((total, width), BF16)] * groups
        + [pltpu.VMEM((per, images, width), BF16)] * 2
        + [pltpu.VMEM((per, images, units), BF16)] * 2,
        32,
        8 * per * images * width * units,
        4 * per * width * units,
        in_specs=[pl.BlockSpec(memory_space=pltpu.VMEM)] * (groups + 3)
        + [pl.BlockSpec(memory_space=pltpu.HBM)] * 2,
        scratch_shapes=[
            pltpu.VMEM(w_first.shape, BF16),
            pltpu.VMEM(w_second.shape, BF16),
            pltpu.SemaphoreType.DMA((2, per)),
        ],
    )(*rows, *weights, in_hbm(w_first), in_hbm(w_second))
    return results[:groups], results[groups:]


def outer_kernel(slots, grad_pre, hidden, grads, *refs):
    for left, right, out in ((slots, grad_pre, refs[-2]), (hidden, grads, refs[-1])):
        height = out.shape[1]
        piece = math.gcd(height, 128)
        for top in range(0, height, piece):
            rows = slice(top, top + piece)
            out[0, rows, :] = dot(left[0, :, rows], right[0], 0, 0).astype(BF16)


def weight_grads(slots, grads, hidden, grad_pre, after, quarter, into):
    per, images, width = slots.shape
    units = hidden.shape[2]
    begin, end = per * quarter // 4, per * (quarter + 1) // 4
    parts = 2 if units % 256 == 0 and width % 256 == 0 else 1
    lefts = lambda size: pl.BlockSpec(
        (1, images, size // parts), lambda k, part: (begin + k, 0, part)
    )
    rights = lambda size: pl.BlockSpec((1, images, size), lambda k, part: (begin + k, 0, 0))
    results = lambda a, b: pl.BlockSpec(
        (1, a // parts, b), lambda k, part: (begin + k, part, 0)
    )
    return call(
        outer_kernel,
        "weight_grads",
        (
            jax.ShapeDtypeStruct((per, width, units), BF16),
            jax.ShapeDtypeStruct((per, units, width), BF16),
        ),
        16,
        4 * (end - begin) * images * width * units,
        4 * (end - begin) * width * units,
        grid=(end - begin, parts),
        in_specs=[
            lefts(width),
            rights(units),
            lefts(units),
            rights(width),
            pl.BlockSpec(memory_space=pl.ANY),
        ]
        + [pl.BlockSpec(memory_space=pltpu.HBM)] * len(into),
        out_specs=[results(width, units), results(units, width)],
        input_output_aliases={5: 0, 6: 1} if into else {},
    )(slots, grad_pre, hidden, grads, after, *map(in_hbm, into))


def logits_kernel(per, groups, count, tokens, cotangent, disp, comb, after, *refs):
    blocks, parts, refs = refs[count - 1 :: -1], refs[count : count + groups], refs[count + groups :]
    outs, grad_logits, terms = refs
    moved = jnp.concatenate([block[...].astype(F32) for block in blocks]).astype(BF16)
    wide = 2 * per
    shape = (moved.shape[0], moved.shape[0])
    chips = shape[0] // wide
    to, start = iota(shape, 0), iota(shape, 1)
    low, _ = digits(chips)
    chip = away_chip(start // (low * wide), start // wide % low, chips)
    rows = dot((to == chip * wide + start % wide).astype(BF16), moved).astype(BF16)
    outs[...] = rows
    disp_prob = disp[...]
    comb_prob = comb[...]
    first = first_half(per, disp_prob.shape)
    grad_comb = dot(cotangent[...], rows, 1, 1)
    grad_disp = dot(tokens[...], rows, 1, 1)
    part_disp = disp_prob * (
        grad_disp - jnp.sum(disp_prob * grad_disp, axis=0, keepdims=True)
    )
    comb_sum = jnp.sum(jnp.where(first, comb_prob * grad_comb, 0.0), axis=1, keepdims=True)
    part_comb = comb_prob * (grad_comb - comb_sum)
    both = jnp.where(first, part_comb, part_disp)
    cols = both.shape[1]
    other = jnp.where(first, pltpu.roll(both, cols - per, 1), pltpu.roll(both, per, 1))
    paired = (both + other).astype(BF16)
    one_each = dot(paired, pick_first(per, cols // 2)).astype(BF16)
    grad_logits[...] = one_each
    term = dot(one_each, tokens[...], 0, 0)
    height = terms.shape[1]
    for part in range(groups):
        terms[part] = term[part * height : (part + 1) * height, :].astype(BF16)
    me = lax.axis_index("dp")
    for part, out in enumerate(parts):
        out[...] = terms[lax.rem(me + part, groups)]


def finish_logits(per, groups, tokens, cotangent, disp, comb, blocks, after):
    seq, width = tokens.shape
    cols = disp.shape[1]
    height = cols // 2 // groups
    results = call(
        functools.partial(logits_kernel, per, groups, len(blocks)),
        "grad_logits",
        [pltpu.VMEM((height, width), BF16)] * groups
        + [pltpu.VMEM((cols, width), BF16), pltpu.VMEM((seq, cols // 2), BF16)],
        12,
        6 * seq * width * cols,
        6 * seq * width,
        in_specs=[pl.BlockSpec(memory_space=pltpu.VMEM)] * 4
        + [pl.BlockSpec(memory_space=pltpu.HBM)]
        + [pl.BlockSpec(memory_space=pltpu.VMEM)] * len(blocks),
        scratch_shapes=[pltpu.VMEM((groups, height, width), BF16)],
    )(tokens, cotangent, disp, comb, in_hbm(after), *blocks[::-1])
    return results[:groups], *results[groups:]


def mixed_kernel(per, outs, comb, mixed):
    first = first_half(per, comb.shape)
    mixed[...] = dot(jnp.where(first, comb[...], 0.0).astype(BF16), outs[...]).astype(BF16)


def finish_mixed(per, outs, comb):
    seq, cols = comb.shape
    width = outs.shape[1]
    return call(
        functools.partial(mixed_kernel, per),
        "mixed",
        jax.ShapeDtypeStruct((seq, width), BF16),
        8,
        2 * seq * width * cols,
        2 * seq * width,
    )(outs, comb)


def tokens_kernel(per, outs, disp, grad_logits, router_t, after, grad_tokens):
    first = first_half(per, disp.shape)
    disp_cols = jnp.where(first, 0.0, disp[...]).astype(BF16)
    grad_tokens[...] = (
        dot(disp_cols, outs[...]) + dot(grad_logits[...], router_t[...])
    ).astype(BF16)


def finish_tokens(per, outs, disp, grad_logits, router_t, after):
    seq, cols = disp.shape
    width = outs.shape[1]
    return call(
        functools.partial(tokens_kernel, per),
        "grad_tokens",
        jax.ShapeDtypeStruct((seq, width), BF16),
        8,
        4 * seq * width * cols,
        2 * seq * width,
        in_specs=[pl.BlockSpec(memory_space=pltpu.VMEM)] * 4 + [pl.BlockSpec(memory_space=pl.ANY)],
    )(outs, disp, grad_logits, router_t, after)


def join_kernel(*refs):
    *parts, out = refs
    groups = len(parts)
    me = lax.axis_index("dp")
    for part, ref in enumerate(parts):
        out[lax.rem(me - part + groups, groups)] = ref[...].astype(F32)


def join(parts):
    height, width = parts[0].shape
    return call(
        join_kernel,
        "join",
        jax.ShapeDtypeStruct((len(parts), height, width), F32),
        4,
        0,
        6 * height * width,
    )(*parts).reshape(-1, width)


def total_over_devices(parts, mixed, beside):
    value = add(exchange(parts, "dp", 1), "add_cores", after=[mixed])
    for digit, size in zip((1, 0), digits(lax.axis_size("expert"))):
        value = add(across_chips([value] * size, digit), "add_chips", after=[beside(value)])
    return value, join(exchange([value] * len(parts), "dp", 1))


def local(tokens, router, weight_in, weight_out, cotangent):
    per = weight_in.shape[0]
    experts = router.shape[1]
    chips = experts // per
    groups = lax.axis_size("dp")
    tokens, cotangent = tokens[0], cotangent[0]
    width = tokens.shape[1]
    router_t = router.T

    rows, disp, comb, tokens, cotangent, router_t, first_top, second_weight = front(
        per, tokens, router_t, cotangent, weight_in, weight_out
    )
    rows = rows.reshape(chips, 2 * per, width)
    rows = lax.all_to_all(rows, "expert", split_axis=0, concat_axis=0, tiled=True)
    rows = rows.reshape(2 * experts, width)
    first_rest, own_rows = fetch(2 * per, rows, weight_in)
    rows = [own_rows, *exchange([rows] * groups, "dp", 1)[1:]]
    back_rows, (slots, grads, hidden, grad_pre) = run_experts(
        rows, (first_top, first_rest, second_weight), weight_in, weight_out
    )
    done, weight_results = 0, ()

    def next_weight_grads(after):
        nonlocal done, weight_results
        weight_results = weight_grads(slots, grads, hidden, grad_pre, after, done, weight_results)
        done += 1
        return weight_results[0]

    blocks = add_groups(exchange(back_rows, "dp", -1), 2 * per)
    blocks = regroup(across_chips(blocks, 1), 2 * per, next_weight_grads(blocks[0]))
    beside = next_weight_grads(blocks[0])
    parts, outs, grad_logits = finish_logits(
        per, groups, tokens, cotangent, disp, comb, across_chips(blocks, 0), beside
    )
    mixed = finish_mixed(per, outs, comb)
    value, total = total_over_devices(parts, mixed, next_weight_grads)
    grad_tokens = finish_tokens(per, outs, disp, grad_logits, router_t, value)
    grad_router, (grad_first, grad_second) = total.T, weight_results
    return (mixed[None], grad_tokens[None], grad_router, grad_first, grad_second)


def solution(mesh):
    return jax.shard_map(
        local,
        mesh=mesh,
        in_specs=(
            P(("dp", "expert"), None, None),
            P(),
            P("expert", None, "dp"),
            P("expert", "dp", None),
            P(("dp", "expert"), None, None),
        ),
        out_specs=(
            P(("dp", "expert"), None, None),
            P(("dp", "expert"), None, None),
            P(),
            P("expert", None, "dp"),
            P("expert", "dp", None),
        ),
        check_vma=False,
    )
```

```python
import functools
import math

import jax
import jax.numpy as jnp
from jax import lax
from jax.experimental import pallas as pl
from jax.experimental.pallas import tpu as pltpu
from jax.sharding import PartitionSpec as P

F32 = jnp.float32
BF16 = jnp.bfloat16
MIB = 1024 * 1024


def dot(left, right, left_dim=1, right_dim=0):
    return lax.dot_general(
        left, right, (((left_dim,), (right_dim,)), ((), ())), preferred_element_type=F32
    )


def iota(shape, dim):
    return lax.broadcasted_iota(jnp.int32, shape, dim)


def in_hbm(value):
    return pltpu.with_memory_space_constraint(value, pltpu.HBM)


def call(kernel, name, out_shape, limit, flops, moved, **more):
    return pl.pallas_call(
        kernel,
        out_shape=out_shape,
        compiler_params=pltpu.CompilerParams(vmem_limit_bytes=limit * MIB),
        cost_estimate=pl.CostEstimate(flops=flops, bytes_accessed=moved, transcendentals=0),
        name=name,
        **more,
    )


def picked_expert(per, rows):
    return (rows // (2 * per)) * per + rows % per


def spread(per, experts):
    shape = (2 * experts, experts)
    return (picked_expert(per, iota(shape, 0)) == iota(shape, 1)).astype(BF16)


def pick_first(per, experts):
    shape = (2 * experts, experts)
    row = iota(shape, 0)
    return ((picked_expert(per, row) == iota(shape, 1)) & (row % (2 * per) < per)).astype(BF16)


def first_half(per, shape):
    return iota(shape, 1) % (2 * per) < per


def front_kernel(per, tokens_hbm, router_hbm, cotangent_hbm, first_hbm, second_hbm, *refs):
    rows, disp, comb, tokens, cotangent, router_t, first_top, second, sems = refs
    copies = [
        pltpu.make_async_copy(source, target, sems.at[index])
        for index, (source, target) in enumerate(
            (
                (router_hbm, router_t),
                (tokens_hbm, tokens),
                (cotangent_hbm, cotangent),
                (second_hbm.at[0], second),
                (first_hbm.at[0, pl.ds(0, first_top.shape[0])], first_top),
            )
        )
    ]
    for copy in copies:
        copy.start()
    matrix = spread(per, router_t.shape[0])
    copies[0].wait()
    paired_router = dot(matrix, router_t[...]).astype(BF16)
    copies[1].wait()
    logits = dot(tokens[...], paired_router, 1, 1)
    first = first_half(per, logits.shape)
    down = jnp.exp(logits - jnp.max(logits, axis=0, keepdims=True))
    disp_prob = down / jnp.sum(down, axis=0, keepdims=True)
    across = jnp.exp(logits - jnp.max(logits, axis=1, keepdims=True))
    comb_prob = across / jnp.sum(jnp.where(first, across, 0.0), axis=1, keepdims=True)
    disp[...] = disp_prob
    comb[...] = comb_prob
    disp_cols = jnp.where(first, disp_prob, 0.0).astype(BF16)
    comb_cols = jnp.where(first, 0.0, comb_prob).astype(BF16)
    copies[2].wait()
    rows[...] = (
        dot(disp_cols, tokens[...], 0, 0) + dot(comb_cols, cotangent[...], 0, 0)
    ).astype(BF16)
    copies[3].wait()
    copies[4].wait()


def front(per, tokens, router_t, cotangent, w_first, w_second):
    seq, width = tokens.shape
    experts = router_t.shape[0]
    return call(
        functools.partial(front_kernel, per),
        "front",
        (
            pltpu.VMEM((2 * experts, width), BF16),
            pltpu.VMEM((seq, 2 * experts), F32),
            pltpu.VMEM((seq, 2 * experts), F32),
            pltpu.VMEM(tokens.shape, BF16),
            pltpu.VMEM(cotangent.shape, BF16),
            pltpu.VMEM(router_t.shape, BF16),
            pltpu.VMEM((width // 4, w_first.shape[2]), BF16),
            pltpu.VMEM(w_second.shape[1:], BF16),
        ),
        8,
        12 * seq * width * experts,
        6 * seq * width,
        in_specs=[pl.BlockSpec(memory_space=pltpu.HBM)] * 5,
        scratch_shapes=[pltpu.SemaphoreType.DMA((5,))],
    )(*map(in_hbm, (tokens, router_t, cotangent, w_first, w_second)))


def digits(chips):
    low = 1 << ((chips.bit_length() - 1) // 2)
    return low, chips // low


def chip_of(first, second, core, chips):
    low, high = digits(chips)
    usual = first * low + second
    return usual + (core % 2 if low == high else 0) * (second * low + first - usual)


def away_chip(first, second, chips):
    return lax.axis_index("expert") ^ chip_of(first, second, lax.axis_index("dp"), chips)


def across_chips(values, digit):
    groups, chips = lax.axis_size("dp"), lax.axis_size("expert")
    got = [values[0]]
    for step in range(1, len(values)):
        away = [
            chip_of(0, step, core, chips) if digit else chip_of(step, 0, core, chips)
            for core in range(groups)
        ]
        pairs = [
            (core * chips + i, core * chips + (i ^ away[core]))
            for core in range(groups)
            for i in range(chips)
        ]
        got.append(lax.ppermute(values[step], ("dp", "expert"), pairs))
    return got


def shifted(value, axis, by):
    size = lax.axis_size(axis)
    return lax.ppermute(value, axis, [(i, (i + by) % size) for i in range(size)])


def exchange(blocks, axis, sign):
    return [blocks[0]] + [shifted(block, axis, sign * k) for k, block in enumerate(blocks) if k]


def sort_matrix(images, wide):
    shape = (images * wide, images * wide)
    to, start = iota(shape, 0), iota(shape, 1)
    return ((to % images) * wide + to // images == start).astype(BF16)


def pair_sum(pieces):
    total = [piece[...].astype(F32) for piece in pieces]
    while len(total) > 1:
        total = [sum(total[index : index + 2]) for index in range(0, len(total), 2)]
    return total[0]


def add_kernel(count, *refs):
    refs[-1][...] = pair_sum(refs[:count]).astype(BF16)


def add(pieces, name, after=()):
    size = pieces[0].size
    return call(
        functools.partial(add_kernel, len(pieces)),
        name,
        pltpu.VMEM(pieces[0].shape, BF16),
        4,
        len(pieces) * size,
        4 * size,
        in_specs=[pl.BlockSpec(memory_space=pltpu.VMEM)] * len(pieces)
        + [pl.BlockSpec(memory_space=pltpu.HBM)] * len(after),
    )(*pieces, *map(in_hbm, after))


def groups_kernel(count, wide, *refs):
    pieces, outs = refs[:count], refs[count:]
    total = pair_sum(pieces).astype(BF16)
    chips = total.shape[0] // wide
    _, high = digits(chips)
    shape = (chips * wide, chips * wide)
    to, start = iota(shape, 0), iota(shape, 1)
    chip = away_chip(to // wide % high, to // (high * wide), chips)
    moved = dot((start == to % wide * chips + chip).astype(BF16), total)
    height = high * wide
    for part, out in enumerate(outs):
        out[...] = moved[part * height : (part + 1) * height, :].astype(BF16)


def add_groups(pieces, wide):
    total, width = pieces[0].shape
    low, _ = digits(total // wide)
    return call(
        functools.partial(groups_kernel, len(pieces), wide),
        "add_groups",
        [pltpu.VMEM((total // low, width), BF16)] * low,
        8,
        2 * total * total * width,
        4 * total * width,
    )(*pieces)


def regroup_kernel(count, wide, *refs):
    blocks, outs = [ref[...].astype(F32) for ref in refs[count - 1 :: -1]], refs[count + 1 :]
    for part, out in enumerate(outs):
        rows = [block[part * wide : (part + 1) * wide, :] for block in blocks]
        out[...] = jnp.concatenate(rows).astype(BF16)


def regroup(blocks, wide, after):
    height, width = blocks[0].shape
    return call(
        functools.partial(regroup_kernel, len(blocks), wide),
        "regroup",
        [pltpu.VMEM((len(blocks) * wide, width), BF16)] * (height // wide),
        4,
        0,
        4 * height * width * len(blocks),
        in_specs=[pl.BlockSpec(memory_space=pltpu.VMEM)] * len(blocks)
        + [pl.BlockSpec(memory_space=pltpu.HBM)],
    )(*blocks[::-1], in_hbm(after))


def fetch_kernel(wide, rows, source, top, target, sorted_rows, sems):
    height = top.shape[0]
    copies = [
        pltpu.make_async_copy(
            source.at[0, pl.ds(part * height, height)],
            target.at[pl.ds(part * height, height)],
            sems.at[part],
        )
        for part in range(1, sems.shape[0])
    ]
    copies.append(pltpu.make_async_copy(top, target.at[pl.ds(0, height)], sems.at[0]))
    for copy in copies:
        copy.start()
    matrix = sort_matrix(rows.shape[0] // wide, wide)
    sorted_rows[...] = dot(matrix, rows[...]).astype(BF16)
    for copy in copies:
        copy.wait()


def fetch(wide, rows, weight, top):
    return call(
        functools.partial(fetch_kernel, wide),
        "fetch_first",
        (pltpu.VMEM(weight.shape[1:], BF16), pltpu.VMEM(rows.shape, BF16)),
        4,
        0,
        4 * weight[0].size,
        in_specs=[
            pl.BlockSpec(memory_space=pltpu.VMEM),
            pl.BlockSpec(memory_space=pltpu.HBM),
            pl.BlockSpec(memory_space=pltpu.VMEM),
        ],
        scratch_shapes=[pltpu.SemaphoreType.DMA((4,))],
    )(rows, in_hbm(weight), top)


def experts_kernel(per, groups, *refs):
    rows, refs = refs[:groups], refs[groups:]
    resident, weights_hbm, refs = refs[:2], refs[2:4], refs[4:]
    back_rows, refs = refs[:groups], refs[groups:]
    slots_out, grads_out, hidden_out, pre_out, w_first, w_second, sems = refs
    wide = 2 * per
    size = rows[0].shape[0] // wide
    span = lambda j: slice(j * size, (j + 1) * size)

    def copy(k, index):
        target = (w_first, w_second)[index]
        return pltpu.make_async_copy(weights_hbm[index].at[k], target.at[k], sems.at[index, k])

    copies = [None] + [(copy(k, 0), copy(k, 1)) for k in range(1, per)]

    def start(k):
        for one in copies[k] if k < per else ():
            one.start()

    start(1)
    matrix = sort_matrix(size, wide)
    for part in range(groups):
        moved = dot(matrix, rows[part][...]).astype(BF16) if part else rows[0][...]
        for k in range(per):
            slots_out[k, span(part), :] = moved[span(k), :]
            grads_out[k, span(part), :] = moved[span(per + k), :]
    for k in range(per):
        for one in copies[k] if k else ():
            one.wait()
        start(k + 2)
        first, second = (w_first.at[k], w_second.at[k]) if k else resident
        pre_act = dot(slots_out[k], first[...])
        grad_hidden = dot(grads_out[k], second[...], 1, 1)
        phi = 0.5 * (1.0 + lax.erf(pre_act * math.sqrt(0.5)))
        density = jnp.exp(pre_act * pre_act * -0.5) * (1.0 / math.sqrt(2.0 * math.pi))
        hidden = (pre_act * phi).astype(BF16)
        hidden_out[k] = hidden
        out = dot(hidden, second[...]).astype(BF16)
        grad_pre = ((phi + pre_act * density) * grad_hidden).astype(BF16)
        pre_out[k] = grad_pre
        grad_slot = dot(grad_pre, first[...], 1, 1).astype(BF16)
        for part, target in enumerate(back_rows):
            target[span(k), :] = out[span(part), :]
            target[span(per + k), :] = grad_slot[span(part), :]


def run_experts(rows, weights, w_first, w_second):
    per, width, units = w_first.shape
    groups = len(rows)
    total = rows[0].shape[0]
    images = groups * total // (2 * per)
    results = call(
        functools.partial(experts_kernel, per, groups),
        "experts",
        [pltpu.VMEM((total, width), BF16)] * groups
        + [pltpu.VMEM((per, images, width), BF16)] * 2
        + [pltpu.VMEM((per, images, units), BF16)] * 2,
        32,
        8 * per * images * width * units,
        4 * per * width * units,
        in_specs=[pl.BlockSpec(memory_space=pltpu.VMEM)] * (groups + 2)
        + [pl.BlockSpec(memory_space=pltpu.HBM)] * 2,
        scratch_shapes=[
            pltpu.VMEM(w_first.shape, BF16),
            pltpu.VMEM(w_second.shape, BF16),
            pltpu.SemaphoreType.DMA((2, per)),
        ],
    )(*rows, *weights, in_hbm(w_first), in_hbm(w_second))
    return results[:groups], results[groups:]


def outer_kernel(slots, grad_pre, hidden, grads, *refs):
    for left, right, out in ((slots, grad_pre, refs[-2]), (hidden, grads, refs[-1])):
        height = out.shape[1]
        piece = math.gcd(height, 128)
        for top in range(0, height, piece):
            rows = slice(top, top + piece)
            out[0, rows, :] = dot(left[0, :, rows], right[0], 0, 0).astype(BF16)


def weight_grads(slots, grads, hidden, grad_pre, after, quarter, into):
    per, images, width = slots.shape
    units = hidden.shape[2]
    begin, end = per * quarter // 4, per * (quarter + 1) // 4
    parts = 2 if units % 256 == 0 and width % 256 == 0 else 1
    lefts = lambda size: pl.BlockSpec(
        (1, images, size // parts), lambda k, part: (begin + k, 0, part)
    )
    rights = lambda size: pl.BlockSpec((1, images, size), lambda k, part: (begin + k, 0, 0))
    results = lambda a, b: pl.BlockSpec(
        (1, a // parts, b), lambda k, part: (begin + k, part, 0)
    )
    return call(
        outer_kernel,
        "weight_grads",
        (
            jax.ShapeDtypeStruct((per, width, units), BF16),
            jax.ShapeDtypeStruct((per, units, width), BF16),
        ),
        16,
        4 * (end - begin) * images * width * units,
        4 * (end - begin) * width * units,
        grid=(end - begin, parts),
        in_specs=[
            lefts(width),
            rights(units),
            lefts(units),
            rights(width),
            pl.BlockSpec(memory_space=pl.ANY),
        ]
        + [pl.BlockSpec(memory_space=pltpu.HBM)] * len(into),
        out_specs=[results(width, units), results(units, width)],
        input_output_aliases={5: 0, 6: 1} if into else {},
    )(slots, grad_pre, hidden, grads, after, *map(in_hbm, into))


def logits_kernel(per, groups, count, tokens, cotangent, disp, comb, after, *refs):
    blocks, parts, refs = refs[count - 1 :: -1], refs[count : count + groups], refs[count + groups :]
    outs, grad_logits, terms = refs
    moved = jnp.concatenate([block[...].astype(F32) for block in blocks]).astype(BF16)
    wide = 2 * per
    shape = (moved.shape[0], moved.shape[0])
    chips = shape[0] // wide
    to, start = iota(shape, 0), iota(shape, 1)
    low, _ = digits(chips)
    chip = away_chip(start // (low * wide), start // wide % low, chips)
    rows = dot((to == chip * wide + start % wide).astype(BF16), moved).astype(BF16)
    outs[...] = rows
    disp_prob = disp[...]
    comb_prob = comb[...]
    first = first_half(per, disp_prob.shape)
    grad_comb = dot(cotangent[...], rows, 1, 1)
    grad_disp = dot(tokens[...], rows, 1, 1)
    part_disp = disp_prob * (
        grad_disp - jnp.sum(disp_prob * grad_disp, axis=0, keepdims=True)
    )
    comb_sum = jnp.sum(jnp.where(first, comb_prob * grad_comb, 0.0), axis=1, keepdims=True)
    part_comb = comb_prob * (grad_comb - comb_sum)
    both = jnp.where(first, part_comb, part_disp)
    cols = both.shape[1]
    other = jnp.where(first, pltpu.roll(both, cols - per, 1), pltpu.roll(both, per, 1))
    paired = (both + other).astype(BF16)
    one_each = dot(paired, pick_first(per, cols // 2)).astype(BF16)
    grad_logits[...] = one_each
    term = dot(one_each, tokens[...], 0, 0)
    height = terms.shape[1]
    for part in range(groups):
        terms[part] = term[part * height : (part + 1) * height, :].astype(BF16)
    me = lax.axis_index("dp")
    for part, out in enumerate(parts):
        out[...] = terms[lax.rem(me + part, groups)]


def finish_logits(per, groups, tokens, cotangent, disp, comb, blocks, after):
    seq, width = tokens.shape
    cols = disp.shape[1]
    height = cols // 2 // groups
    results = call(
        functools.partial(logits_kernel, per, groups, len(blocks)),
        "grad_logits",
        [pltpu.VMEM((height, width), BF16)] * groups
        + [pltpu.VMEM((cols, width), BF16), pltpu.VMEM((seq, cols // 2), BF16)],
        12,
        6 * seq * width * cols,
        6 * seq * width,
        in_specs=[pl.BlockSpec(memory_space=pltpu.VMEM)] * 4
        + [pl.BlockSpec(memory_space=pltpu.HBM)]
        + [pl.BlockSpec(memory_space=pltpu.VMEM)] * len(blocks),
        scratch_shapes=[pltpu.VMEM((groups, height, width), BF16)],
    )(tokens, cotangent, disp, comb, in_hbm(after), *blocks[::-1])
    return results[:groups], *results[groups:]


def mixed_kernel(per, outs, comb, mixed):
    first = first_half(per, comb.shape)
    mixed[...] = dot(jnp.where(first, comb[...], 0.0).astype(BF16), outs[...]).astype(BF16)


def finish_mixed(per, outs, comb):
    seq, cols = comb.shape
    width = outs.shape[1]
    return call(
        functools.partial(mixed_kernel, per),
        "mixed",
        jax.ShapeDtypeStruct((seq, width), BF16),
        8,
        2 * seq * width * cols,
        2 * seq * width,
    )(outs, comb)


def tokens_kernel(per, outs, disp, grad_logits, router_t, after, grad_tokens):
    first = first_half(per, disp.shape)
    disp_cols = jnp.where(first, 0.0, disp[...]).astype(BF16)
    grad_tokens[...] = (
        dot(disp_cols, outs[...]) + dot(grad_logits[...], router_t[...])
    ).astype(BF16)


def finish_tokens(per, outs, disp, grad_logits, router_t, after):
    seq, cols = disp.shape
    width = outs.shape[1]
    return call(
        functools.partial(tokens_kernel, per),
        "grad_tokens",
        jax.ShapeDtypeStruct((seq, width), BF16),
        8,
        4 * seq * width * cols,
        2 * seq * width,
        in_specs=[pl.BlockSpec(memory_space=pltpu.VMEM)] * 4 + [pl.BlockSpec(memory_space=pl.ANY)],
    )(outs, disp, grad_logits, router_t, after)


def join_kernel(*refs):
    *parts, out = refs
    groups = len(parts)
    me = lax.axis_index("dp")
    for part, ref in enumerate(parts):
        out[lax.rem(me - part + groups, groups)] = ref[...].astype(F32)


def join(parts):
    height, width = parts[0].shape
    return call(
        join_kernel,
        "join",
        jax.ShapeDtypeStruct((len(parts), height, width), F32),
        4,
        0,
        6 * height * width,
    )(*parts).reshape(-1, width)


def total_over_devices(parts, mixed, beside):
    value = add(exchange(parts, "dp", 1), "add_cores", after=[mixed])
    for digit, size in zip((1, 0), digits(lax.axis_size("expert"))):
        value = add(across_chips([value] * size, digit), "add_chips", after=[beside(value)])
    return value, join(exchange([value] * len(parts), "dp", 1))


def local(tokens, router, weight_in, weight_out, cotangent):
    per = weight_in.shape[0]
    experts = router.shape[1]
    chips = experts // per
    groups = lax.axis_size("dp")
    tokens, cotangent = tokens[0], cotangent[0]
    width = tokens.shape[1]
    router_t = router.T

    rows, disp, comb, tokens, cotangent, router_t, first_top, second_weight = front(
        per, tokens, router_t, cotangent, weight_in, weight_out
    )
    rows = rows.reshape(chips, 2 * per, width)
    rows = lax.all_to_all(rows, "expert", split_axis=0, concat_axis=0, tiled=True)
    rows = rows.reshape(2 * experts, width)
    first_weight, own_rows = fetch(2 * per, rows, weight_in, first_top)
    rows = [own_rows, *exchange([rows] * groups, "dp", 1)[1:]]
    back_rows, (slots, grads, hidden, grad_pre) = run_experts(
        rows, (first_weight, second_weight), weight_in, weight_out
    )
    done, weight_results = 0, ()

    def next_weight_grads(after):
        nonlocal done, weight_results
        weight_results = weight_grads(slots, grads, hidden, grad_pre, after, done, weight_results)
        done += 1
        return weight_results[0]

    blocks = add_groups(exchange(back_rows, "dp", -1), 2 * per)
    blocks = regroup(across_chips(blocks, 1), 2 * per, next_weight_grads(blocks[0]))
    beside = next_weight_grads(blocks[0])
    parts, outs, grad_logits = finish_logits(
        per, groups, tokens, cotangent, disp, comb, across_chips(blocks, 0), beside
    )
    mixed = finish_mixed(per, outs, comb)
    value, total = total_over_devices(parts, mixed, next_weight_grads)
    grad_tokens = finish_tokens(per, outs, disp, grad_logits, router_t, value)
    grad_router, (grad_first, grad_second) = total.T, weight_results
    return (mixed[None], grad_tokens[None], grad_router, grad_first, grad_second)


def solution(mesh):
    return jax.shard_map(
        local,
        mesh=mesh,
        in_specs=(
            P(("dp", "expert"), None, None),
            P(),
            P("expert", None, "dp"),
            P("expert", "dp", None),
            P(("dp", "expert"), None, None),
        ),
        out_specs=(
            P(("dp", "expert"), None, None),
            P(("dp", "expert"), None, None),
            P(),
            P("expert", None, "dp"),
            P("expert", "dp", None),
        ),
        check_vma=False,
    )
```

```python
import functools
import math

import jax
import jax.numpy as jnp
from jax import lax
from jax.experimental import pallas as pl
from jax.experimental.pallas import tpu as pltpu
from jax.sharding import PartitionSpec as P

F32 = jnp.float32
BF16 = jnp.bfloat16
MIB = 1024 * 1024


def dot(left, right, left_dim=1, right_dim=0):
    return lax.dot_general(
        left, right, (((left_dim,), (right_dim,)), ((), ())), preferred_element_type=F32
    )


def iota(shape, dim):
    return lax.broadcasted_iota(jnp.int32, shape, dim)


def in_hbm(value):
    return pltpu.with_memory_space_constraint(value, pltpu.HBM)


def call(kernel, name, out_shape, limit, flops, moved, **more):
    return pl.pallas_call(
        kernel,
        out_shape=out_shape,
        compiler_params=pltpu.CompilerParams(vmem_limit_bytes=limit * MIB),
        cost_estimate=pl.CostEstimate(flops=flops, bytes_accessed=moved, transcendentals=0),
        name=name,
        **more,
    )


def picked_expert(per, rows):
    return (rows // (2 * per)) * per + rows % per


def spread(per, experts):
    shape = (2 * experts, experts)
    return (picked_expert(per, iota(shape, 0)) == iota(shape, 1)).astype(BF16)


def pick_first(per, experts):
    shape = (2 * experts, experts)
    row = iota(shape, 0)
    return ((picked_expert(per, row) == iota(shape, 1)) & (row % (2 * per) < per)).astype(BF16)


def first_half(per, shape):
    return iota(shape, 1) % (2 * per) < per


def front_kernel(per, tokens_hbm, router_hbm, cotangent_hbm, first_hbm, second_hbm, *refs):
    rows, disp, comb, tokens, cotangent, router_t, first_top, second, sems = refs
    copies = [
        pltpu.make_async_copy(source, target, sems.at[index])
        for index, (source, target) in enumerate(
            (
                (router_hbm, router_t),
                (tokens_hbm, tokens),
                (cotangent_hbm, cotangent),
                (second_hbm.at[0], second),
                (first_hbm.at[0, pl.ds(0, first_top.shape[0])], first_top),
            )
        )
    ]
    for copy in copies:
        copy.start()
    matrix = spread(per, router_t.shape[0])
    copies[0].wait()
    paired_router = dot(matrix, router_t[...]).astype(BF16)
    copies[1].wait()
    logits = dot(tokens[...], paired_router, 1, 1)
    first = first_half(per, logits.shape)
    down = jnp.exp(logits - jnp.max(logits, axis=0, keepdims=True))
    disp_prob = down / jnp.sum(down, axis=0, keepdims=True)
    across = jnp.exp(logits - jnp.max(logits, axis=1, keepdims=True))
    comb_prob = across / jnp.sum(jnp.where(first, across, 0.0), axis=1, keepdims=True)
    disp[...] = disp_prob
    comb[...] = comb_prob
    disp_cols = jnp.where(first, disp_prob, 0.0).astype(BF16)
    comb_cols = jnp.where(first, 0.0, comb_prob).astype(BF16)
    copies[2].wait()
    rows[...] = (
        dot(disp_cols, tokens[...], 0, 0) + dot(comb_cols, cotangent[...], 0, 0)
    ).astype(BF16)
    copies[3].wait()
    copies[4].wait()


def front(per, tokens, router_t, cotangent, w_first, w_second):
    seq, width = tokens.shape
    experts = router_t.shape[0]
    return call(
        functools.partial(front_kernel, per),
        "front",
        (
            pltpu.VMEM((2 * experts, width), BF16),
            pltpu.VMEM((seq, 2 * experts), F32),
            pltpu.VMEM((seq, 2 * experts), F32),
            pltpu.VMEM(tokens.shape, BF16),
            pltpu.VMEM(cotangent.shape, BF16),
            pltpu.VMEM(router_t.shape, BF16),
            pltpu.VMEM((width // 4, w_first.shape[2]), BF16),
            pltpu.VMEM(w_second.shape[1:], BF16),
        ),
        8,
        12 * seq * width * experts,
        6 * seq * width,
        in_specs=[pl.BlockSpec(memory_space=pltpu.HBM)] * 5,
        scratch_shapes=[pltpu.SemaphoreType.DMA((5,))],
    )(*map(in_hbm, (tokens, router_t, cotangent, w_first, w_second)))


def digits(chips):
    low = 1 << ((chips.bit_length() - 1) // 2)
    return low, chips // low


def chip_of(first, second, core, chips):
    low, high = digits(chips)
    usual = first * low + second
    return usual + (core % 2 if low == high else 0) * (second * low + first - usual)


def away_chip(first, second, chips):
    return lax.axis_index("expert") ^ chip_of(first, second, lax.axis_index("dp"), chips)


def across_chips(values, digit):
    groups, chips = lax.axis_size("dp"), lax.axis_size("expert")
    got = [values[0]]
    for step in range(1, len(values)):
        away = [
            chip_of(0, step, core, chips) if digit else chip_of(step, 0, core, chips)
            for core in range(groups)
        ]
        pairs = [
            (core * chips + i, core * chips + (i ^ away[core]))
            for core in range(groups)
            for i in range(chips)
        ]
        got.append(lax.ppermute(values[step], ("dp", "expert"), pairs))
    return got


def shifted(value, axis, by):
    size = lax.axis_size(axis)
    return lax.ppermute(value, axis, [(i, (i + by) % size) for i in range(size)])


def exchange(blocks, axis, sign):
    return [blocks[0]] + [shifted(block, axis, sign * k) for k, block in enumerate(blocks) if k]


def sort_matrix(images, wide):
    shape = (images * wide, images * wide)
    to, start = iota(shape, 0), iota(shape, 1)
    return ((to % images) * wide + to // images == start).astype(BF16)


def pair_sum(pieces):
    total = [piece[...].astype(F32) for piece in pieces]
    while len(total) > 1:
        total = [sum(total[index : index + 2]) for index in range(0, len(total), 2)]
    return total[0]


def add_kernel(count, *refs):
    refs[-1][...] = pair_sum(refs[:count]).astype(BF16)


def add(pieces, name, after=()):
    size = pieces[0].size
    return call(
        functools.partial(add_kernel, len(pieces)),
        name,
        pltpu.VMEM(pieces[0].shape, BF16),
        4,
        len(pieces) * size,
        4 * size,
        in_specs=[pl.BlockSpec(memory_space=pltpu.VMEM)] * len(pieces)
        + [pl.BlockSpec(memory_space=pltpu.HBM)] * len(after),
    )(*pieces, *map(in_hbm, after))


def groups_kernel(count, wide, *refs):
    pieces, outs = refs[:count], refs[count:]
    halves = [pair_sum(pieces[: count // 2]), pair_sum(pieces[count // 2 :])]
    total = jnp.concatenate(halves).astype(BF16)
    chips = total.shape[0] // wide
    _, high = digits(chips)
    shape = (chips * wide, chips * wide)
    to, start = iota(shape, 0), iota(shape, 1)
    chip = away_chip(to // wide % high, to // (high * wide), chips)
    moved = dot((start == to % wide * chips + chip).astype(BF16), total)
    height = high * wide
    for part, out in enumerate(outs):
        out[...] = moved[part * height : (part + 1) * height, :].astype(BF16)


def add_groups(pieces, wide):
    total, width = 2 * pieces[0].shape[0], pieces[0].shape[1]
    low, _ = digits(total // wide)
    return call(
        functools.partial(groups_kernel, len(pieces), wide),
        "add_groups",
        [pltpu.VMEM((total // low, width), BF16)] * low,
        8,
        2 * total * total * width,
        4 * total * width,
    )(*pieces)


def regroup_kernel(count, wide, *refs):
    blocks, outs = [ref[...].astype(F32) for ref in refs[count - 1 :: -1]], refs[count + 1 :]
    for part, out in enumerate(outs):
        rows = [block[part * wide : (part + 1) * wide, :] for block in blocks]
        out[...] = jnp.concatenate(rows).astype(BF16)


def regroup(blocks, wide, after):
    height, width = blocks[0].shape
    return call(
        functools.partial(regroup_kernel, len(blocks), wide),
        "regroup",
        [pltpu.VMEM((len(blocks) * wide, width), BF16)] * (height // wide),
        4,
        0,
        4 * height * width * len(blocks),
        in_specs=[pl.BlockSpec(memory_space=pltpu.VMEM)] * len(blocks)
        + [pl.BlockSpec(memory_space=pltpu.HBM)],
    )(*blocks[::-1], in_hbm(after))


def fetch_kernel(wide, rows, source, top, target, sorted_rows, sems):
    height = top.shape[0]
    copies = [
        pltpu.make_async_copy(
            source.at[0, pl.ds(part * height, height)],
            target.at[pl.ds(part * height, height)],
            sems.at[part],
        )
        for part in range(1, sems.shape[0])
    ]
    copies.append(pltpu.make_async_copy(top, target.at[pl.ds(0, height)], sems.at[0]))
    for copy in copies:
        copy.start()
    matrix = sort_matrix(rows.shape[0] // wide, wide)
    sorted_rows[...] = dot(matrix, rows[...]).astype(BF16)
    for copy in copies:
        copy.wait()


def fetch(wide, rows, weight, top):
    return call(
        functools.partial(fetch_kernel, wide),
        "fetch_first",
        (pltpu.VMEM(weight.shape[1:], BF16), pltpu.VMEM(rows.shape, BF16)),
        4,
        0,
        4 * weight[0].size,
        in_specs=[
            pl.BlockSpec(memory_space=pltpu.VMEM),
            pl.BlockSpec(memory_space=pltpu.HBM),
            pl.BlockSpec(memory_space=pltpu.VMEM),
        ],
        scratch_shapes=[pltpu.SemaphoreType.DMA((4,))],
    )(rows, in_hbm(weight), top)


def experts_kernel(per, groups, *refs):
    rows, refs = refs[:groups], refs[groups:]
    resident, weights_hbm, refs = refs[:2], refs[2:4], refs[4:]
    back_outs, back_grads, refs = refs[:groups], refs[groups : 2 * groups], refs[2 * groups :]
    slots_out, grads_out, hidden_out, pre_out, w_first, w_second, sems = refs
    wide = 2 * per
    size = rows[0].shape[0] // wide
    span = lambda j: slice(j * size, (j + 1) * size)

    def copy(k, index):
        target = (w_first, w_second)[index]
        return pltpu.make_async_copy(weights_hbm[index].at[k], target.at[k], sems.at[index, k])

    copies = [None] + [(copy(k, 0), copy(k, 1)) for k in range(1, per)]

    def start(k):
        for one in copies[k] if k < per else ():
            one.start()

    start(1)
    matrix = sort_matrix(size, wide)
    for part in range(groups):
        moved = dot(matrix, rows[part][...]).astype(BF16) if part else rows[0][...]
        for k in range(per):
            slots_out[k, span(part), :] = moved[span(k), :]
            grads_out[k, span(part), :] = moved[span(per + k), :]
    for k in range(per):
        for one in copies[k] if k else ():
            one.wait()
        start(k + 2)
        first, second = (w_first.at[k], w_second.at[k]) if k else resident
        pre_act = dot(slots_out[k], first[...])
        grad_hidden = dot(grads_out[k], second[...], 1, 1)
        phi = 0.5 * (1.0 + lax.erf(pre_act * math.sqrt(0.5)))
        density = jnp.exp(pre_act * pre_act * -0.5) * (1.0 / math.sqrt(2.0 * math.pi))
        hidden = (pre_act * phi).astype(BF16)
        hidden_out[k] = hidden
        out = dot(hidden, second[...]).astype(BF16)
        grad_pre = ((phi + pre_act * density) * grad_hidden).astype(BF16)
        pre_out[k] = grad_pre
        grad_slot = dot(grad_pre, first[...], 1, 1).astype(BF16)
        for part in range(groups):
            back_outs[part][span(k), :] = out[span(part), :]
            back_grads[part][span(k), :] = grad_slot[span(part), :]


def run_experts(rows, weights, w_first, w_second):
    per, width, units = w_first.shape
    groups = len(rows)
    total = rows[0].shape[0]
    images = groups * total // (2 * per)
    results = call(
        functools.partial(experts_kernel, per, groups),
        "experts",
        [pltpu.VMEM((total // 2, width), BF16)] * (2 * groups)
        + [pltpu.VMEM((per, images, width), BF16)] * 2
        + [pltpu.VMEM((per, images, units), BF16)] * 2,
        32,
        8 * per * images * width * units,
        4 * per * width * units,
        in_specs=[pl.BlockSpec(memory_space=pltpu.VMEM)] * (groups + 2)
        + [pl.BlockSpec(memory_space=pltpu.HBM)] * 2,
        scratch_shapes=[
            pltpu.VMEM(w_first.shape, BF16),
            pltpu.VMEM(w_second.shape, BF16),
            pltpu.SemaphoreType.DMA((2, per)),
        ],
    )(*rows, *weights, in_hbm(w_first), in_hbm(w_second))
    return results[:groups], results[groups : 2 * groups], results[2 * groups :]


def outer_kernel(slots, grad_pre, hidden, grads, *refs):
    for left, right, out in ((slots, grad_pre, refs[-2]), (hidden, grads, refs[-1])):
        height = out.shape[1]
        piece = math.gcd(height, 128)
        for top in range(0, height, piece):
            rows = slice(top, top + piece)
            out[0, rows, :] = dot(left[0, :, rows], right[0], 0, 0).astype(BF16)


def weight_grads(slots, grads, hidden, grad_pre, after, quarter, into):
    per, images, width = slots.shape
    units = hidden.shape[2]
    begin, end = per * quarter // 4, per * (quarter + 1) // 4
    parts = 2 if units % 256 == 0 and width % 256 == 0 else 1
    lefts = lambda size: pl.BlockSpec(
        (1, images, size // parts), lambda k, part: (begin + k, 0, part)
    )
    rights = lambda size: pl.BlockSpec((1, images, size), lambda k, part: (begin + k, 0, 0))
    results = lambda a, b: pl.BlockSpec(
        (1, a // parts, b), lambda k, part: (begin + k, part, 0)
    )
    return call(
        outer_kernel,
        "weight_grads",
        (
            jax.ShapeDtypeStruct((per, width, units), BF16),
            jax.ShapeDtypeStruct((per, units, width), BF16),
        ),
        16,
        4 * (end - begin) * images * width * units,
        4 * (end - begin) * width * units,
        grid=(end - begin, parts),
        in_specs=[
            lefts(width),
            rights(units),
            lefts(units),
            rights(width),
            pl.BlockSpec(memory_space=pl.ANY),
        ]
        + [pl.BlockSpec(memory_space=pltpu.HBM)] * len(into),
        out_specs=[results(width, units), results(units, width)],
        input_output_aliases={5: 0, 6: 1} if into else {},
    )(slots, grad_pre, hidden, grads, after, *map(in_hbm, into))


def logits_kernel(per, groups, count, tokens, cotangent, disp, comb, after, *refs):
    blocks, parts, refs = refs[count - 1 :: -1], refs[count : count + groups], refs[count + groups :]
    outs, grad_logits, terms = refs
    moved = jnp.concatenate([block[...] for block in blocks])
    wide = 2 * per
    shape = (moved.shape[0], moved.shape[0])
    chips = shape[0] // wide
    to, start = iota(shape, 0), iota(shape, 1)
    low, _ = digits(chips)
    chip = away_chip(start // (low * wide), start // wide % low, chips)
    rows = dot((to == chip * wide + start % wide).astype(BF16), moved).astype(BF16)
    outs[...] = rows
    disp_prob = disp[...]
    comb_prob = comb[...]
    first = first_half(per, disp_prob.shape)
    grad_comb = dot(cotangent[...], rows, 1, 1)
    grad_disp = dot(tokens[...], rows, 1, 1)
    part_disp = disp_prob * (
        grad_disp - jnp.sum(disp_prob * grad_disp, axis=0, keepdims=True)
    )
    comb_sum = jnp.sum(jnp.where(first, comb_prob * grad_comb, 0.0), axis=1, keepdims=True)
    part_comb = comb_prob * (grad_comb - comb_sum)
    both = jnp.where(first, part_comb, part_disp)
    cols = both.shape[1]
    other = jnp.where(first, pltpu.roll(both, cols - per, 1), pltpu.roll(both, per, 1))
    paired = (both + other).astype(BF16)
    one_each = dot(paired, pick_first(per, cols // 2)).astype(BF16)
    grad_logits[...] = one_each
    term = dot(one_each, tokens[...], 0, 0)
    height = terms.shape[1]
    for part in range(groups):
        terms[part] = term[part * height : (part + 1) * height, :].astype(BF16)
    me = lax.axis_index("dp")
    for part, out in enumerate(parts):
        out[...] = terms[lax.rem(me + part, groups)]


def finish_logits(per, groups, tokens, cotangent, disp, comb, blocks, after):
    seq, width = tokens.shape
    cols = disp.shape[1]
    height = cols // 2 // groups
    results = call(
        functools.partial(logits_kernel, per, groups, len(blocks)),
        "grad_logits",
        [pltpu.VMEM((height, width), BF16)] * groups
        + [pltpu.VMEM((cols, width), BF16), pltpu.VMEM((seq, cols // 2), BF16)],
        12,
        6 * seq * width * cols,
        6 * seq * width,
        in_specs=[pl.BlockSpec(memory_space=pltpu.VMEM)] * 4
        + [pl.BlockSpec(memory_space=pltpu.HBM)]
        + [pl.BlockSpec(memory_space=pltpu.VMEM)] * len(blocks),
        scratch_shapes=[pltpu.VMEM((groups, height, width), BF16)],
    )(tokens, cotangent, disp, comb, in_hbm(after), *blocks[::-1])
    return results[:groups], *results[groups:]


def mixed_kernel(per, outs, comb, mixed):
    first = first_half(per, comb.shape)
    mixed[...] = dot(jnp.where(first, comb[...], 0.0).astype(BF16), outs[...]).astype(BF16)


def finish_mixed(per, outs, comb):
    seq, cols = comb.shape
    width = outs.shape[1]
    return call(
        functools.partial(mixed_kernel, per),
        "mixed",
        jax.ShapeDtypeStruct((seq, width), BF16),
        8,
        2 * seq * width * cols,
        2 * seq * width,
    )(outs, comb)


def tokens_kernel(per, outs, disp, grad_logits, router_t, after, grad_tokens):
    first = first_half(per, disp.shape)
    disp_cols = jnp.where(first, 0.0, disp[...]).astype(BF16)
    grad_tokens[...] = (
        dot(disp_cols, outs[...]) + dot(grad_logits[...], router_t[...])
    ).astype(BF16)


def finish_tokens(per, outs, disp, grad_logits, router_t, after):
    seq, cols = disp.shape
    width = outs.shape[1]
    return call(
        functools.partial(tokens_kernel, per),
        "grad_tokens",
        jax.ShapeDtypeStruct((seq, width), BF16),
        8,
        4 * seq * width * cols,
        2 * seq * width,
        in_specs=[pl.BlockSpec(memory_space=pltpu.VMEM)] * 4 + [pl.BlockSpec(memory_space=pl.ANY)],
    )(outs, disp, grad_logits, router_t, after)


def join_kernel(*refs):
    *parts, out = refs
    groups = len(parts)
    me = lax.axis_index("dp")
    for part, ref in enumerate(parts):
        out[lax.rem(me - part + groups, groups)] = ref[...].astype(F32)


def join(parts):
    height, width = parts[0].shape
    return call(
        join_kernel,
        "join",
        jax.ShapeDtypeStruct((len(parts), height, width), F32),
        4,
        0,
        6 * height * width,
    )(*parts).reshape(-1, width)


def total_over_devices(parts, mixed, beside):
    value = add(exchange(parts, "dp", 1), "add_cores", after=[mixed])
    for digit, size in zip((1, 0), digits(lax.axis_size("expert"))):
        value = add(across_chips([value] * size, digit), "add_chips", after=[beside(value)])
    return value, join(exchange([value] * len(parts), "dp", 1))


def local(tokens, router, weight_in, weight_out, cotangent):
    per = weight_in.shape[0]
    experts = router.shape[1]
    chips = experts // per
    groups = lax.axis_size("dp")
    tokens, cotangent = tokens[0], cotangent[0]
    width = tokens.shape[1]
    router_t = router.T

    rows, disp, comb, tokens, cotangent, router_t, first_top, second_weight = front(
        per, tokens, router_t, cotangent, weight_in, weight_out
    )
    rows = rows.reshape(chips, 2 * per, width)
    rows = lax.all_to_all(rows, "expert", split_axis=0, concat_axis=0, tiled=True)
    rows = rows.reshape(2 * experts, width)
    first_weight, own_rows = fetch(2 * per, rows, weight_in, first_top)
    rows = [own_rows, *exchange([rows] * groups, "dp", 1)[1:]]
    back_outs, back_grads, (slots, grads, hidden, grad_pre) = run_experts(
        rows, (first_weight, second_weight), weight_in, weight_out
    )
    done, weight_results = 0, ()

    def next_weight_grads(after):
        nonlocal done, weight_results
        weight_results = weight_grads(slots, grads, hidden, grad_pre, after, done, weight_results)
        done += 1
        return weight_results[0]

    pieces = [*exchange(back_outs, "dp", -1), *exchange(back_grads, "dp", -1)]
    blocks = add_groups(pieces, 2 * per)
    blocks = regroup(across_chips(blocks, 1), 2 * per, next_weight_grads(blocks[0]))
    beside = next_weight_grads(blocks[0])
    parts, outs, grad_logits = finish_logits(
        per, groups, tokens, cotangent, disp, comb, across_chips(blocks, 0), beside
    )
    mixed = finish_mixed(per, outs, comb)
    value, total = total_over_devices(parts, mixed, next_weight_grads)
    grad_tokens = finish_tokens(per, outs, disp, grad_logits, router_t, value)
    grad_router, (grad_first, grad_second) = total.T, weight_results
    return (mixed[None], grad_tokens[None], grad_router, grad_first, grad_second)


def solution(mesh):
    return jax.shard_map(
        local,
        mesh=mesh,
        in_specs=(
            P(("dp", "expert"), None, None),
            P(),
            P("expert", None, "dp"),
            P("expert", "dp", None),
            P(("dp", "expert"), None, None),
        ),
        out_specs=(
            P(("dp", "expert"), None, None),
            P(("dp", "expert"), None, None),
            P(),
            P("expert", None, "dp"),
            P("expert", "dp", None),
        ),
        check_vma=False,
    )
```
